32 devices in a mesh: dp: 4 (over y, x), fsdp: 8 (over z, core).
Axes of the slice: x: 2, y: 2, z: 4, core: 2. Of those that a mesh axis runs over, the one named last changes fastest.
Arguments:
- tokens: bfloat16 [2, 32, 1024, 1024], P(None, ('dp', 'fsdp')), may hold values from -6 to 6
- document_length_list: int32 [2, 32, 8], P(None, ('dp', 'fsdp')), may hold values from 1 to 256, 1024 in all within a row
- joint_projection_weight: bfloat16 [1024, 3072], P('fsdp'), may hold values from -0.25 to 0.25
- attention_out_weight: bfloat16 [1024, 1024], P('fsdp'), may hold values from -0.375 to 0.375
- feed_up_weight: bfloat16 [1024, 4096], P('fsdp'), may hold values from -0.1875 to 0.1875
- feed_down_weight: bfloat16 [4096, 1024], P('fsdp'), may hold values from -0.09375 to 0.09375
- frozen_norm_gains: bfloat16 [2, 1024], P(None, 'fsdp'), may hold values from 0.5 to 1.5
- biases: bfloat16 [6, 1024], P(None, 'fsdp'), may hold values from -4 to 4
- hidden_up_bias: bfloat16 [4096], P('fsdp'), may hold values from -6 to 6
- query_down_adapter: bfloat16 [1024, 4], replicated, may hold values from -0.1875 to 0.1875
- query_up_adapter: bfloat16 [4, 1024], replicated, may hold values from -0.4375 to 0.4375
- value_down_adapter: bfloat16 [1024, 4], replicated, may hold values from -0.1875 to 0.1875
- value_up_adapter: bfloat16 [4, 1024], replicated, may hold values from -0.4375 to 0.4375
- cotangent: bfloat16 [2, 32, 1024, 1024], P(None, ('dp', 'fsdp')), may hold values from -6 to 6
Outputs:
- block_output: bfloat16 [2, 32, 1024, 1024], P(None, ('dp', 'fsdp'))
- input_grad: bfloat16 [2, 32, 1024, 1024], P(None, ('dp', 'fsdp'))
- grad_lora_a_q: float32 [1024, 4], replicated
- grad_lora_b_q: float32 [4, 1024], replicated
- grad_lora_a_v: float32 [1024, 4], replicated
- grad_lora_b_v: float32 [4, 1024], replicated
The draws below stay inside these ranges and needn't reach their ends.
Inputs may be any that keep to these rules, and one draw needn't show every extreme that they name: `document_length_list`: the 8 lengths of a slot sum to 1024, and the largest of them is exactly 256.
All inputs are finite; a program needn't handle non-finite values.
Results may differ from the reference program's by a relative error of at most 0.015.
Values may be sent and summed in bfloat16 or wider, within the bound.
No kernel may reach another device: no remote copies, remote signals or barrier semaphores. Data moves between devices by JAX's collectives and lax.ppermute only.
A program may use at most 320 MiB of HBM per device.

```python
import math
import jax
import jax.numpy as jnp
import numpy as np
from jax import lax

MODEL_WIDTH = 1024
HEADS = 16
HEAD_DIM = 64
FF = 4096
ADAPTER_RANK = 4
SEQ = 1024
DOCS = 8
DOC_MOST = 256
MICRO = 2
SLOTS = 32


def level_of(rng, extent, split, smallest, high):
    def one(dim, blocks):
        heights = jax.random.uniform(jax.random.fold_in(jax.random.fold_in(rng, 6), dim), (blocks,), jnp.float32, smallest / len(split), high / len(split))
        return jnp.repeat(jnp.exp(heights), extent[dim] // blocks).reshape((-1,) + (1,) * (len(extent) - dim - 1))

    loudness = one(*split[0])
    for cut in split[1:]:
        loudness = loudness * one(*cut)
    return loudness


def split_up(amount, total, bound, lean):
    loads = [(1 << 20) // math.isqrt(grade ** lean) + 1 for grade in range(2, amount + 1)]
    surplus, counts = total - bound - (amount - 1), [1] * (amount - 1)
    while surplus > 0:
        candidates = [i for i in range(amount - 1) if counts[i] < bound]
        pool, remaining = sum([loads[i] for i in candidates]), surplus
        for i in candidates:
            addition = min(bound - counts[i], max(1, remaining * loads[i] // pool), surplus)
            counts[i] = counts[i] + addition
            surplus = surplus - addition
    return np.array([bound] + counts)


def ragged_sizes(rng, amount, total, limit, slope):
    if amount == 2:
        one = jax.random.randint(rng, (), max(1, total - limit), min(limit, total - 1) + 1)
        return jnp.stack([one, total - one])
    sizes = jnp.asarray(split_up(amount, total, limit, slope), jnp.int32)
    pairs = (amount - 1) // 2
    giver, receiver = sizes[1:1 + 2 * pairs:2], sizes[2:2 + 2 * pairs:2]
    margin = jnp.minimum(giver - 1, limit - receiver)
    passed = jax.random.randint(jax.random.fold_in(rng, 1), (pairs,), 0, 1 << 20) % (margin + 1)
    sizes = sizes.at[1:1 + 2 * pairs:2].set(giver - passed).at[2:2 + 2 * pairs:2].set(receiver + passed)
    return sizes[jax.random.permutation(jax.random.fold_in(rng, 2), amount)]


def scatter_about(stream_key, shape, deviation, reach, pieces=(), kind=jnp.bfloat16):
    array = jax.random.normal(stream_key, shape, jnp.float32) * deviation
    if len(pieces) > 0:
        array = level_of(stream_key, shape, pieces, -0.22, 0.18) * array
    return jnp.clip(array, min=-reach, max=reach).astype(kind)


def setup_inputs(seed: int = 0) -> dict:
    splits = jax.random.split(jax.random.key(seed), 15)
    return {
        "tokens": scatter_about(splits[0], (MICRO, SLOTS, SEQ, MODEL_WIDTH), 1.0, 6.0, ((1, 32),)),
        "document_length_list": jax.vmap(lambda own: ragged_sizes(own, DOCS, SEQ, DOC_MOST, 1))(jax.random.split(splits[1], MICRO * SLOTS)).reshape((MICRO, SLOTS, DOCS)).astype(jnp.int32),
        "joint_projection_weight": scatter_about(splits[2], (MODEL_WIDTH, 3 * MODEL_WIDTH), (MODEL_WIDTH // 2) ** -0.5, 0.25, ((0, 8),)),
        "attention_out_weight": scatter_about(splits[3], (MODEL_WIDTH, MODEL_WIDTH), (MODEL_WIDTH // 4) ** -0.5, 0.375, ((0, 8),)),
        "feed_up_weight": scatter_about(splits[4], (MODEL_WIDTH, FF), MODEL_WIDTH ** -0.5, 0.1875, ((0, 8),)),
        "feed_down_weight": scatter_about(splits[5], (FF, MODEL_WIDTH), FF ** -0.5, 0.09375, ((0, 8),)),
        "frozen_norm_gains": jnp.clip(1.0 + 0.1 * jax.random.normal(splits[6], (2, MODEL_WIDTH), jnp.float32), 0.5, 1.5).astype(jnp.bfloat16),
        "biases": scatter_about(splits[7], (6, MODEL_WIDTH), 0.3, 4.0, ((1, 8),)),
        "hidden_up_bias": scatter_about(splits[8], (FF,), 0.5, 6.0, ((0, 8),)),
        "query_down_adapter": scatter_about(splits[9], (MODEL_WIDTH, ADAPTER_RANK), MODEL_WIDTH ** -0.5, 0.1875),
        "query_up_adapter": scatter_about(splits[10], (ADAPTER_RANK, MODEL_WIDTH), 0.03, 0.4375),
        "value_down_adapter": scatter_about(splits[11], (MODEL_WIDTH, ADAPTER_RANK), MODEL_WIDTH ** -0.5, 0.1875),
        "value_up_adapter": scatter_about(splits[12], (ADAPTER_RANK, MODEL_WIDTH), 0.03, 0.4375),
        "cotangent": scatter_about(splits[13], (MICRO, SLOTS, SEQ, MODEL_WIDTH), 1.0, 6.0, ((1, 32),)),
    }


epsilon = 1e-05
adapter_scale = 8.0
masked_fill = -1e+30

@jax.custom_vjp
def narrow_rows(v):
    return lax.optimization_barrier(v.astype(jnp.bfloat16)).astype(jnp.float32)

@jax.custom_vjp
def narrow_reverse(v):
    return v

def low_keep(v):
    return (narrow_rows(v), None)

def low_pass(kept, grad):
    return (grad,)

def back_keep(v):
    return (v, None)

def back_low(kept, grad):
    return (narrow_rows(grad),)
narrow_rows.defvjp(low_keep, low_pass)
narrow_reverse.defvjp(back_keep, back_low)

def layer_norm(inputs, norm_gain, norm_shift):
    average = lax.optimization_barrier(jnp.mean(inputs, axis=-1, keepdims=True))
    centred = inputs - average
    variance = lax.optimization_barrier(jnp.mean(centred * centred, axis=-1, keepdims=True))
    return centred * lax.rsqrt(variance + epsilon) * norm_gain + norm_shift

def document_ids(document_length_list, seq_len):
    starts = (jnp.cumsum(document_length_list, axis=-1) - document_length_list).astype(jnp.int32)
    places = jnp.arange(seq_len, dtype=jnp.int32)
    reached = places[:, None] >= starts[..., None, :]
    return lax.optimization_barrier(jnp.sum(reached.astype(jnp.int32), axis=-1)).astype(jnp.int32)

def matrix_product(left, right):
    return jnp.dot(left, right, precision=lax.Precision.HIGHEST)

def attention(query_vectors, key_rows, value_vectors, documents):
    seq_len = query_vectors.shape[1]
    places = jnp.arange(seq_len, dtype=jnp.int32)
    allowed = (documents[:, :, None] == documents[:, None, :]) & (places[None, None, :] <= places[None, :, None])
    scores = narrow_reverse(HEAD_DIM ** (-0.5) * jnp.einsum('gqhd,gkhd->ghqk', query_vectors, key_rows, precision=lax.Precision.HIGHEST))
    masked = jnp.where(allowed[:, None], scores, masked_fill)
    highest = lax.optimization_barrier(jnp.max(masked, axis=-1, keepdims=True))
    exponent = jnp.exp(masked - highest)
    prob_low = narrow_rows(exponent / lax.optimization_barrier(jnp.sum(exponent, axis=-1, keepdims=True)))
    return jnp.einsum('ghqk,gkhd->gqhd', prob_low, value_vectors, precision=lax.Precision.HIGHEST)

def residual_block_apply(residual_input, documents, frozen_weights, adapter_list):
    joint_projection_weight, attention_out_weight, feed_up_weight, feed_down_weight, frozen_norm_gains, biases, hidden_up_bias = frozen_weights
    query_down_adapter, query_up_adapter, value_down_adapter, value_up_adapter = adapter_list
    group_size, seq_len, feature_width = residual_input.shape
    token_rows = residual_input.reshape(group_size * seq_len, feature_width)
    normalized_rows = narrow_rows(layer_norm(token_rows, frozen_norm_gains[0], biases[0]))
    query_narrow = narrow_rows(narrow_reverse(matrix_product(normalized_rows, query_down_adapter)))
    value_narrow = narrow_rows(narrow_reverse(matrix_product(normalized_rows, value_down_adapter)))
    attention_mixed = matrix_product(normalized_rows, joint_projection_weight)
    query_vectors = narrow_rows(narrow_reverse(attention_mixed[:, :feature_width] + biases[2] + adapter_scale * matrix_product(query_narrow, query_up_adapter)))
    key_rows = narrow_rows(narrow_reverse(attention_mixed[:, feature_width:2 * feature_width]))
    value_vectors = narrow_rows(narrow_reverse(attention_mixed[:, 2 * feature_width:] + biases[3] + adapter_scale * matrix_product(value_narrow, value_up_adapter)))
    four_way = (group_size, seq_len, HEADS, HEAD_DIM)
    attended = attention(query_vectors.reshape(four_way), key_rows.reshape(four_way), value_vectors.reshape(four_way), documents)
    attended = narrow_rows(narrow_reverse(attended.reshape(group_size * seq_len, feature_width)))
    hidden_one = token_rows + narrow_reverse(matrix_product(attended, attention_out_weight) + biases[4])
    normed_two = narrow_rows(layer_norm(hidden_one, frozen_norm_gains[1], biases[1]))
    pre_act = narrow_reverse(matrix_product(normed_two, feed_up_weight) + hidden_up_bias)
    activated = narrow_rows(jax.nn.gelu(pre_act, approximate=True))
    result = hidden_one + narrow_reverse(matrix_product(activated, feed_down_weight) + biases[5])
    return result.reshape(group_size, seq_len, feature_width)

def reference(tokens, document_length_list, joint_projection_weight, attention_out_weight, feed_up_weight, feed_down_weight, frozen_norm_gains, biases, hidden_up_bias, query_down_adapter, query_up_adapter, value_down_adapter, value_up_adapter, cotangent):
    frozen_weights = tuple((bundle_member.astype(jnp.float32) for bundle_member in (joint_projection_weight, attention_out_weight, feed_up_weight, feed_down_weight, frozen_norm_gains, biases, hidden_up_bias)))
    adapter_list = tuple((bundle_member.astype(jnp.float32) for bundle_member in (query_down_adapter, query_up_adapter, value_down_adapter, value_up_adapter)))
    group_size = 2
    steps_count = MICRO * SLOTS // group_size
    grouped = tokens.astype(jnp.float32).reshape(steps_count, group_size, SEQ, MODEL_WIDTH)
    documents = document_ids(document_length_list.reshape(steps_count, group_size, DOCS), SEQ)
    cot_rows = cotangent.astype(jnp.float32).reshape(steps_count, group_size, SEQ, MODEL_WIDTH)

    def one_group(running_offset, inputs):
        rows_group, document_group, cotangent_group = inputs

        def forward_apply(residual_input, adapter_bundle):
            return residual_block_apply(residual_input, document_group, frozen_weights, adapter_bundle)
        result, reverse_function = jax.vjp(forward_apply, rows_group, adapter_list)
        row_gradients, adapter_gradients = reverse_function(cotangent_group)
        running_offset = tuple((total_length + part for total_length, part in zip(running_offset, adapter_gradients)))
        return (running_offset, (result.astype(jnp.bfloat16), row_gradients.astype(jnp.bfloat16)))
    zero_grads = tuple((jnp.zeros_like(bundle_member) for bundle_member in adapter_list))
    totals, (outputs, input_gradient_rows) = lax.scan(one_group, zero_grads, (grouped, documents, cot_rows))
    full_shape = (MICRO, SLOTS, SEQ, MODEL_WIDTH)
    return (outputs.reshape(full_shape), input_gradient_rows.reshape(full_shape), totals[0], totals[1], totals[2], totals[3])
```

```python
import functools
import math

import jax
import jax.numpy as jnp
from jax import lax
from jax.experimental import pallas as pl
from jax.experimental.pallas import tpu as pltpu
from jax.sharding import PartitionSpec as P

f32 = jnp.float32
bf16 = jnp.bfloat16
LANES = 128
PAIR = 128
BAND = 3
EPS = 1e-5
MASKED = -1e30
SCORE_SCALE = 0.125 * math.log2(math.e)
GELU_C = math.sqrt(2.0 / math.pi)
VMEM_LIMIT = 58 * 2**20
NT = (((1,), (1,)), ((), ()))
TN = (((0,), (0,)), ((), ()))


def dot(a, b):
    return jnp.dot(a, b, preferred_element_type=f32)


def dot_nt(a, b):
    return lax.dot_general(a, b, NT, preferred_element_type=f32)


def dot_tn(a, b):
    return lax.dot_general(a, b, TN, preferred_element_type=f32)


def params():
    return pltpu.CompilerParams(vmem_limit_bytes=VMEM_LIMIT)


def resident(array):
    zeros = (0,) * array.ndim
    return pl.BlockSpec(array.shape, lambda *_: zeros, pipeline_mode=pl.Buffered(1))


def normalise(x):
    centred = x - jnp.mean(x, axis=-1, keepdims=True)
    r = lax.rsqrt(jnp.mean(centred * centred, axis=-1, keepdims=True) + EPS)
    return centred * r, r


def norm_back(n, r, w):
    return r * (w - jnp.mean(w, axis=-1, keepdims=True) - n * jnp.mean(w * n, axis=-1, keepdims=True))


def gelu_and_slope(x):
    x2 = x * x
    t = jnp.tanh(x * (GELU_C + (GELU_C * 0.044715) * x2))
    half = 0.5 + 0.5 * t
    slope = half + (0.5 * x) * ((1.0 - t * t) * (GELU_C + (3 * GELU_C * 0.044715) * x2))
    return x * half, slope


def project_kernel(tok, w, down, up, vec, q_ref, k_ref, v_ref, low_ref):
    width = tok.shape[1]
    n, _ = normalise(tok[...].astype(f32))
    normed = (n * vec[6:7, :] + vec[0:1, :]).astype(bf16)
    low = dot(normed, down[...]).astype(bf16)
    low_ref[...] = low
    q = dot(normed, w[:, :width]) + dot(low, up[:, :width]) + vec[2:3, :]
    q_ref[...] = (q * SCORE_SCALE).astype(bf16)
    k_ref[...] = dot(normed, w[:, width : 2 * width]).astype(bf16)
    v = dot(normed, w[:, 2 * width :]) + dot(low, up[:, width:]) + vec[3:4, :]
    v_ref[...] = v.astype(bf16)


def project(tok, w, down, up, vec):
    tokens, width = tok.shape
    rows = 512
    row = pl.BlockSpec((rows, width), lambda i: (i, 0))
    return pl.pallas_call(
        project_kernel,
        grid=(tokens // rows,),
        in_specs=[row, resident(w), resident(down), resident(up), resident(vec)],
        out_specs=[row] * 3 + [pl.BlockSpec((rows, LANES), lambda i: (i, 0))],
        out_shape=[jax.ShapeDtypeStruct((tokens, width), bf16)] * 3
        + [jax.ShapeDtypeStruct((tokens, LANES), bf16)],
        compiler_params=params(),
        name="project",
    )(tok, w, down, up, vec)


def document_of(place, starts):
    number = jnp.zeros(place.shape, jnp.int32)
    for start in starts:
        number = number + (place >= start).astype(jnp.int32)
    return number


def fill_masks(lengths, slot, mask, blocks):
    starts = []
    total = jnp.int32(0)
    for d in range(lengths.shape[1]):
        starts.append(total)
        total = total + lengths[slot, d]
    for qb in range(blocks):
        first = max(0, qb - BAND + 1)
        rows = (qb - first + 1) * LANES
        key = first * LANES + lax.broadcasted_iota(jnp.int32, (rows, LANES), 0)
        query = qb * LANES + lax.broadcasted_iota(jnp.int32, (rows, LANES), 1)
        ok = (document_of(key, starts) == document_of(query, starts)) & (key <= query)
        mask[qb, :rows, :] = jnp.where(ok, 0.0, MASKED)


def half_lanes():
    return lax.broadcasted_iota(jnp.int32, (LANES, LANES), 1) < 64


def half_rows():
    return lax.broadcasted_iota(jnp.int32, (LANES, LANES), 0) < 64


def split_heads(x, left):
    zero = jnp.zeros_like(x)
    return jnp.concatenate([jnp.where(left, x, zero), jnp.where(left, zero, x)], axis=0)


def pipelined(units, stages, lags):
    for t in range(len(units) + lags[-1]):
        for stage, lag in zip(stages, lags):
            if 0 <= t - lag < len(units):
                stage(units[t - lag])


def geometry(qb):
    first = max(0, qb - BAND + 1)
    return first * LANES, (qb - first + 1) * LANES


def attend_kernel(pairs, blocks, lengths, q_ref, k_ref, v_ref, o_ref, p_ref, linv_ref, mask):
    @pl.when(pl.program_id(1) == 0)
    def _():
        fill_masks(lengths, pl.program_id(0), mask, blocks)

    left, top = half_lanes(), half_rows()
    scores, probs = {}, {}

    def score(unit):
        pair, qb = unit
        cols = slice(pair * PAIR, (pair + 1) * PAIR)
        key0, rows = geometry(qb)
        q = split_heads(q_ref[qb * LANES : (qb + 1) * LANES, cols], left)
        scores[unit] = dot_nt(k_ref[key0 : key0 + rows, cols], q)

    def soften(unit):
        pair, qb = unit
        key0, rows = geometry(qb)
        bias = mask[qb, :rows, :]
        s = scores.pop(unit) + jnp.concatenate([bias, bias], axis=1)
        p = jnp.exp2(s - jnp.max(s, axis=0, keepdims=True))
        linv = 1.0 / jnp.sum(p, axis=0, keepdims=True)
        linv_ref[0, pair, qb : qb + 1, :] = linv
        low = p.astype(bf16)
        p_ref[0, pair, qb, :rows, :] = low
        probs[unit] = (low, linv)

    def mix(unit):
        pair, qb = unit
        cols = slice(pair * PAIR, (pair + 1) * PAIR)
        key0, rows = geometry(qb)
        low, linv = probs.pop(unit)
        o = dot_tn(v_ref[key0 : key0 + rows, cols], low)
        o = jnp.where(top, o[:, :LANES] * linv[:, :LANES], o[:, LANES:] * linv[:, LANES:])
        o_ref[qb * LANES : (qb + 1) * LANES, cols] = o.T.astype(bf16)

    units = [(pair, qb) for qb in range(blocks) for pair in range(pairs)]
    pipelined(units, (score, soften, mix), (0, 2, 5))


def attend(lengths, q, k, v):
    slots = lengths.shape[0]
    tokens, width = q.shape
    seq = tokens // slots
    blocks, heads2, pairs = seq // LANES, width // PAIR, 2
    rows = BAND * LANES
    tile = pl.BlockSpec((seq, pairs * PAIR), lambda s, h, _: (s, h))
    return pl.pallas_call(
        functools.partial(attend_kernel, pairs, blocks),
        grid_spec=pltpu.PrefetchScalarGridSpec(
            num_scalar_prefetch=1,
            grid=(slots, heads2 // pairs),
            in_specs=[tile] * 3,
            out_specs=[
                tile,
                pl.BlockSpec((1, pairs, blocks, rows, 2 * LANES), lambda s, h, _: (s, h, 0, 0, 0)),
                pl.BlockSpec((1, pairs, blocks, 2 * LANES), lambda s, h, _: (s, h, 0, 0)),
            ],
            scratch_shapes=[pltpu.VMEM((blocks, rows, LANES), f32)],
        ),
        out_shape=[
            jax.ShapeDtypeStruct(q.shape, bf16),
            jax.ShapeDtypeStruct((slots, heads2, blocks, rows, 2 * LANES), bf16),
            jax.ShapeDtypeStruct((slots, heads2, blocks, 2 * LANES), f32),
        ],
        compiler_params=params(),
        name="attend",
    )(lengths, q, k, v)


def attend_back_kernel(
    pairs, blocks, q_ref, k_ref, v_ref, g_ref, o_ref, p_ref, linv_ref, dq_ref, dk_ref, dv_ref, dk_sum, dv_sum
):
    left, top = half_lanes(), half_rows()
    ones = jnp.ones((BAND * LANES, LANES), bf16)
    dk_sum[...] = jnp.zeros_like(dk_sum)
    dv_sum[...] = jnp.zeros_like(dv_sum)
    first, second = {}, {}

    def grad_probs(unit):
        pair, qb = unit
        cols = slice(pair * PAIR, (pair + 1) * PAIR)
        key0, rows = geometry(qb)
        here = slice(qb * LANES, (qb + 1) * LANES)
        linv = linv_ref[0, pair, qb : qb + 1, :]
        linv = jnp.where(top, linv[:, :LANES], linv[:, LANES:]).T
        g = g_ref[here, cols].astype(f32) * linv
        delta = split_heads(-(g * o_ref[here, cols].astype(f32)).astype(bf16), left)
        g = split_heads(g.astype(bf16), left)
        values = jnp.concatenate([v_ref[key0 : key0 + rows, cols], ones[:rows]], axis=1)
        first[unit] = (dot_nt(values, jnp.concatenate([g, delta], axis=1)), g)

    def grad_values(unit):
        pair, qb = unit
        cols = slice(pair * PAIR, (pair + 1) * PAIR)
        key0, rows = geometry(qb)
        dp, g = first.pop(unit)
        low = p_ref[0, pair, qb, :rows, :]
        second[unit] = low * dp.astype(bf16)
        dv_sum[key0 : key0 + rows, cols] += dot(low, g)

    def grad_queries_keys(unit):
        pair, qb = unit
        cols = slice(pair * PAIR, (pair + 1) * PAIR)
        key0, rows = geometry(qb)
        here = slice(qb * LANES, (qb + 1) * LANES)
        ds = second.pop(unit)
        dk_sum[key0 : key0 + rows, cols] += dot(ds, split_heads(q_ref[here, cols], left))
        dq = dot_tn(k_ref[key0 : key0 + rows, cols], ds)
        dq = jnp.where(top, dq[:, :LANES], dq[:, LANES:]) * 0.125
        dq_ref[here, cols] = dq.T.astype(bf16)

    units = [(pair, qb) for qb in range(blocks) for pair in range(pairs)]
    pipelined(units, (grad_probs, grad_values, grad_queries_keys), (0, 2, 4))
    dk_ref[...] = (dk_sum[...] * (0.125 / SCORE_SCALE)).astype(bf16)
    dv_ref[...] = dv_sum[...].astype(bf16)


def attend_back(slots, q, k, v, g, o, p, linv):
    tokens, width = q.shape
    seq = tokens // slots
    blocks, heads2, pairs = seq // LANES, width // PAIR, 2
    rows = BAND * LANES
    tile = pl.BlockSpec((seq, pairs * PAIR), lambda s, h: (s, h))
    return pl.pallas_call(
        functools.partial(attend_back_kernel, pairs, blocks),
        grid=(slots, heads2 // pairs),
        in_specs=[tile] * 5
        + [
            pl.BlockSpec((1, pairs, blocks, rows, 2 * LANES), lambda s, h: (s, h, 0, 0, 0)),
            pl.BlockSpec((1, pairs, blocks, 2 * LANES), lambda s, h: (s, h, 0, 0)),
        ],
        out_specs=[tile] * 3,
        scratch_shapes=[pltpu.VMEM((seq, pairs * PAIR), f32)] * 2,
        out_shape=[jax.ShapeDtypeStruct(q.shape, bf16)] * 3,
        compiler_params=params(),
        name="attend_back",
    )(q, k, v, g, o, p, linv)


def feed_chunk(normed, cot, up, down, bias):
    act, slope = gelu_and_slope(dot(normed, up) + bias)
    grad = slope * dot_nt(cot, down)
    return dot(act.astype(bf16), down), dot_nt(grad.astype(bf16), up)


def feed_first_kernel(tok, att, cot, wo, up, down, vec, bias, h1_ref, normed_ref, sum_o, sum_g):
    h1 = tok[...].astype(f32) + dot(att[...], wo[...]) + vec[4:5, :]
    h1_ref[...] = h1
    n, _ = normalise(h1)
    normed = (n * vec[7:8, :] + vec[1:2, :]).astype(bf16)
    normed_ref[...] = normed
    sum_o[...], sum_g[...] = feed_chunk(normed, cot[...], up[...], down[...], bias[...])


def feed_middle_kernel(normed, cot, old_o, old_g, up, down, bias, sum_o, sum_g):
    o, g = feed_chunk(normed[...], cot[...], up[...], down[...], bias[...])
    sum_o[...] = old_o[...] + o
    sum_g[...] = old_g[...] + g


def feed_last_kernel(h1, normed, cot, old_o, old_g, wo, up, down, vec, bias, out_ref, gh_ref, ga_ref):
    o, g = feed_chunk(normed[...], cot[...], up[...], down[...], bias[...])
    x = h1[...]
    out_ref[...] = (x + (old_o[...] + o) + vec[5:6, :]).astype(bf16)
    n, r = normalise(x)
    grad = cot[...].astype(f32) + norm_back(n, r, (old_g[...] + g) * vec[7:8, :])
    low = grad.astype(bf16)
    gh_ref[...] = low
    ga_ref[...] = dot_nt(low, wo[...]).astype(bf16)


def feed_call(kernel, name, rowwise, shared, out_types):
    tokens, width = rowwise[0].shape
    rows = 512
    row = pl.BlockSpec((rows, width), lambda i: (i, 0))
    return pl.pallas_call(
        kernel,
        grid=(tokens // rows,),
        in_specs=[row] * len(rowwise) + [resident(a) for a in shared],
        out_specs=[row] * len(out_types),
        out_shape=[jax.ShapeDtypeStruct((tokens, width), t) for t in out_types],
        compiler_params=params(),
        name=name,
    )(*rowwise, *shared)


def adapter_kernel(tok, dq, dv, low, up, vec, glow_ref, grads):
    width = tok.shape[1]
    n, _ = normalise(tok[...].astype(f32))
    normed = (n * vec[6:7, :] + vec[0:1, :]).astype(bf16)
    glow = (dot_nt(dq[...], up[:, :width]) + dot_nt(dv[...], up[:, width:])).astype(bf16)
    glow_ref[...] = glow
    part = jnp.concatenate(
        [
            dot_tn(low[...], dq[...])[0:4] * 8.0,
            dot_tn(low[...], dv[...])[4:8] * 8.0,
            dot_tn(glow, normed)[0:8],
        ],
        axis=0,
    )

    @pl.when(pl.program_id(0) == 0)
    def _():
        grads[...] = part

    @pl.when(pl.program_id(0) != 0)
    def _():
        grads[...] += part


def adapter_grads(tok, dq, dv, low, up, vec):
    tokens, width = tok.shape
    rows = 1024
    row = pl.BlockSpec((rows, width), lambda i: (i, 0))
    thin = pl.BlockSpec((rows, LANES), lambda i: (i, 0))
    return pl.pallas_call(
        adapter_kernel,
        grid=(tokens // rows,),
        in_specs=[row, row, row, thin, resident(up), resident(vec)],
        out_specs=[thin, pl.BlockSpec((16, width), lambda i: (0, 0))],
        out_shape=[jax.ShapeDtypeStruct((tokens, LANES), bf16), jax.ShapeDtypeStruct((16, width), f32)],
        compiler_params=params(),
        name="adapter_grads",
    )(tok, dq, dv, low, up, vec)


def input_kernel(tok, gh, dq, dk, dv, glow, w, down, vec, out_ref):
    width = tok.shape[1]
    g = dot_nt(dq[...], w[:, :width])
    g = g + dot_nt(dk[...], w[:, width : 2 * width])
    g = g + dot_nt(dv[...], w[:, 2 * width :])
    g = g + dot_nt(glow[...], down[...])
    n, r = normalise(tok[...].astype(f32))
    out_ref[...] = (gh[...].astype(f32) + norm_back(n, r, g * vec[6:7, :])).astype(bf16)


def input_grad(tok, gh, dq, dk, dv, glow, w, down, vec):
    tokens, width = tok.shape
    rows = 512
    row = pl.BlockSpec((rows, width), lambda i: (i, 0))
    thin = pl.BlockSpec((rows, LANES), lambda i: (i, 0))
    return pl.pallas_call(
        input_kernel,
        grid=(tokens // rows,),
        in_specs=[row] * 5 + [thin, resident(w), resident(down), resident(vec)],
        out_specs=row,
        out_shape=jax.ShapeDtypeStruct((tokens, width), bf16),
        compiler_params=params(),
        name="input_grad",
    )(tok, gh, dq, dk, dv, glow, w, down, vec)


def per_device(
    tokens,
    document_length_list,
    joint_projection_weight,
    attention_out_weight,
    feed_up_weight,
    feed_down_weight,
    frozen_norm_gains,
    biases,
    hidden_up_bias,
    query_down_adapter,
    query_up_adapter,
    value_down_adapter,
    value_up_adapter,
    cotangent,
):
    micro, local, seq, width = tokens.shape
    slots = micro * local
    shards = width // joint_projection_weight.shape[0]
    hidden = feed_down_weight.shape[0]
    tok = tokens.reshape(slots * seq, width)
    cot = cotangent.reshape(slots * seq, width)
    lengths = document_length_list.reshape(slots, -1)

    small = jnp.concatenate([biases, frozen_norm_gains], axis=0)
    small = jnp.concatenate([small.reshape(-1), hidden_up_bias])
    small = lax.all_gather(small, "fsdp", axis=0, tiled=False).astype(f32)
    head = small.shape[1] - hidden
    vec = small[:, :head].reshape(shards, 8, width // shards).transpose(1, 0, 2).reshape(8, width)
    hidden_bias = small[:, head:]

    joint = lax.all_gather(joint_projection_weight, "fsdp", axis=0, tiled=True)
    wo = lax.all_gather(attention_out_weight, "fsdp", axis=0, tiled=True)

    chunks = 4
    part = hidden // chunks
    up_parts = feed_up_weight.reshape(-1, shards, chunks, part)
    feeds = []
    for j in range(chunks):
        up = up_parts[:, :, j, :].reshape(-1, shards * part)
        down = feed_down_weight[j * part : (j + 1) * part]
        up = lax.all_gather(up, "fsdp", axis=0, tiled=True)
        down = lax.all_gather(down, "fsdp", axis=0, tiled=True)
        bias = hidden_bias[:, j * part : (j + 1) * part].reshape(1, -1)
        feeds.append((up, down, bias))

    rank = query_down_adapter.shape[1]
    down_map = jnp.concatenate([query_down_adapter, value_down_adapter], axis=1)
    down_map = jnp.pad(down_map, ((0, 0), (0, LANES - 2 * rank)))
    zero = jnp.zeros_like(query_up_adapter)
    up_map = jnp.concatenate(
        [
            jnp.concatenate([query_up_adapter, zero], axis=1),
            jnp.concatenate([zero, value_up_adapter], axis=1),
        ],
        axis=0,
    )
    up_map = jnp.pad(up_map * 8, ((0, LANES - 2 * rank), (0, 0))).astype(bf16)

    q, k, v, low = project(tok, joint, down_map, up_map, vec)
    att, probs, linv = attend(lengths, q, k, v)

    up, down, bias = feeds[0]
    h1, normed, sum_o, sum_g = feed_call(
        feed_first_kernel, "feed_first", [tok, att, cot], [wo, up, down, vec, bias], [f32, bf16, f32, f32]
    )
    for up, down, bias in feeds[1:-1]:
        sum_o, sum_g = feed_call(
            feed_middle_kernel, "feed_middle", [normed, cot, sum_o, sum_g], [up, down, bias], [f32, f32]
        )
    up, down, bias = feeds[-1]
    out, gh, ga = feed_call(
        feed_last_kernel,
        "feed_last",
        [h1, normed, cot, sum_o, sum_g],
        [wo, up, down, vec, bias],
        [bf16, bf16, bf16],
    )

    dq, dk, dv = attend_back(slots, q, k, v, ga, att, probs, linv)
    glow, grads = adapter_grads(tok, dq, dv, low, up_map, vec)
    grads = lax.all_gather(grads, ("dp", "fsdp"), axis=0, tiled=False)
    grad_in = input_grad(tok, gh, dq, dk, dv, glow, joint, down_map, vec)
    grads = jnp.sum(grads, axis=0)
    return (
        out.reshape(tokens.shape),
        grad_in.reshape(tokens.shape),
        grads[8:12].T,
        grads[0:4],
        grads[12:16].T,
        grads[4:8],
    )


def solution(mesh):
    slots = P(None, ("dp", "fsdp"), None, None)
    return jax.shard_map(
        per_device,
        mesh=mesh,
        in_specs=(
            slots,
            P(None, ("dp", "fsdp"), None),
            P("fsdp", None),
            P("fsdp", None),
            P("fsdp", None),
            P("fsdp", None),
            P(None, "fsdp"),
            P(None, "fsdp"),
            P("fsdp"),
            P(),
            P(),
            P(),
            P(),
            slots,
        ),
        out_specs=(slots, slots, P(), P(), P(), P()),
        check_vma=False,
    )
```

```python
import functools
import math

import jax
import jax.numpy as jnp
from jax import lax
from jax.experimental import pallas as pl
from jax.experimental.pallas import tpu as pltpu
from jax.sharding import PartitionSpec as P

f32 = jnp.float32
bf16 = jnp.bfloat16
LANES = 128
PAIR = 128
BAND = 3
EPS = 1e-5
MASKED = -1e30
SCORE_SCALE = 0.125 * math.log2(math.e)
GELU_C = math.sqrt(2.0 / math.pi)
VMEM_LIMIT = 58 * 2**20
COST = 8
NT = (((1,), (1,)), ((), ()))
TN = (((0,), (0,)), ((), ()))


def dot(a, b):
    return jnp.dot(a, b, preferred_element_type=f32)


def dot_nt(a, b):
    return lax.dot_general(a, b, NT, preferred_element_type=f32)


def dot_tn(a, b):
    return lax.dot_general(a, b, TN, preferred_element_type=f32)


def params():
    return pltpu.CompilerParams(vmem_limit_bytes=VMEM_LIMIT)


def resident(array):
    zeros = (0,) * array.ndim
    return pl.BlockSpec(array.shape, lambda *_: zeros, pipeline_mode=pl.Buffered(1))


def normalise(x):
    centred = x - jnp.mean(x, axis=-1, keepdims=True)
    r = lax.rsqrt(jnp.mean(centred * centred, axis=-1, keepdims=True) + EPS)
    return centred * r, r


def norm_back(n, r, w):
    return r * (w - jnp.mean(w, axis=-1, keepdims=True) - n * jnp.mean(w * n, axis=-1, keepdims=True))


def gelu_and_slope(x):
    x2 = x * x
    t = jnp.tanh(x * (GELU_C + (GELU_C * 0.044715) * x2))
    half = 0.5 + 0.5 * t
    slope = half + (0.5 * x) * ((1.0 - t * t) * (GELU_C + (3 * GELU_C * 0.044715) * x2))
    return x * half, slope


def ring_pairs(dp, fsdp, move):
    pairs = []
    for d in range(dp):
        for f in range(fsdp):
            e, g = move(d, f)
            pairs.append((d * fsdp + f, e * fsdp + g))
    return pairs


def after(x, others):
    return lax.optimization_barrier((x, others))[0]


def after_all(xs, others):
    return lax.optimization_barrier((xs, others))[0]


class Gather:
    def __init__(self, dp, fsdp):
        self.dp, self.fsdp = dp, fsdp

    def move(self, x, where):
        return lax.ppermute(x, ("dp", "fsdp"), ring_pairs(self.dp, self.fsdp, where))

    def step_1(self, mine):
        fsdp = self.fsdp
        return [self.move(mine, lambda d, f, k=k: (d, (f + 2 * k) % fsdp)) for k in range(1, fsdp // 2)]

    def step_2(self, near):
        near = jnp.broadcast_to(near[None], (self.dp,) + near.shape)
        return lax.all_to_all(near, "dp", 0, 0, tiled=False)

    def step_3(self, far):
        return [far, self.swap(far)]

    def swap(self, x):
        return self.move(x, lambda d, f: (d, f ^ 1))


def copies(weight, refs, whole, sems, place, cols):
    made = []
    start, size = cols

    def add(source, first, at, rows):
        target = whole.at[pl.ds(at, rows), pl.ds(start, size)]
        made.append(pltpu.make_async_copy(source.at[:, pl.ds(first + start, size)], target, sems.at[len(made)]))

    if len(weight) == 1:
        add(refs[0], 0, 0, whole.shape[0])
        return made
    offset = weight[-1]
    index = place[1]
    rows = refs[0].shape[0]
    fsdp = whole.shape[0] // rows
    dp, near, _ = refs[2].shape
    part = near // (fsdp // 2 - 1)
    core = lax.rem(index, 2)
    for swapped in (0, 1):
        owner = index + swapped * (1 - 2 * core)
        add(refs[swapped], offset, pl.multiple_of(owner * rows, rows), rows)
        for e in range(dp):
            for k in range(1, fsdp // 2):
                owner = lax.rem(index + fsdp - 2 * k, fsdp) + swapped * (1 - 2 * core)
                at = pl.multiple_of(owner * rows + e * part, part)
                add(refs[2 + swapped].at[e, pl.ds((k - 1) * part, part)], 0, at, part)
    return made


def copy_count(weight, fsdp):
    return 1 if len(weight) == 1 else 2 + 2 * weight[2].shape[0] * (fsdp // 2 - 1)


def weight_call(kernel, name, weights, order, grid, blocked, in_specs, out_specs, out_shape, scratch, place, cost, fsdp, old=()):
    arrays = [w if len(w) == 1 else w[:-1] for w, _ in weights]
    flat = [a for some in arrays for a in some]
    counts = [copy_count(weights[i][0], fsdp) for i, _, _ in order]

    def body(place_ref, *refs):
        refs = list(refs)
        take = lambda n: [refs.pop(0) for _ in range(n)]
        sources = [take(len(some)) for some in arrays]
        ins, _, outs = take(len(blocked)), take(len(old)), take(len(out_shape))
        wholes, sems = take(len(weights)), take(len(order))

        first_step = pl.program_id(0) == 0
        for axis in range(1, len(grid)):
            first_step = first_step & (pl.program_id(axis) == 0)

        def group(n):
            i, start, size = order[n]
            return copies(weights[i][0], sources[i], wholes[i], sems[n], place_ref, (start, size))

        @pl.when(first_step)
        def _():
            for n in range(len(order)):
                for copy in group(n):
                    copy.start()

        def wait(n):
            @pl.when(first_step)
            def _():
                for copy in group(n):
                    copy.wait()

        kernel(wholes, wait, ins, outs, refs)

    return pl.pallas_call(
        body,
        grid_spec=pltpu.PrefetchScalarGridSpec(
            num_scalar_prefetch=1,
            grid=grid,
            in_specs=[pl.BlockSpec(memory_space=pl.ANY)] * len(flat)
            + in_specs
            + [pl.BlockSpec(memory_space=pl.ANY)] * len(old),
            out_specs=out_specs,
            scratch_shapes=[pltpu.VMEM(shape, bf16) for _, shape in weights]
            + [pltpu.SemaphoreType.DMA((n,)) for n in counts]
            + scratch,
        ),
        out_shape=out_shape,
        compiler_params=params(),
        cost_estimate=pl.CostEstimate(flops=cost // COST, bytes_accessed=2**20, transcendentals=0),
        input_output_aliases={1 + len(flat) + len(blocked) + i: i for i in range(len(old))},
        name=name,
    )(place, *flat, *blocked, *old)


def own_quarter(rows):
    return pl.ds(pl.multiple_of(lax.axis_index("dp") * rows, rows), rows)


def stack_rows(arrays, rows):
    arrays = [a.astype(f32) for a in arrays]
    used = sum(a.shape[0] for a in arrays)
    return jnp.concatenate(arrays + [jnp.zeros((rows - used, arrays[0].shape[1]), f32)], axis=0).astype(bf16)


def cut_kernel(joint, biases, gains, hidden, first, second, quarter):
    half = second.shape[1] // 3
    for i in range(3):
        first[:, i * half : (i + 1) * half] = joint[:, 2 * i * half : (2 * i + 1) * half]
        second[:, i * half : (i + 1) * half] = joint[:, (2 * i + 1) * half : (2 * i + 2) * half]
    small = [biases[...], gains[...]] + [hidden[:, i : i + LANES] for i in range(0, hidden.shape[1], LANES)]
    first[:, 3 * half :] = stack_rows(small, first.shape[0])
    rows = own_quarter(quarter.shape[0])
    quarter[:, : first.shape[1]] = first[rows, :]
    quarter[:, first.shape[1] :] = second[rows, :]


def local_call(kernel, name, shapes, arrays):
    return pl.pallas_call(
        kernel,
        out_shape=[jax.ShapeDtypeStruct(s, bf16) for s in shapes],
        compiler_params=params(),
        name=name,
    )(*arrays)


def cut(joint, biases, gains, hidden, dp):
    rows, width = joint.shape
    shapes = [(rows, width // 2 + LANES), (rows, width // 2), (rows // dp, width + LANES)]
    return local_call(cut_kernel, "cut", shapes, [joint, biases, gains, hidden])


def pack_kernel(chunks, shards, up, down, wo, q_down, q_up, v_down, v_up, *refs):
    outs, parts = refs[:chunks], refs[chunks : chunks + 2]
    down_map, up_map = refs[chunks + 2 :]
    hidden, width = down.shape
    part = hidden // chunks
    for j, out in enumerate(outs):
        for s in range(shards):
            start = s * hidden + j * part
            out[:, s * part : (s + 1) * part] = up[:, start : start + part]
        out[:, width : 2 * width] = down[j * part : (j + 1) * part, :]
    outs[0][:, 2 * width :] = wo[...]
    for out, part_ref in zip((outs[1], outs[3]), parts):
        part_ref[...] = out[own_quarter(part_ref.shape[0]), :]
    rank = q_up.shape[0]
    down_map[...] = jnp.zeros_like(down_map)
    down_map[:, :rank] = q_down[...]
    down_map[:, rank : 2 * rank] = v_down[...]
    zero = jnp.zeros(q_up.shape, f32)
    rows = [jnp.concatenate([q_up[...].astype(f32) * 8.0, zero], axis=1)]
    rows += [jnp.concatenate([zero, v_up[...].astype(f32) * 8.0], axis=1)]
    up_map[...] = stack_rows(rows, up_map.shape[0])


def pack(up, down, wo, adapters, chunks, shards, dp):
    rows, width = up.shape[0], down.shape[1]
    columns = [3 * width, 2 * width, 2 * width, 2 * width]
    shapes = [(rows, c) for c in columns] + [(rows // dp, columns[j]) for j in (1, 3)]
    shapes += [(width, LANES), (LANES, 2 * width)]
    return local_call(functools.partial(pack_kernel, chunks, shards), "pack", shapes, [up, down, wo, *adapters])


def project_slot(first, carried, shards, w, wait, ins, outs):
    rows_in, down, up = ins[:3]
    q_ref, k_ref, v_ref = outs[:3]
    half = q_ref.shape[1]
    width = 2 * half
    cols = slice(0, half) if first else slice(half, width)
    wait(0)
    if first:
        low_ref, normed_ref, vec = outs[3:6]

        @pl.when(pl.program_id(0) == 0)
        def _():
            if carried:
                rows = w.shape[0] // shards
                parts = [w[s * rows : s * rows + vec.shape[0], 3 * half :] for s in range(shards)]
                vec[...] = jnp.concatenate(parts, axis=1).astype(f32)
            else:
                vec[...] = ins[3][...]
    else:
        low_in, vec = ins[3:]
    sub = 256
    state = {}

    def norm(r):
        rr = slice(r, r + sub)
        if first:
            n, _ = normalise(rows_in[rr, :].astype(f32))
            normed = (n * vec[6:7, :] + vec[0:1, :]).astype(bf16)
            normed_ref[rr, :] = normed
        else:
            normed = rows_in[rr, :]
        state[r] = normed

    def mix(r):
        rr = slice(r, r + sub)
        normed = state.pop(r)
        k_ref[rr, :] = dot(normed, w[:, half : 2 * half]).astype(bf16)
        if first:
            low = dot(normed, down[...]).astype(bf16)
            low_ref[rr, :] = low
        else:
            low = low_in[rr, :]
        q = dot(normed, w[:, :half]) + dot(low, up[:, cols]) + vec[2:3, cols]
        q_ref[rr, :] = (q * SCORE_SCALE).astype(bf16)
        v = dot(normed, w[:, 2 * half : 3 * half]) + dot(low, up[:, width:][:, cols]) + vec[3:4, cols]
        v_ref[rr, :] = v.astype(bf16)

    pipelined(list(range(0, rows_in.shape[0], sub)), (norm, mix), (0, 1))


def heads_kernel(first, carried, shards, pairs, wholes, wait, ins, outs, scratch):
    lengths, ins = ins[0], ins[1:]
    q_ref, k_ref, v_ref = outs[:3]
    o_ref, p_ref, linv_ref = outs[-3:]
    (mask,) = scratch
    blocks = q_ref.shape[0] // LANES

    @pl.when(pl.program_id(1) == 0)
    def _():
        project_slot(first, carried, shards, wholes[0], wait, ins, outs)
        fill_masks(lengths, pl.program_id(0), mask, blocks)

    @pl.when(pl.program_id(1) != 0)
    def _():
        at = pl.multiple_of((pl.program_id(1) - 1) * pairs * PAIR, pairs * PAIR)
        attend_pairs(pairs, blocks, at, q_ref, k_ref, v_ref, o_ref, p_ref, linv_ref, mask)


def heads(weight, place, fsdp, lengths, x, down, up, vec=None, low=None, old=()):
    tokens, width = x.shape
    slots = lengths.shape[0]
    seq = tokens // slots
    blocks, heads2, pairs = seq // LANES, width // PAIR, 2
    steps = heads2 // pairs // 2
    first = low is None
    here = 0 if first else 1
    row = pl.BlockSpec((seq, width), lambda s, j, _: (s, 0))
    thin = pl.BlockSpec((seq, LANES), lambda s, j, _: (s, 0))
    half = pl.BlockSpec((seq, width // 2), lambda s, j, _: (s, here))
    group = lambda j: here * steps + jnp.maximum(j - 1, 0)
    tile = pl.BlockSpec((seq, pairs * PAIR), lambda s, j, _: (s, group(j)))
    probs = (pairs, blocks, BAND * LANES, 2 * LANES)
    sums = (pairs, blocks, 2 * LANES)
    ins = [lengths, x, down, up]
    in_specs = [pl.BlockSpec(memory_space=pltpu.SMEM), row, resident(down), resident(up)]
    outs, out_specs = [jax.ShapeDtypeStruct((tokens, width), bf16)] * 3, [half] * 3
    if first:
        outs = outs + [jax.ShapeDtypeStruct((tokens, n), bf16) for n in (LANES, width)]
        outs = outs + [jax.ShapeDtypeStruct((16, width), f32)]
        out_specs = out_specs + [thin, row, pl.BlockSpec((16, width), lambda s, j, _: (0, 0))]
    else:
        ins, in_specs = ins + [low], in_specs + [thin]
    if vec is not None:
        ins, in_specs = ins + [vec], in_specs + [resident(vec)]
    outs = outs + [
        jax.ShapeDtypeStruct((tokens, width), bf16),
        jax.ShapeDtypeStruct((slots, heads2) + probs[1:], bf16),
        jax.ShapeDtypeStruct((slots, heads2) + sums[1:], f32),
    ]
    out_specs = out_specs + [
        tile,
        pl.BlockSpec((1,) + probs, lambda s, j, _: (s, group(j), 0, 0, 0)),
        pl.BlockSpec((1,) + sums, lambda s, j, _: (s, group(j), 0, 0)),
    ]
    carried = first and vec is None
    columns = 3 * width // 2 + (LANES if carried else 0)
    return weight_call(
        functools.partial(heads_kernel, first, carried, fsdp, pairs),
        "heads",
        [(weight, (width, columns))],
        [(0, 0, columns)],
        (slots, 1 + steps),
        ins,
        in_specs,
        out_specs,
        outs,
        [pltpu.VMEM((blocks, BAND * LANES, LANES), f32)],
        place,
        9 * tokens * width * width,
        fsdp,
        old,
    )


def fill_masks(lengths, slot, mask, blocks):
    starts = []
    total = jnp.int32(0)
    for d in range(lengths.shape[1]):
        starts.append(total)
        total = total + lengths[slot, d]
    for qb in range(blocks):
        first = max(0, qb - BAND + 1)
        rows = (qb - first + 1) * LANES
        query = qb * LANES + lax.broadcasted_iota(jnp.int32, (8, LANES), 1)
        begin = jnp.zeros((8, LANES), jnp.int32)
        for start in starts:
            begin = jnp.where(query >= start, start, begin)
        key = first * LANES + lax.broadcasted_iota(jnp.int32, (rows, LANES), 0)
        ok = (key >= begin[0:1]) & (key <= query[0:1])
        mask[qb, :rows, :] = jnp.where(ok, 0.0, MASKED)


def half_lanes():
    return lax.broadcasted_iota(jnp.int32, (LANES, LANES), 1) < 64


def half_rows():
    return lax.broadcasted_iota(jnp.int32, (LANES, LANES), 0) < 64


def split_heads(x, left):
    zero = jnp.zeros_like(x)
    return jnp.concatenate([jnp.where(left, x, zero), jnp.where(left, zero, x)], axis=0)


def pipelined(units, stages, lags):
    for t in range(len(units) + lags[-1]):
        for stage, lag in zip(stages, lags):
            if 0 <= t - lag < len(units):
                stage(units[t - lag])


def geometry(qb):
    first = max(0, qb - BAND + 1)
    return first * LANES, (qb - first + 1) * LANES


def attend_pairs(pairs, blocks, at, q_ref, k_ref, v_ref, o_ref, p_ref, linv_ref, mask):
    left, top = half_lanes(), half_rows()
    scores, probs = {}, {}

    def score(unit):
        pair, qb = unit
        cols = pl.ds(at + pair * PAIR, PAIR)
        key0, rows = geometry(qb)
        q = split_heads(q_ref[qb * LANES : (qb + 1) * LANES, cols], left)
        scores[unit] = dot_nt(k_ref[key0 : key0 + rows, cols], q)

    def soften(unit):
        pair, qb = unit
        key0, rows = geometry(qb)
        bias = mask[qb, :rows, :]
        s = scores.pop(unit) + jnp.concatenate([bias, bias], axis=1)
        p = jnp.exp2(s - jnp.max(s, axis=0, keepdims=True))
        linv = 1.0 / jnp.sum(p, axis=0, keepdims=True)
        linv_ref[0, pair, qb : qb + 1, :] = linv
        low = p.astype(bf16)
        p_ref[0, pair, qb, :rows, :] = low
        probs[unit] = (low, linv)

    def mix(unit):
        pair, qb = unit
        key0, rows = geometry(qb)
        low, linv = probs.pop(unit)
        o = dot_tn(v_ref[key0 : key0 + rows, pl.ds(at + pair * PAIR, PAIR)], low)
        o = jnp.where(top, o[:, :LANES] * linv[:, :LANES], o[:, LANES:] * linv[:, LANES:])
        o_ref[qb * LANES : (qb + 1) * LANES, pair * PAIR : (pair + 1) * PAIR] = o.T.astype(bf16)

    units = [(pair, qb) for qb in range(blocks) for pair in range(pairs)]
    pipelined(units, (score, soften, mix), (0, 2, 5))


def attend_back_kernel(
    pairs, blocks, q_ref, k_ref, v_ref, g_ref, o_ref, p_ref, linv_ref, low, normed, up, *refs
):
    dq_ref, dk_ref, dv_ref, glow_ref, grads, dk_sum, dv_sum, glow_sum = refs
    left, top = half_lanes(), half_rows()
    ones = jnp.ones((BAND * LANES, LANES), bf16)
    dk_sum[...] = jnp.zeros_like(dk_sum)
    dv_sum[...] = jnp.zeros_like(dv_sum)
    first, second = {}, {}

    def grad_probs(unit):
        pair, qb = unit
        cols = slice(pair * PAIR, (pair + 1) * PAIR)
        key0, rows = geometry(qb)
        here = slice(qb * LANES, (qb + 1) * LANES)
        linv = linv_ref[0, pair, qb : qb + 1, :]
        linv = jnp.where(top, linv[:, :LANES], linv[:, LANES:]).T
        g = g_ref[here, cols].astype(f32) * linv
        delta = split_heads(-(g * o_ref[here, cols].astype(f32)).astype(bf16), left)
        g = split_heads(g.astype(bf16), left)
        values = jnp.concatenate([v_ref[key0 : key0 + rows, cols], ones[:rows]], axis=1)
        first[unit] = (dot_nt(values, jnp.concatenate([g, delta], axis=1)), g)

    def grad_values(unit):
        pair, qb = unit
        cols = slice(pair * PAIR, (pair + 1) * PAIR)
        key0, rows = geometry(qb)
        dp, g = first.pop(unit)
        low = p_ref[0, pair, qb, :rows, :]
        second[unit] = low * dp.astype(bf16)
        dv_sum[key0 : key0 + rows, cols] += dot(low, g)

    def grad_queries_keys(unit):
        pair, qb = unit
        cols = slice(pair * PAIR, (pair + 1) * PAIR)
        key0, rows = geometry(qb)
        here = slice(qb * LANES, (qb + 1) * LANES)
        ds = second.pop(unit)
        dk_sum[key0 : key0 + rows, cols] += dot(ds, split_heads(q_ref[here, cols], left))
        dq = dot_tn(k_ref[key0 : key0 + rows, cols], ds)
        dq = jnp.where(top, dq[:, :LANES], dq[:, LANES:]) * 0.125
        dq_ref[here, cols] = dq.T.astype(bf16)

    units = [(pair, qb) for qb in range(blocks) for pair in range(pairs)]
    pipelined(units, (grad_probs, grad_values, grad_queries_keys), (0, 2, 4))
    dk_ref[...] = (dk_sum[...] * (0.125 / SCORE_SCALE)).astype(bf16)
    dv_ref[...] = dv_sum[...].astype(bf16)

    slot, step, last = pl.program_id(0), pl.program_id(1), pl.num_programs(1) - 1
    width = normed.shape[1]
    at = pl.multiple_of(step * pairs * PAIR, pairs * PAIR)
    here = pl.ds(at, pairs * PAIR)
    part = [dot_tn(low[...], dq_ref[...])[0:4], dot_tn(low[...], dv_ref[...])[4:8]]
    part = jnp.concatenate(part, axis=0) * 8.0
    grads[0:8, here] = jnp.where(slot == 0, part, grads[0:8, here] + part)
    glow = dot_nt(dq_ref[...], up[:, here]) + dot_nt(dv_ref[...], up[:, pl.ds(width + at, pairs * PAIR)])
    glow_sum[...] = jnp.where(step == 0, glow, glow_sum[...] + glow)

    @pl.when(step == last)
    def _():
        glow = glow_sum[...].astype(bf16)
        glow_ref[...] = glow
        part = dot_tn(glow, normed[...])[0:8]
        grads[8:16, :] = jnp.where(slot == 0, part, grads[8:16, :] + part)


def attend_back(slots, q, k, v, g, o, p, linv, low, normed, up):
    tokens, width = q.shape
    seq = tokens // slots
    blocks, heads2, pairs = seq // LANES, width // PAIR, 2
    rows = BAND * LANES
    tile = pl.BlockSpec((seq, pairs * PAIR), lambda s, h: (s, h))
    thin = pl.BlockSpec((seq, LANES), lambda s, h: (s, 0))
    return pl.pallas_call(
        functools.partial(attend_back_kernel, pairs, blocks),
        grid=(slots, heads2 // pairs),
        in_specs=[tile] * 5
        + [
            pl.BlockSpec((1, pairs, blocks, rows, 2 * LANES), lambda s, h: (s, h, 0, 0, 0)),
            pl.BlockSpec((1, pairs, blocks, 2 * LANES), lambda s, h: (s, h, 0, 0)),
            thin,
            pl.BlockSpec((seq, width), lambda s, h: (s, 0)),
            resident(up),
        ],
        out_specs=[tile] * 3 + [thin, pl.BlockSpec((16, width), lambda s, h: (0, 0))],
        scratch_shapes=[pltpu.VMEM((seq, pairs * PAIR), f32)] * 2 + [pltpu.VMEM((seq, LANES), f32)],
        out_shape=[jax.ShapeDtypeStruct(q.shape, bf16)] * 3
        + [jax.ShapeDtypeStruct((tokens, LANES), bf16), jax.ShapeDtypeStruct((16, width), f32)],
        compiler_params=params(),
        cost_estimate=pl.CostEstimate(flops=14 * tokens * width * width // COST, bytes_accessed=2**20, transcendentals=0),
        name="attend_back",
    )(q, k, v, g, o, p, linv, low, normed, up)


def feed_chunk(wait, first, normed, cot, w, bias):
    width = cot.shape[1]
    wait(first)
    wait(first + 1)
    size = width // 4
    acts, grads = [], []
    for i in range(0, width, size):
        grad = dot_nt(cot, w[i : i + size, width : 2 * width])
        act, slope = gelu_and_slope(dot(normed, w[:, i : i + size]) + bias[:, i : i + size])
        acts.append(act.astype(bf16))
        grads.append((slope * grad).astype(bf16))
    o = dot(jnp.concatenate(acts, axis=1), w[:, width : 2 * width])
    return o, dot_nt(jnp.concatenate(grads, axis=1), w[:, :width])


def feed_first_kernel(wholes, wait, ins, outs, _):
    tok, att, cot, vec = ins
    h1_ref, normed_ref, o_ref, g_ref = outs
    width = tok.shape[1]
    wait(0)
    h1 = tok[...].astype(f32) + dot(att[...], wholes[0][:, 2 * width :]) + vec[4:5, :]
    h1_ref[...] = h1
    n, _ = normalise(h1)
    normed = (n * vec[7:8, :] + vec[1:2, :]).astype(bf16)
    normed_ref[...] = normed
    o_ref[...], g_ref[...] = feed_chunk(wait, 1, normed, cot[...], wholes[0], vec[8:9, :])
    o, g = feed_chunk(wait, 3, normed, cot[...], wholes[1], vec[9:10, :])
    o_ref[...] += o
    g_ref[...] += g


def feed_last_kernel(wholes, wait, ins, outs, scratch):
    h1, normed, old_o, old_g, cot, vec = ins
    out_ref, gh_ref, ga_ref = outs
    o_sum, g_sum = scratch
    width = cot.shape[1]
    o, g = feed_chunk(wait, 0, normed[...], cot[...], wholes[0], vec[10:11, :])
    o_sum[...] = old_o[...] + o
    g_sum[...] = old_g[...] + g
    o, g = feed_chunk(wait, 2, normed[...], cot[...], wholes[1], vec[11:12, :])
    x = h1[...]
    out_ref[...] = (x + (o_sum[...] + o) + vec[5:6, :]).astype(bf16)
    n, r = normalise(x)
    grad = cot[...].astype(f32) + norm_back(n, r, (g_sum[...] + g) * vec[7:8, :])
    low = grad.astype(bf16)
    gh_ref[...] = low
    wait(4)
    ga_ref[...] = dot_nt(low, wholes[2][:, 2 * width :]).astype(bf16)


def feed_call(kernel, name, weights, order, place, fsdp, rowwise, vec, out_types, sums):
    tokens, width = rowwise[0].shape
    rows = 512
    row = pl.BlockSpec((rows, width), lambda i, _: (i, 0))
    return weight_call(
        kernel,
        name,
        weights,
        order,
        (tokens // rows,),
        rowwise + [vec],
        [row] * len(rowwise) + [resident(vec)],
        [row] * len(out_types),
        [jax.ShapeDtypeStruct((tokens, width), t) for t in out_types],
        [pltpu.VMEM((rows, width), f32)] * sums,
        place,
        18 * tokens * width * width,
        fsdp,
    )


def feed_first(feeds, place, fsdp, tok, att, cot, vec):
    width = tok.shape[1]
    weights = [(feeds[0], (width, 3 * width)), (feeds[1], (width, 2 * width))]
    order = [(0, 2 * width, width), (0, width, width), (0, 0, width), (1, width, width), (1, 0, width)]
    types = [f32, bf16, f32, f32]
    return feed_call(feed_first_kernel, "feed_first", weights, order, place, fsdp, [tok, att, cot], vec, types, 0)


def feed_last(feeds, place, fsdp, h1, normed, o, g, cot, vec):
    width = cot.shape[1]
    weights = [(feeds[2], (width, 2 * width)), (feeds[3], (width, 2 * width)), (feeds[0], (width, 3 * width))]
    order = [(0, width, width), (0, 0, width), (1, width, width), (1, 0, width), (2, 2 * width, width)]
    rowwise = [h1, normed, o, g, cot]
    return feed_call(feed_last_kernel, "feed_last", weights, order, place, fsdp, rowwise, vec, [bf16] * 3, 2)


def input_kernel(wholes, wait, ins, outs, _):
    tok, gh, dq, dk, dv, glow, down, vec = ins
    (out_ref,) = outs
    half = tok.shape[1] // 2
    g = dot_nt(glow[...], down[...])
    for i, w in enumerate(wholes):
        wait(i)
        cols = slice(i * half, (i + 1) * half)
        g = g + dot_nt(dq[:, cols], w[:, :half])
        g = g + dot_nt(dk[:, cols], w[:, half : 2 * half])
        g = g + dot_nt(dv[:, cols], w[:, 2 * half : 3 * half])
    n, r = normalise(tok[...].astype(f32))
    out_ref[...] = (gh[...].astype(f32) + norm_back(n, r, g * vec[6:7, :])).astype(bf16)


def input_grad(joint, place, fsdp, tok, gh, dq, dk, dv, glow, down, vec):
    tokens, width = tok.shape
    rows = 512
    row = pl.BlockSpec((rows, width), lambda i, _: (i, 0))
    thin = pl.BlockSpec((rows, LANES), lambda i, _: (i, 0))
    return weight_call(
        input_kernel,
        "input_grad",
        [(w, (width, 3 * width // 2)) for w in joint],
        [(0, 0, 3 * width // 2), (1, 0, 3 * width // 2)],
        (tokens // rows,),
        [tok, gh, dq, dk, dv, glow, down, vec],
        [row] * 5 + [thin, resident(down), resident(vec)],
        [row],
        [jax.ShapeDtypeStruct((tokens, width), bf16)],
        [],
        place,
        6 * tokens * width * width,
        fsdp,
    )[0]


def per_device(
    tokens,
    document_length_list,
    joint_projection_weight,
    attention_out_weight,
    feed_up_weight,
    feed_down_weight,
    frozen_norm_gains,
    biases,
    hidden_up_bias,
    query_down_adapter,
    query_up_adapter,
    value_down_adapter,
    value_up_adapter,
    cotangent,
):
    micro, local, seq, width = tokens.shape
    slots = micro * local
    shards = width // joint_projection_weight.shape[0]
    hidden = feed_down_weight.shape[0]
    tok = tokens.reshape(slots * seq, width)
    cot = cotangent.reshape(slots * seq, width)
    lengths = document_length_list.reshape(slots, -1)

    dp = lax.axis_size("dp")
    place = jnp.stack([lax.axis_index("dp"), lax.axis_index("fsdp")]).astype(jnp.int32)
    chunks = 4
    part = hidden // chunks
    stepped = dp == 4 and shards == 8 and part == LANES and width == shards * LANES

    def gather(x):
        return lax.all_gather(x, "fsdp", axis=0, tiled=True)

    adapters = [query_down_adapter, query_up_adapter, value_down_adapter, value_up_adapter]
    if stepped:
        hidden_bias = hidden_up_bias.reshape(1, -1)
        a, b, quarter = cut(joint_projection_weight, biases, frozen_norm_gains, hidden_bias, dp)
        link = Gather(dp, shards)
        near = link.step_1(quarter)
        up, down = after_all([feed_up_weight, feed_down_weight], quarter)
        *packed, down_map, up_map = pack(up, down, attention_out_weight, adapters, chunks, shards, dp)
        c0, c1, c2, c3, c1_part, c3_part = packed
        split = a.shape[1]
        a_far = link.step_2(jnp.concatenate([x[:, :split] for x in near], axis=0))
        c0, c1_part = after_all([c0, c1_part], near)
        feeds = [[gather(c0)]]
        c1_near = link.step_1(c1_part)
        near = jnp.concatenate([x[:, split:] for x in near], axis=0)
        b_far = link.step_2(after(near, a_far))
        joint = [[a, link.swap(a)] + link.step_3(a_far) + [0]]
        vec = None
    else:
        small = jnp.concatenate([biases, frozen_norm_gains], axis=0)
        small = lax.all_gather(small, "fsdp", axis=1, tiled=True)
        hidden_bias = lax.all_gather(hidden_up_bias, "fsdp", axis=0, tiled=False)
        hidden_bias = [hidden_bias[:, j * part : (j + 1) * part].reshape(1, -1) for j in range(chunks)]
        vec = jnp.concatenate([small] + hidden_bias, axis=0)
        vec = jnp.pad(vec, ((0, 16 - 8 - chunks), (0, 0))).astype(f32)
        third = [width * i // 2 for i in range(6)]
        joint = []
        for i in (0, 1):
            cols = [lax.slice_in_dim(joint_projection_weight, t, t + width // 2, axis=1) for t in third[i::2]]
            joint.append([gather(jnp.concatenate(cols, axis=1))])
        up_parts = feed_up_weight.reshape(-1, shards, chunks, part)
        feeds = []
        for j in range(chunks):
            cols = [up_parts[:, :, j, :].reshape(-1, shards * part), feed_down_weight[j * part : (j + 1) * part]]
            if j == 0:
                cols.append(attention_out_weight)
            feeds.append([gather(jnp.concatenate(cols, axis=1))])
        rank = query_down_adapter.shape[1]
        down_map = jnp.concatenate([query_down_adapter, value_down_adapter], axis=1)
        down_map = jnp.pad(down_map, ((0, 0), (0, LANES - 2 * rank)))
        zero = jnp.zeros_like(query_up_adapter)
        up_map = jnp.concatenate(
            [
                jnp.concatenate([query_up_adapter, zero], axis=1),
                jnp.concatenate([zero, value_up_adapter], axis=1),
            ],
            axis=0,
        )
        up_map = jnp.pad(up_map * 8, ((0, LANES - 2 * rank), (0, 0))).astype(bf16)

    q, k, v, low, normed, vec, *kept = heads(joint[0], place, shards, lengths, tok, down_map, up_map, vec)
    if stepped:
        b_far, *c1_near, q, c3_part = after_all([b_far] + c1_near + [q, c3_part], low)
        joint.append([b, link.swap(b)] + link.step_3(b_far) + [0])
        c1_far = link.step_2(jnp.concatenate(c1_near, axis=0))
        c3_near = link.step_1(c3_part)
    old = [q, k, v] + kept
    q, k, v, att, probs, linv = heads(joint[1], place, shards, lengths, normed, down_map, up_map, vec, low, old)
    if stepped:
        c1_far, *c3_near, att, c2 = after_all([c1_far] + c3_near + [att, c2], linv)
        c3_far = link.step_2(jnp.concatenate(c3_near, axis=0))
        feeds += [[c1, link.swap(c1)] + link.step_3(c1_far) + [0], [gather(c2)]]
    h1, normed_2, o, g = feed_first(feeds, place, shards, tok, att, cot, vec)
    if stepped:
        c3_far, o = after_all([c3_far, o], h1)
        feeds.append([c3, link.swap(c3)] + link.step_3(c3_far) + [0])
    out, gh, ga = feed_last(feeds, place, shards, h1, normed_2, o, g, cot, vec)

    dq, dk, dv, glow, grads = attend_back(slots, q, k, v, ga, att, probs, linv, low, normed, up_map)
    if stepped:
        total = Gather(dp, shards)
        grads = grads + total.move(grads, lambda d, f: (d, f ^ 1))
        a, b, c = [total.move(grads, lambda d, f, e=e: (d ^ e, f)) for e in (1, 2, 3)]
        grads = (grads + a) + (b + c)
        a, b, c = [total.move(grads, lambda d, f, k=k: (d, (f + 2 * k) % shards)) for k in (1, 2, 3)]
        dq = after(dq, grads)
        grad_in = input_grad(joint, place, shards, tok, gh, dq, dk, dv, glow, down_map, vec)
        a, b, c = after_all([a, b, c], grad_in)
        grads = (grads + b) + (a + c)
    else:
        grads = jnp.sum(lax.all_gather(grads, ("dp", "fsdp"), axis=0, tiled=False), axis=0)
        grad_in = input_grad(joint, place, shards, tok, gh, dq, dk, dv, glow, down_map, vec)
    return (
        out.reshape(tokens.shape),
        grad_in.reshape(tokens.shape),
        grads[8:12].T,
        grads[0:4],
        grads[12:16].T,
        grads[4:8],
    )


def solution(mesh):
    slots = P(None, ("dp", "fsdp"), None, None)
    return jax.shard_map(
        per_device,
        mesh=mesh,
        in_specs=(
            slots,
            P(None, ("dp", "fsdp"), None),
            P("fsdp", None),
            P("fsdp", None),
            P("fsdp", None),
            P("fsdp", None),
            P(None, "fsdp"),
            P(None, "fsdp"),
            P("fsdp"),
            P(),
            P(),
            P(),
            P(),
            slots,
        ),
        out_specs=(slots, slots, P(), P(), P(), P()),
        check_vma=False,
    )
```

```python
import functools
import math

import jax
import jax.numpy as jnp
from jax import lax
from jax.experimental import pallas as pl
from jax.experimental.pallas import tpu as pltpu
from jax.sharding import PartitionSpec as P

f32 = jnp.float32
bf16 = jnp.bfloat16
LANES = 128
PAIR = 128
BAND = 3
EPS = 1e-5
MASKED = -1e30
SCORE_SCALE = 0.125 * math.log2(math.e)
GELU_C = math.sqrt(2.0 / math.pi)
VMEM_LIMIT = 58 * 2**20
COST = 8
NT = (((1,), (1,)), ((), ()))
TN = (((0,), (0,)), ((), ()))


def dot(a, b):
    return jnp.dot(a, b, preferred_element_type=f32)


def dot_nt(a, b):
    return lax.dot_general(a, b, NT, preferred_element_type=f32)


def dot_tn(a, b):
    return lax.dot_general(a, b, TN, preferred_element_type=f32)


def params():
    return pltpu.CompilerParams(vmem_limit_bytes=VMEM_LIMIT)


def resident(array):
    zeros = (0,) * array.ndim
    return pl.BlockSpec(array.shape, lambda *_: zeros, pipeline_mode=pl.Buffered(1))


def normalise(x):
    centred = x - jnp.mean(x, axis=-1, keepdims=True)
    r = lax.rsqrt(jnp.mean(centred * centred, axis=-1, keepdims=True) + EPS)
    return centred * r, r


def norm_back(n, r, w):
    return r * (w - jnp.mean(w, axis=-1, keepdims=True) - n * jnp.mean(w * n, axis=-1, keepdims=True))


def gelu_and_slope(x):
    x2 = x * x
    t = jnp.tanh(x * (GELU_C + (GELU_C * 0.044715) * x2))
    half = 0.5 + 0.5 * t
    slope = half + (0.5 * x) * ((1.0 - t * t) * (GELU_C + (3 * GELU_C * 0.044715) * x2))
    return x * half, slope


def ring_pairs(dp, fsdp, move):
    pairs = []
    for d in range(dp):
        for f in range(fsdp):
            e, g = move(d, f)
            pairs.append((d * fsdp + f, e * fsdp + g))
    return pairs


def after(x, others):
    return lax.optimization_barrier((x, others))[0]


def after_all(xs, others):
    return lax.optimization_barrier((xs, others))[0]


class Gather:
    def __init__(self, dp, fsdp):
        self.dp, self.fsdp = dp, fsdp

    def move(self, x, where):
        return lax.ppermute(x, ("dp", "fsdp"), ring_pairs(self.dp, self.fsdp, where))

    def step_1(self, mine):
        fsdp = self.fsdp
        return [self.move(mine, lambda d, f, k=k: (d, (f + 2 * k) % fsdp)) for k in range(1, fsdp // 2)]

    def all_far(self, near):
        near = [jnp.broadcast_to(x[None], (self.dp,) + x.shape) for x in near]
        return lax.all_to_all(jnp.concatenate(near, axis=1), "dp", 0, 0, tiled=False)

    def each_far(self, near):
        near = stack(near) if len(near) > 1 else near[0]
        return [near] + [self.move(near, lambda d, f, e=e: (d ^ e, f)) for e in range(1, self.dp)]

    def swap(self, x):
        return self.move(x, lambda d, f: (d, f ^ 1))


def pieces(shard, other_shard, far, other_far, shard_column=0, far_column=0):
    made = [(shard, shard_column, 0, "shard"), (other_shard, shard_column, 1, "shard")]
    for swapped, arrays in ((0, far), (1, other_far)):
        if len(arrays) == 1:
            made.append((arrays[0], far_column, swapped, "all"))
        else:
            made += [(x, far_column, swapped, e) for e, x in enumerate(arrays)]
    return made


def copies(weight, refs, whole, sems, place, cols, base, dp, fsdp):
    made = []
    start, size = cols
    rows = whole.shape[0] // fsdp
    part = rows // dp
    index = place[1]

    def add(source, first, at, rows):
        target = whole.at[pl.ds(at, rows), pl.ds(start - base, size)]
        made.append(pltpu.make_async_copy(source.at[:, pl.ds(first + start, size)], target, sems.at[len(made)]))

    for (_, column, swapped, what), ref in zip(weight, refs):
        other = swapped * (1 - 2 * lax.rem(index, 2))
        if what == "whole":
            add(ref, column, 0, whole.shape[0])
        elif what == "shard":
            add(ref, column, pl.multiple_of((index + other) * rows, rows), rows)
        else:
            for e in range(dp) if what == "all" else [what]:
                quarter = e if what == "all" else jnp.bitwise_xor(place[0], e)
                for k in range(1, fsdp // 2):
                    owner = lax.rem(index + fsdp - 2 * k, fsdp) + other
                    at = pl.multiple_of(owner * rows + quarter * part, part)
                    here = pl.ds((k - 1) * part, part)
                    add(ref.at[e, here] if what == "all" else ref.at[here], column, at, part)
    return made


def copy_count(weight, dp, fsdp):
    count = 0
    for _, _, _, what in weight:
        count += 1 if what in ("whole", "shard") else (fsdp // 2 - 1) * (dp if what == "all" else 1)
    return count


def weight_call(kernel, name, weights, order, grid, blocked, in_specs, out_specs, out_shape, scratch, place, cost, fsdp, old=()):
    dp = lax.axis_size("dp")
    arrays = [[piece[0] for piece in w] for w, _ in weights]
    flat = [a for some in arrays for a in some]
    counts = [copy_count(weights[i][0], dp, fsdp) for i, _, _ in order]

    def body(place_ref, *refs):
        refs = list(refs)
        take = lambda n: [refs.pop(0) for _ in range(n)]
        sources = [take(len(some)) for some in arrays]
        ins, _, outs = take(len(blocked)), take(len(old)), take(len(out_shape))
        wholes, sems = take(len(weights)), take(len(order))

        first_step = pl.program_id(0) == 0
        for axis in range(1, len(grid)):
            first_step = first_step & (pl.program_id(axis) == 0)

        def group(n):
            i, start, size = order[n]
            base = start if wholes[i].shape[1] == size else 0
            return copies(weights[i][0], sources[i], wholes[i], sems[n], place_ref, (start, size), base, dp, fsdp)

        @pl.when(first_step)
        def _():
            for n in range(len(order)):
                for copy in group(n):
                    copy.start()

        def wait(n):
            @pl.when(first_step)
            def _():
                for copy in group(n):
                    copy.wait()

        kernel(wholes, wait, ins, outs, refs)

    return pl.pallas_call(
        body,
        grid_spec=pltpu.PrefetchScalarGridSpec(
            num_scalar_prefetch=1,
            grid=grid,
            in_specs=[pl.BlockSpec(memory_space=pltpu.HBM)] * len(flat)
            + in_specs
            + [pl.BlockSpec(memory_space=pl.ANY)] * len(old),
            out_specs=out_specs,
            scratch_shapes=[pltpu.VMEM(shape, bf16) for _, shape in weights]
            + [pltpu.SemaphoreType.DMA((n,)) for n in counts]
            + scratch,
        ),
        out_shape=out_shape,
        compiler_params=params(),
        cost_estimate=pl.CostEstimate(flops=cost // COST, bytes_accessed=2**20, transcendentals=0),
        input_output_aliases={1 + len(flat) + len(blocked) + i: i for i in range(len(old))},
        name=name,
    )(place, *flat, *blocked, *old)


def own_quarter(rows):
    return pl.ds(pl.multiple_of(lax.axis_index("dp") * rows, rows), rows)


def stack_rows(arrays, rows):
    arrays = [a.astype(f32) for a in arrays]
    used = sum(a.shape[0] for a in arrays)
    return jnp.concatenate(arrays + [jnp.zeros((rows - used, arrays[0].shape[1]), f32)], axis=0).astype(bf16)


def stack_kernel(*refs):
    rows = refs[0].shape[0]
    for i, ref in enumerate(refs[:-1]):
        refs[-1][i * rows : (i + 1) * rows, :] = ref[...]


def stack(arrays):
    rows, columns = arrays[0].shape
    return local_call(stack_kernel, "stack", [(rows * len(arrays), columns)], arrays)[0]


def cut_kernel(joint, biases, gains, hidden, first, part):
    half = joint.shape[1] // 6
    for i in range(3):
        first[:, i * half : (i + 1) * half] = joint[:, 2 * i * half : (2 * i + 1) * half]
    small = [biases[...], gains[...], hidden[...].astype(f32).reshape(-1, LANES)]
    first[:, 3 * half :] = stack_rows(small, first.shape[0])
    part[...] = first[own_quarter(part.shape[0]), :]


def local_call(kernel, name, shapes, arrays):
    return pl.pallas_call(
        kernel,
        out_shape=[jax.ShapeDtypeStruct(s, bf16) for s in shapes],
        compiler_params=params(),
        name=name,
    )(*arrays)


def cut(joint, biases, gains, hidden, dp):
    rows, width = joint.shape
    columns = width // 2 + LANES
    return local_call(cut_kernel, "cut", [(rows, columns), (rows // dp, columns)], [joint, biases, gains, hidden])


def pack_kernel(chunks, shards, joint, up, down, wo, q_down, q_up, v_down, v_up, *refs):
    outs, parts = refs[:2], refs[2:4]
    down_map, up_map = refs[4:]
    hidden, width = down.shape
    part = hidden // chunks
    half = joint.shape[1] // 6
    for i in range(3):
        outs[0][:, i * half : (i + 1) * half] = joint[:, (2 * i + 1) * half : (2 * i + 2) * half]
    for j in range(chunks):
        out, at = (outs[1], (j - 1) * 2 * width) if j else (outs[0], 3 * half)
        for s in range(shards):
            start = s * hidden + j * part
            out[:, at + s * part : at + (s + 1) * part] = up[:, start : start + part]
        out[:, at + width : at + 2 * width] = down[j * part : (j + 1) * part, :]
    outs[0][:, 3 * half + 2 * width :] = wo[...]
    for out, part_ref in zip(outs, parts):
        part_ref[...] = out[own_quarter(part_ref.shape[0]), :]
    rank = q_up.shape[0]
    down_map[...] = jnp.zeros_like(down_map)
    down_map[:, :rank] = q_down[...]
    down_map[:, rank : 2 * rank] = v_down[...]
    zero = jnp.zeros(q_up.shape, f32)
    rows = [jnp.concatenate([q_up[...].astype(f32) * 8.0, zero], axis=1)]
    rows += [jnp.concatenate([zero, v_up[...].astype(f32) * 8.0], axis=1)]
    up_map[...] = stack_rows(rows, up_map.shape[0])


def pack(joint, up, down, wo, adapters, chunks, shards, dp):
    rows, width = up.shape[0], down.shape[1]
    shapes = [(rows, joint.shape[1] // 2 + 3 * width), (rows, 2 * (chunks - 1) * width)]
    shapes += [(r // dp, c) for r, c in shapes]
    shapes += [(width, LANES), (LANES, 2 * width)]
    return local_call(functools.partial(pack_kernel, chunks, shards), "pack", shapes, [joint, up, down, wo, *adapters])


def project_slot(first, carried, shards, w, wait, ins, outs):
    rows_in, down, up = ins[:3]
    q_ref, k_ref, v_ref = outs[:3]
    half = q_ref.shape[1]
    width = 2 * half
    cols = slice(0, half) if first else slice(half, width)
    wait(0)
    if first:
        low_ref, normed_ref, vec = outs[3:6]

        @pl.when(pl.program_id(0) == 0)
        def _():
            if carried:
                rows = w.shape[0] // shards
                parts = [w[s * rows : s * rows + vec.shape[0], 3 * half :] for s in range(shards)]
                vec[...] = jnp.concatenate(parts, axis=1).astype(f32)
            else:
                vec[...] = ins[3][...]
    else:
        low_in, vec = ins[3:]
    sub = 256
    state = {}

    def norm(r):
        rr = slice(r, r + sub)
        if first:
            n, _ = normalise(rows_in[rr, :].astype(f32))
            normed = (n * vec[6:7, :] + vec[0:1, :]).astype(bf16)
            normed_ref[rr, :] = normed
        else:
            normed = rows_in[rr, :]
        state[r] = normed

    def mix(r):
        rr = slice(r, r + sub)
        normed = state.pop(r)
        k_ref[rr, :] = dot(normed, w[:, half : 2 * half]).astype(bf16)
        if first:
            low = dot(normed, down[...]).astype(bf16)
            low_ref[rr, :] = low
        else:
            low = low_in[rr, :]
        q = dot(normed, w[:, :half]) + dot(low, up[:, cols]) + vec[2:3, cols]
        q_ref[rr, :] = (q * SCORE_SCALE).astype(bf16)
        v = dot(normed, w[:, 2 * half : 3 * half]) + dot(low, up[:, width:][:, cols]) + vec[3:4, cols]
        v_ref[rr, :] = v.astype(bf16)

    pipelined(list(range(0, rows_in.shape[0], sub)), (norm, mix), (0, 1))


def heads_kernel(first, carried, shards, pairs, wholes, wait, ins, outs, scratch):
    lengths, ins = ins[0], ins[1:]
    q_ref, k_ref, v_ref = outs[:3]
    o_ref, p_ref, linv_ref = outs[-3:]
    (mask,) = scratch
    blocks = q_ref.shape[0] // LANES

    @pl.when(pl.program_id(1) == 0)
    def _():
        project_slot(first, carried, shards, wholes[0], wait, ins, outs)
        fill_masks(lengths, pl.program_id(0), mask, blocks)

    @pl.when(pl.program_id(1) != 0)
    def _():
        at = pl.multiple_of((pl.program_id(1) - 1) * pairs * PAIR, pairs * PAIR)
        attend_pairs(pairs, blocks, at, q_ref, k_ref, v_ref, o_ref, p_ref, linv_ref, mask)


def heads(weight, place, fsdp, lengths, x, down, up, vec=None, low=None, old=()):
    tokens, width = x.shape
    slots = lengths.shape[0]
    seq = tokens // slots
    blocks, heads2, pairs = seq // LANES, width // PAIR, 2
    steps = heads2 // pairs // 2
    first = low is None
    here = 0 if first else 1
    row = pl.BlockSpec((seq, width), lambda s, j, _: (s, 0))
    thin = pl.BlockSpec((seq, LANES), lambda s, j, _: (s, 0))
    half = pl.BlockSpec((seq, width // 2), lambda s, j, _: (s, here))
    group = lambda j: here * steps + jnp.maximum(j - 1, 0)
    tile = pl.BlockSpec((seq, pairs * PAIR), lambda s, j, _: (s, group(j)))
    probs = (pairs, blocks, BAND * LANES, 2 * LANES)
    sums = (pairs, blocks, 2 * LANES)
    ins = [lengths, x, down, up]
    in_specs = [pl.BlockSpec(memory_space=pltpu.SMEM), row, resident(down), resident(up)]
    outs, out_specs = [jax.ShapeDtypeStruct((tokens, width), bf16)] * 3, [half] * 3
    if first:
        outs = outs + [jax.ShapeDtypeStruct((tokens, n), bf16) for n in (LANES, width)]
        outs = outs + [jax.ShapeDtypeStruct((16, width), f32)]
        out_specs = out_specs + [thin, row, pl.BlockSpec((16, width), lambda s, j, _: (0, 0))]
    else:
        ins, in_specs = ins + [low], in_specs + [thin]
    if vec is not None:
        ins, in_specs = ins + [vec], in_specs + [resident(vec)]
    outs = outs + [
        jax.ShapeDtypeStruct((tokens, width), bf16),
        jax.ShapeDtypeStruct((slots, heads2) + probs[1:], bf16),
        jax.ShapeDtypeStruct((slots, heads2) + sums[1:], f32),
    ]
    out_specs = out_specs + [
        tile,
        pl.BlockSpec((1,) + probs, lambda s, j, _: (s, group(j), 0, 0, 0)),
        pl.BlockSpec((1,) + sums, lambda s, j, _: (s, group(j), 0, 0)),
    ]
    carried = first and vec is None
    columns = 3 * width // 2 + (LANES if carried else 0)
    return weight_call(
        functools.partial(heads_kernel, first, carried, fsdp, pairs),
        "heads",
        [(weight, (width, columns))],
        [(0, 0, columns)],
        (slots, 1 + steps),
        ins,
        in_specs,
        out_specs,
        outs,
        [pltpu.VMEM((blocks, BAND * LANES, LANES), f32)],
        place,
        9 * tokens * width * width,
        fsdp,
        old,
    )


def fill_masks(lengths, slot, mask, blocks):
    starts = []
    total = jnp.int32(0)
    for d in range(lengths.shape[1]):
        starts.append(total)
        total = total + lengths[slot, d]
    for qb in range(blocks):
        first = max(0, qb - BAND + 1)
        rows = (qb - first + 1) * LANES
        query = qb * LANES + lax.broadcasted_iota(jnp.int32, (8, LANES), 1)
        begin = jnp.zeros((8, LANES), jnp.int32)
        for start in starts:
            begin = jnp.where(query >= start, start, begin)
        key = first * LANES + lax.broadcasted_iota(jnp.int32, (rows, LANES), 0)
        ok = (key >= begin[0:1]) & (key <= query[0:1])
        mask[qb, :rows, :] = jnp.where(ok, 0.0, MASKED)


def half_lanes():
    return lax.broadcasted_iota(jnp.int32, (LANES, LANES), 1) < 64


def half_rows():
    return lax.broadcasted_iota(jnp.int32, (LANES, LANES), 0) < 64


def split_heads(x, left):
    zero = jnp.zeros_like(x)
    return jnp.concatenate([jnp.where(left, x, zero), jnp.where(left, zero, x)], axis=0)


def pipelined(units, stages, lags):
    for t in range(len(units) + lags[-1]):
        for stage, lag in zip(stages, lags):
            if 0 <= t - lag < len(units):
                stage(units[t - lag])


def geometry(qb):
    first = max(0, qb - BAND + 1)
    return first * LANES, (qb - first + 1) * LANES


def attend_pairs(pairs, blocks, at, q_ref, k_ref, v_ref, o_ref, p_ref, linv_ref, mask):
    left, top = half_lanes(), half_rows()
    scores, probs = {}, {}

    def score(unit):
        pair, qb = unit
        cols = pl.ds(at + pair * PAIR, PAIR)
        key0, rows = geometry(qb)
        q = split_heads(q_ref[qb * LANES : (qb + 1) * LANES, cols], left)
        scores[unit] = dot_nt(k_ref[key0 : key0 + rows, cols], q)

    def soften(unit):
        pair, qb = unit
        key0, rows = geometry(qb)
        bias = mask[qb, :rows, :]
        s = scores.pop(unit) + jnp.concatenate([bias, bias], axis=1)
        p = jnp.exp2(s - jnp.max(s, axis=0, keepdims=True))
        linv = 1.0 / jnp.sum(p, axis=0, keepdims=True)
        linv_ref[0, pair, qb : qb + 1, :] = linv
        low = p.astype(bf16)
        p_ref[0, pair, qb, :rows, :] = low
        probs[unit] = (low, linv)

    def mix(unit):
        pair, qb = unit
        key0, rows = geometry(qb)
        low, linv = probs.pop(unit)
        o = dot_tn(v_ref[key0 : key0 + rows, pl.ds(at + pair * PAIR, PAIR)], low)
        o = jnp.where(top, o[:, :LANES] * linv[:, :LANES], o[:, LANES:] * linv[:, LANES:])
        o_ref[qb * LANES : (qb + 1) * LANES, pair * PAIR : (pair + 1) * PAIR] = o.T.astype(bf16)

    units = [(pair, qb) for qb in range(blocks) for pair in range(pairs)]
    pipelined(units, (score, soften, mix), (0, 2, 5))


def attend_back_kernel(
    pairs, blocks, q_ref, k_ref, v_ref, g_ref, o_ref, p_ref, linv_ref, low, normed, up, *refs
):
    dq_ref, dk_ref, dv_ref, glow_ref, grads, dk_sum, dv_sum, glow_sum = refs
    left, top = half_lanes(), half_rows()
    ones = jnp.ones((BAND * LANES, LANES), bf16)
    dk_sum[...] = jnp.zeros_like(dk_sum)
    dv_sum[...] = jnp.zeros_like(dv_sum)
    first, second = {}, {}

    def grad_probs(unit):
        pair, qb = unit
        cols = slice(pair * PAIR, (pair + 1) * PAIR)
        key0, rows = geometry(qb)
        here = slice(qb * LANES, (qb + 1) * LANES)
        linv = linv_ref[0, pair, qb : qb + 1, :]
        linv = jnp.where(top, linv[:, :LANES], linv[:, LANES:]).T
        g = g_ref[here, cols].astype(f32) * linv
        delta = split_heads(-(g * o_ref[here, cols].astype(f32)).astype(bf16), left)
        g = split_heads(g.astype(bf16), left)
        values = jnp.concatenate([v_ref[key0 : key0 + rows, cols], ones[:rows]], axis=1)
        first[unit] = (dot_nt(values, jnp.concatenate([g, delta], axis=1)), g)

    def grad_values(unit):
        pair, qb = unit
        cols = slice(pair * PAIR, (pair + 1) * PAIR)
        key0, rows = geometry(qb)
        dp, g = first.pop(unit)
        low = p_ref[0, pair, qb, :rows, :]
        second[unit] = low * dp.astype(bf16)
        dv_sum[key0 : key0 + rows, cols] += dot(low, g)

    def grad_queries_keys(unit):
        pair, qb = unit
        cols = slice(pair * PAIR, (pair + 1) * PAIR)
        key0, rows = geometry(qb)
        here = slice(qb * LANES, (qb + 1) * LANES)
        ds = second.pop(unit)
        dk_sum[key0 : key0 + rows, cols] += dot(ds, split_heads(q_ref[here, cols], left))
        dq = dot_tn(k_ref[key0 : key0 + rows, cols], ds)
        dq = jnp.where(top, dq[:, :LANES], dq[:, LANES:]) * 0.125
        dq_ref[here, cols] = dq.T.astype(bf16)

    units = [(pair, qb) for qb in range(blocks) for pair in range(pairs)]
    pipelined(units, (grad_probs, grad_values, grad_queries_keys), (0, 2, 4))
    dk_ref[...] = (dk_sum[...] * (0.125 / SCORE_SCALE)).astype(bf16)
    dv_ref[...] = dv_sum[...].astype(bf16)

    slot, step, last = pl.program_id(0), pl.program_id(1), pl.num_programs(1) - 1
    width = normed.shape[1]
    at = pl.multiple_of(step * pairs * PAIR, pairs * PAIR)
    here = pl.ds(at, pairs * PAIR)
    part = [dot_tn(low[...], dq_ref[...])[0:4], dot_tn(low[...], dv_ref[...])[4:8]]
    part = jnp.concatenate(part, axis=0) * 8.0
    grads[0:8, here] = jnp.where(slot == 0, part, grads[0:8, here] + part)
    glow = dot_nt(dq_ref[...], up[:, here]) + dot_nt(dv_ref[...], up[:, pl.ds(width + at, pairs * PAIR)])
    glow_sum[...] = jnp.where(step == 0, glow, glow_sum[...] + glow)

    @pl.when(step == last)
    def _():
        glow = glow_sum[...].astype(bf16)
        glow_ref[...] = glow
        part = dot_tn(glow, normed[...])[0:8]
        grads[8:16, :] = jnp.where(slot == 0, part, grads[8:16, :] + part)


def attend_back(slots, q, k, v, g, o, p, linv, low, normed, up):
    tokens, width = q.shape
    seq = tokens // slots
    blocks, heads2, pairs = seq // LANES, width // PAIR, 2
    rows = BAND * LANES
    tile = pl.BlockSpec((seq, pairs * PAIR), lambda s, h: (s, h))
    thin = pl.BlockSpec((seq, LANES), lambda s, h: (s, 0))
    return pl.pallas_call(
        functools.partial(attend_back_kernel, pairs, blocks),
        grid=(slots, heads2 // pairs),
        in_specs=[tile] * 5
        + [
            pl.BlockSpec((1, pairs, blocks, rows, 2 * LANES), lambda s, h: (s, h, 0, 0, 0)),
            pl.BlockSpec((1, pairs, blocks, 2 * LANES), lambda s, h: (s, h, 0, 0)),
            thin,
            pl.BlockSpec((seq, width), lambda s, h: (s, 0)),
            resident(up),
        ],
        out_specs=[tile] * 3 + [thin, pl.BlockSpec((16, width), lambda s, h: (0, 0))],
        scratch_shapes=[pltpu.VMEM((seq, pairs * PAIR), f32)] * 2 + [pltpu.VMEM((seq, LANES), f32)],
        out_shape=[jax.ShapeDtypeStruct(q.shape, bf16)] * 3
        + [jax.ShapeDtypeStruct((tokens, LANES), bf16), jax.ShapeDtypeStruct((16, width), f32)],
        compiler_params=params(),
        cost_estimate=pl.CostEstimate(flops=14 * tokens * width * width // COST, bytes_accessed=2**20, transcendentals=0),
        name="attend_back",
    )(q, k, v, g, o, p, linv, low, normed, up)


def feed_chunk(wait, first, normed, cot, w, at, bias):
    width = cot.shape[1]
    wait(first)
    wait(first + 1)
    size = width // 4
    up, down = slice(at, at + width), slice(at + width, at + 2 * width)
    acts, grads = [], []
    for i in range(0, width, size):
        grad = dot_nt(cot, w[i : i + size, down])
        act, slope = gelu_and_slope(dot(normed, w[:, at + i : at + i + size]) + bias[:, i : i + size])
        acts.append(act.astype(bf16))
        grads.append((slope * grad).astype(bf16))
    return dot(jnp.concatenate(acts, axis=1), w[:, down]), dot_nt(jnp.concatenate(grads, axis=1), w[:, up])


def feed_first_kernel(wholes, wait, ins, outs, _):
    tok, att, cot, vec = ins
    h1_ref, normed_ref, o_ref, g_ref = outs
    width = tok.shape[1]
    wait(0)
    h1 = tok[...].astype(f32) + dot(att[...], wholes[0][:, 2 * width :]) + vec[4:5, :]
    h1_ref[...] = h1
    n, _ = normalise(h1)
    normed = (n * vec[7:8, :] + vec[1:2, :]).astype(bf16)
    normed_ref[...] = normed
    o_ref[...], g_ref[...] = feed_chunk(wait, 1, normed, cot[...], wholes[0], 0, vec[8:9, :])


def feed_last_kernel(wholes, wait, ins, outs, scratch):
    h1, normed, old_o, old_g, cot, vec = ins
    out_ref, gh_ref, ga_ref = outs
    o_sum, g_sum = scratch
    width = cot.shape[1]
    o_sum[...] = old_o[...]
    g_sum[...] = old_g[...]
    chunks = wholes[0].shape[1] // (2 * width)
    for j in range(chunks):
        bias = vec[9 + j : 10 + j, :]
        o, g = feed_chunk(wait, 2 * j, normed[...], cot[...], wholes[0], 2 * j * width, bias)
        if j < chunks - 1:
            o_sum[...] += o
            g_sum[...] += g
    x = h1[...]
    out_ref[...] = (x + (o_sum[...] + o) + vec[5:6, :]).astype(bf16)
    n, r = normalise(x)
    grad = cot[...].astype(f32) + norm_back(n, r, (g_sum[...] + g) * vec[7:8, :])
    low = grad.astype(bf16)
    gh_ref[...] = low
    wait(2 * chunks)
    ga_ref[...] = dot_nt(low, wholes[1][...]).astype(bf16)


def feed_call(kernel, name, weights, order, place, fsdp, rowwise, vec, out_types, sums):
    tokens, width = rowwise[0].shape
    rows = 512
    row = pl.BlockSpec((rows, width), lambda i, _: (i, 0))
    return weight_call(
        kernel,
        name,
        weights,
        order,
        (tokens // rows,),
        rowwise + [vec],
        [row] * len(rowwise) + [resident(vec)],
        [row] * len(out_types),
        [jax.ShapeDtypeStruct((tokens, width), t) for t in out_types],
        [pltpu.VMEM((rows, width), f32)] * sums,
        place,
        18 * tokens * width * width,
        fsdp,
    )


def feed_order(width, chunks):
    return [(0, (2 * j + 1 - i) * width, width) for j in range(chunks) for i in (0, 1)]


def feed_first(feeds, place, fsdp, tok, att, cot, vec):
    width = tok.shape[1]
    weights = [(feeds[0], (width, 3 * width))]
    order = [(0, 2 * width, width)] + feed_order(width, 1)
    types = [f32, bf16, f32, f32]
    return feed_call(feed_first_kernel, "feed_first", weights, order, place, fsdp, [tok, att, cot], vec, types, 0)


def feed_last(feeds, place, fsdp, h1, normed, o, g, cot, vec):
    width = cot.shape[1]
    weights = [(feeds[1], (width, 6 * width)), (feeds[0], (width, width))]
    order = feed_order(width, 3) + [(1, 2 * width, width)]
    rowwise = [h1, normed, o, g, cot]
    return feed_call(feed_last_kernel, "feed_last", weights, order, place, fsdp, rowwise, vec, [bf16] * 3, 2)


def input_kernel(wholes, wait, ins, outs, _):
    tok, gh, dq, dk, dv, glow, down, vec = ins
    (out_ref,) = outs
    half = tok.shape[1] // 2
    g = dot_nt(glow[...], down[...])
    for i, w in enumerate(wholes):
        wait(i)
        cols = slice(i * half, (i + 1) * half)
        g = g + dot_nt(dq[:, cols], w[:, :half])
        g = g + dot_nt(dk[:, cols], w[:, half : 2 * half])
        g = g + dot_nt(dv[:, cols], w[:, 2 * half : 3 * half])
    n, r = normalise(tok[...].astype(f32))
    out_ref[...] = (gh[...].astype(f32) + norm_back(n, r, g * vec[6:7, :])).astype(bf16)


def input_grad(joint, place, fsdp, tok, gh, dq, dk, dv, glow, down, vec):
    tokens, width = tok.shape
    rows = 512
    row = pl.BlockSpec((rows, width), lambda i, _: (i, 0))
    thin = pl.BlockSpec((rows, LANES), lambda i, _: (i, 0))
    return weight_call(
        input_kernel,
        "input_grad",
        [(w, (width, 3 * width // 2)) for w in joint],
        [(0, 0, 3 * width // 2), (1, 0, 3 * width // 2)],
        (tokens // rows,),
        [tok, gh, dq, dk, dv, glow, down, vec],
        [row] * 5 + [thin, resident(down), resident(vec)],
        [row],
        [jax.ShapeDtypeStruct((tokens, width), bf16)],
        [],
        place,
        6 * tokens * width * width,
        fsdp,
    )[0]


def per_device(
    tokens,
    document_length_list,
    joint_projection_weight,
    attention_out_weight,
    feed_up_weight,
    feed_down_weight,
    frozen_norm_gains,
    biases,
    hidden_up_bias,
    query_down_adapter,
    query_up_adapter,
    value_down_adapter,
    value_up_adapter,
    cotangent,
):
    micro, local, seq, width = tokens.shape
    slots = micro * local
    shards = width // joint_projection_weight.shape[0]
    hidden = feed_down_weight.shape[0]
    tok = tokens.reshape(slots * seq, width)
    cot = cotangent.reshape(slots * seq, width)
    lengths = document_length_list.reshape(slots, -1)

    dp = lax.axis_size("dp")
    place = jnp.stack([lax.axis_index("dp"), lax.axis_index("fsdp")]).astype(jnp.int32)
    chunks = 4
    part = hidden // chunks
    stepped = dp == 4 and shards == 8 and part == LANES and width == shards * LANES

    def gather(x):
        return lax.all_gather(x, "fsdp", axis=0, tiled=True)

    adapters = [query_down_adapter, query_up_adapter, value_down_adapter, value_up_adapter]
    if stepped:
        a, part_a = cut(joint_projection_weight, biases, frozen_norm_gains, hidden_up_bias, dp)
        link = Gather(dp, shards)
        near = link.step_1(part_a)
        shards_here = [joint_projection_weight, feed_up_weight, feed_down_weight, attention_out_weight]
        *shards_here, part_a = after_all(shards_here + [part_a], a)
        b, c, part_b, part_c, down_map, up_map = pack(*shards_here, adapters, chunks, shards, dp)
        *near, part_b = after_all(near + [part_b], part_c)
        a_far = link.all_far(near)
        b_near = link.step_1(part_b)
        b_far = link.all_far(b_near)
        c_near = link.step_1(after(part_c, b_near))
        joint = [pieces(a, link.swap(a), [a_far], [link.swap(a_far)])]
        vec = None
    else:
        small = jnp.concatenate([biases, frozen_norm_gains], axis=0)
        small = lax.all_gather(small, "fsdp", axis=1, tiled=True)
        hidden_bias = lax.all_gather(hidden_up_bias, "fsdp", axis=0, tiled=False)
        hidden_bias = [hidden_bias[:, j * part : (j + 1) * part].reshape(1, -1) for j in range(chunks)]
        vec = jnp.concatenate([small] + hidden_bias, axis=0)
        vec = jnp.pad(vec, ((0, 16 - 8 - chunks), (0, 0))).astype(f32)
        third = [width * i // 2 for i in range(6)]
        joint = []
        for i in (0, 1):
            cols = [lax.slice_in_dim(joint_projection_weight, t, t + width // 2, axis=1) for t in third[i::2]]
            joint.append([(gather(jnp.concatenate(cols, axis=1)), 0, 0, "whole")])
        up_parts = feed_up_weight.reshape(-1, shards, chunks, part)
        feeds = []
        for group in ((0,), tuple(range(1, chunks))):
            cols = []
            for j in group:
                cols.append(up_parts[:, :, j, :].reshape(-1, shards * part))
                cols.append(feed_down_weight[j * part : (j + 1) * part])
            if group[0] == 0:
                cols.append(attention_out_weight)
            feeds.append([(gather(jnp.concatenate(cols, axis=1)), 0, 0, "whole")])
        rank = query_down_adapter.shape[1]
        down_map = jnp.concatenate([query_down_adapter, value_down_adapter], axis=1)
        down_map = jnp.pad(down_map, ((0, 0), (0, LANES - 2 * rank)))
        zero = jnp.zeros_like(query_up_adapter)
        up_map = jnp.concatenate(
            [
                jnp.concatenate([query_up_adapter, zero], axis=1),
                jnp.concatenate([zero, value_up_adapter], axis=1),
            ],
            axis=0,
        )
        up_map = jnp.pad(up_map * 8, ((0, LANES - 2 * rank), (0, 0))).astype(bf16)

    q, k, v, low, normed, vec, *kept = heads(joint[0], place, shards, lengths, tok, down_map, up_map, vec)
    if stepped:
        b_far, *c_near, q = after_all([b_far] + c_near + [q], low)
        b_rest = [link.swap(b), [b_far], [link.swap(b_far)]]
        c_far = link.each_far(c_near)
        joint.append(pieces(b, *b_rest))
    old = [q, k, v] + kept
    q, k, v, att, probs, linv = heads(joint[1], place, shards, lengths, normed, down_map, up_map, vec, low, old)
    if stepped:
        feeds = [pieces(b, *b_rest, joint_projection_weight.shape[1] // 2, joint_projection_weight.shape[1] // 2)]
        c_other = [link.swap(c_far[0])]
        *c_other, att = after_all(c_other + [att], vec)
    h1, normed_2, o, g = feed_first(feeds, place, shards, tok, att, cot, vec)
    if stepped:
        *far, o = after_all(c_far[1:] + [o], h1)
        c_other += [link.swap(x) for x in far]
        feeds.append(pieces(c, link.swap(after(c, vec)), c_far[:1] + far, c_other))
    out, gh, ga = feed_last(feeds, place, shards, h1, normed_2, o, g, cot, vec)

    dq, dk, dv, glow, grads = attend_back(slots, q, k, v, ga, att, probs, linv, low, normed, up_map)
    if stepped:
        total = Gather(dp, shards)
        grads = grads + total.move(grads, lambda d, f: (d, f ^ 1))
        _, a, b, c = total.each_far([grads])
        grads = (grads + a) + (b + c)
        a, b, c = [total.move(grads, lambda d, f, k=k: (d, (f + 2 * k) % shards)) for k in (1, 2, 3)]
        dq = after(dq, grads)
        grad_in = input_grad(joint, place, shards, tok, gh, dq, dk, dv, glow, down_map, vec)
        a, b, c = after_all([a, b, c], grad_in)
        grads = (grads + b) + (a + c)
    else:
        grads = jnp.sum(lax.all_gather(grads, ("dp", "fsdp"), axis=0, tiled=False), axis=0)
        grad_in = input_grad(joint, place, shards, tok, gh, dq, dk, dv, glow, down_map, vec)
    return (
        out.reshape(tokens.shape),
        grad_in.reshape(tokens.shape),
        grads[8:12].T,
        grads[0:4],
        grads[12:16].T,
        grads[4:8],
    )


def solution(mesh):
    slots = P(None, ("dp", "fsdp"), None, None)
    return jax.shard_map(
        per_device,
        mesh=mesh,
        in_specs=(
            slots,
            P(None, ("dp", "fsdp"), None),
            P("fsdp", None),
            P("fsdp", None),
            P("fsdp", None),
            P("fsdp", None),
            P(None, "fsdp"),
            P(None, "fsdp"),
            P("fsdp"),
            P(),
            P(),
            P(),
            P(),
            slots,
        ),
        out_specs=(slots, slots, P(), P(), P(), P()),
        check_vma=False,
    )
```

```python
import functools
import math

import jax
import jax.numpy as jnp
from jax import lax
from jax.experimental import pallas as pl
from jax.experimental.pallas import tpu as pltpu
from jax.sharding import PartitionSpec as P

f32 = jnp.float32
bf16 = jnp.bfloat16
LANES = 128
PAIR = 128
BAND = 3
EPS = 1e-5
MASKED = -1e30
SCORE_SCALE = 0.125 * math.log2(math.e)
GELU_C = math.sqrt(2.0 / math.pi)
VMEM_LIMIT = 58 * 2**20
COST = 8
NT = (((1,), (1,)), ((), ()))
TN = (((0,), (0,)), ((), ()))


def dot(a, b):
    return jnp.dot(a, b, preferred_element_type=f32)


def dot_nt(a, b):
    return lax.dot_general(a, b, NT, preferred_element_type=f32)


def dot_tn(a, b):
    return lax.dot_general(a, b, TN, preferred_element_type=f32)


def params():
    return pltpu.CompilerParams(vmem_limit_bytes=VMEM_LIMIT)


def resident(array):
    zeros = (0,) * array.ndim
    return pl.BlockSpec(array.shape, lambda *_: zeros, pipeline_mode=pl.Buffered(1))


def normalise(x):
    centred = x - jnp.mean(x, axis=-1, keepdims=True)
    r = lax.rsqrt(jnp.mean(centred * centred, axis=-1, keepdims=True) + EPS)
    return centred * r, r


def norm_back(n, r, w):
    return r * (w - jnp.mean(w, axis=-1, keepdims=True) - n * jnp.mean(w * n, axis=-1, keepdims=True))


def gelu_and_slope(x):
    x2 = x * x
    t = jnp.tanh(x * (GELU_C + (GELU_C * 0.044715) * x2))
    half = 0.5 + 0.5 * t
    slope = half + (0.5 * x) * ((1.0 - t * t) * (GELU_C + (3 * GELU_C * 0.044715) * x2))
    return x * half, slope


def ring_pairs(dp, fsdp, move):
    pairs = []
    for d in range(dp):
        for f in range(fsdp):
            e, g = move(d, f)
            pairs.append((d * fsdp + f, e * fsdp + g))
    return pairs


def after(x, others):
    return lax.optimization_barrier((x, others))[0]


def after_all(xs, others):
    return lax.optimization_barrier((xs, others))[0]


class Gather:
    def __init__(self, dp, fsdp):
        self.dp, self.fsdp = dp, fsdp

    def move(self, x, where):
        return lax.ppermute(x, ("dp", "fsdp"), ring_pairs(self.dp, self.fsdp, where))

    def step_1(self, mine):
        fsdp = self.fsdp
        return [self.move(mine, lambda d, f, k=k: (d, (f + 2 * k) % fsdp)) for k in range(1, fsdp // 2)]

    def all_far(self, near):
        near = [jnp.broadcast_to(x[None], (self.dp,) + x.shape) for x in near]
        return lax.all_to_all(jnp.concatenate(near, axis=1), "dp", 0, 0, tiled=False)

    def each_far(self, near):
        near = stack(near) if len(near) > 1 else near[0]
        return [near] + [self.move(near, lambda d, f, e=e: (d ^ e, f)) for e in range(1, self.dp)]

    def swap(self, x):
        return self.move(x, lambda d, f: (d, f ^ 1))


def pieces(shard, other_shard, far, other_far, shard_column=0, far_column=0):
    made = [(shard, shard_column, 0, "shard"), (other_shard, shard_column, 1, "shard")]
    for swapped, arrays in ((0, far), (1, other_far)):
        if len(arrays) == 1:
            made.append((arrays[0], far_column, swapped, "all"))
        else:
            made += [(x, far_column, swapped, e) for e, x in enumerate(arrays)]
    return made


def copies(weight, refs, whole, sems, place, cols, base, dp, fsdp):
    made = []
    start, size = cols
    rows = whole.shape[0] // fsdp
    part = rows // dp
    index = place[1]

    def add(source, first, at, rows):
        target = whole.at[pl.ds(at, rows), pl.ds(start - base, size)]
        made.append(pltpu.make_async_copy(source.at[:, pl.ds(first + start, size)], target, sems.at[len(made)]))

    for (_, column, swapped, what), ref in zip(weight, refs):
        other = swapped * (1 - 2 * lax.rem(index, 2))
        if what == "whole":
            add(ref, column, 0, whole.shape[0])
        elif what == "shard":
            add(ref, column, pl.multiple_of((index + other) * rows, rows), rows)
        else:
            for e in range(dp) if what == "all" else [what]:
                quarter = e if what == "all" else jnp.bitwise_xor(place[0], e)
                for k in range(1, fsdp // 2):
                    owner = lax.rem(index + fsdp - 2 * k, fsdp) + other
                    at = pl.multiple_of(owner * rows + quarter * part, part)
                    here = pl.ds((k - 1) * part, part)
                    add(ref.at[e, here] if what == "all" else ref.at[here], column, at, part)
    return made


def copy_count(weight, dp, fsdp):
    count = 0
    for _, _, _, what in weight:
        count += 1 if what in ("whole", "shard") else (fsdp // 2 - 1) * (dp if what == "all" else 1)
    return count


def weight_call(kernel, name, weights, order, grid, blocked, in_specs, out_specs, out_shape, scratch, cost, fsdp, old=()):
    dp = lax.axis_size("dp")
    arrays = [[piece[0] for piece in w] for w, _ in weights]
    flat = [a for some in arrays for a in some]
    counts = [copy_count(weights[i][0], dp, fsdp) for i, _, _ in order]

    def body(*refs):
        refs = list(refs)
        place = [lax.axis_index("dp"), lax.axis_index("fsdp")]
        take = lambda n: [refs.pop(0) for _ in range(n)]
        sources = [take(len(some)) for some in arrays]
        ins, _, outs = take(len(blocked)), take(len(old)), take(len(out_shape))
        wholes, sems = take(len(weights)), take(len(order))

        first_step = pl.program_id(0) == 0
        for axis in range(1, len(grid)):
            first_step = first_step & (pl.program_id(axis) == 0)

        def group(n):
            i, start, size = order[n]
            base = start if wholes[i].shape[1] == size else 0
            return copies(weights[i][0], sources[i], wholes[i], sems[n], place, (start, size), base, dp, fsdp)

        @pl.when(first_step)
        def _():
            for n in range(len(order)):
                for copy in group(n):
                    copy.start()

        def wait(n):
            @pl.when(first_step)
            def _():
                for copy in group(n):
                    copy.wait()

        kernel(wholes, wait, ins, outs, refs)

    return pl.pallas_call(
        body,
        grid=grid,
        in_specs=[pl.BlockSpec(memory_space=pltpu.HBM)] * len(flat)
        + in_specs
        + [pl.BlockSpec(memory_space=pl.ANY)] * len(old),
        out_specs=out_specs,
        scratch_shapes=[pltpu.VMEM(shape, bf16) for _, shape in weights]
        + [pltpu.SemaphoreType.DMA((n,)) for n in counts]
        + scratch,
        out_shape=out_shape,
        compiler_params=params(),
        cost_estimate=pl.CostEstimate(flops=cost // COST, bytes_accessed=2**20, transcendentals=0),
        input_output_aliases={len(flat) + len(blocked) + i: i for i in range(len(old))},
        name=name,
    )(*flat, *blocked, *old)


def own_quarter(rows):
    return pl.ds(pl.multiple_of(lax.axis_index("dp") * rows, rows), rows)


def stack_rows(arrays, rows):
    arrays = [a.astype(f32) for a in arrays]
    used = sum(a.shape[0] for a in arrays)
    return jnp.concatenate(arrays + [jnp.zeros((rows - used, arrays[0].shape[1]), f32)], axis=0).astype(bf16)


def stack_kernel(*refs):
    rows = refs[0].shape[0]
    for i, ref in enumerate(refs[:-1]):
        refs[-1][i * rows : (i + 1) * rows, :] = ref[...]


def stack(arrays):
    rows, columns = arrays[0].shape
    return local_call(stack_kernel, "stack", [(rows * len(arrays), columns)], arrays)[0]


def cut_kernel(joint, biases, gains, hidden, first, part):
    half = joint.shape[1] // 6
    for i in range(3):
        first[:, i * half : (i + 1) * half] = joint[:, 2 * i * half : (2 * i + 1) * half]
    small = [biases[...], gains[...], hidden[...].astype(f32).reshape(-1, LANES)]
    first[:, 3 * half :] = stack_rows(small, first.shape[0])
    part[...] = first[own_quarter(part.shape[0]), :]


def local_call(kernel, name, shapes, arrays):
    return pl.pallas_call(
        kernel,
        out_shape=[jax.ShapeDtypeStruct(s, bf16) for s in shapes],
        compiler_params=params(),
        name=name,
    )(*arrays)


def cut(joint, biases, gains, hidden, dp):
    rows, width = joint.shape
    columns = width // 2 + LANES
    return local_call(cut_kernel, "cut", [(rows, columns), (rows // dp, columns)], [joint, biases, gains, hidden])


def pack_kernel(chunks, shards, joint, up, down, wo, q_down, q_up, v_down, v_up, *refs):
    outs, parts = refs[:2], refs[2:4]
    down_map, up_map = refs[4:]
    hidden, width = down.shape
    part = hidden // chunks
    half = joint.shape[1] // 6
    for i in range(3):
        outs[0][:, i * half : (i + 1) * half] = joint[:, (2 * i + 1) * half : (2 * i + 2) * half]
    for j in range(chunks):
        out, at = (outs[1], (j - 1) * 2 * width) if j else (outs[0], 3 * half)
        for s in range(shards):
            start = s * hidden + j * part
            out[:, at + s * part : at + (s + 1) * part] = up[:, start : start + part]
        out[:, at + width : at + 2 * width] = down[j * part : (j + 1) * part, :]
    outs[0][:, 3 * half + 2 * width :] = wo[...]
    for out, part_ref in zip(outs, parts):
        part_ref[...] = out[own_quarter(part_ref.shape[0]), :]
    rank = q_up.shape[0]
    down_map[...] = jnp.zeros_like(down_map)
    down_map[:, :rank] = q_down[...]
    down_map[:, rank : 2 * rank] = v_down[...]
    zero = jnp.zeros(q_up.shape, f32)
    rows = [jnp.concatenate([q_up[...].astype(f32) * 8.0, zero], axis=1)]
    rows += [jnp.concatenate([zero, v_up[...].astype(f32) * 8.0], axis=1)]
    up_map[...] = stack_rows(rows, up_map.shape[0])


def pack(joint, up, down, wo, adapters, chunks, shards, dp):
    rows, width = up.shape[0], down.shape[1]
    shapes = [(rows, joint.shape[1] // 2 + 3 * width), (rows, 2 * (chunks - 1) * width)]
    shapes += [(r // dp, c) for r, c in shapes]
    shapes += [(width, LANES), (LANES, 2 * width)]
    return local_call(functools.partial(pack_kernel, chunks, shards), "pack", shapes, [joint, up, down, wo, *adapters])


def project_slot(first, carried, shards, w, wait, ins, outs, load):
    rows_in, down, up = ins[:3]
    q_ref, k_ref, v_ref = outs[:3]
    half = q_ref.shape[1]
    width = 2 * half
    cols = slice(0, half) if first else slice(half, width)
    wait(0)
    if first:
        low_ref, normed_ref, vec = outs[3:6]

        @pl.when(pl.program_id(0) == 0)
        def _():
            if carried:
                rows = w.shape[0] // shards
                parts = [w[s * rows : s * rows + vec.shape[0], 3 * half :] for s in range(shards)]
                vec[...] = jnp.concatenate(parts, axis=1).astype(f32)
            else:
                vec[...] = ins[3][...]
    else:
        low_in, vec = ins[3:]
    load.wait()
    sub = 256
    state = {}

    def norm(r):
        rr = slice(r, r + sub)
        if first:
            n, _ = normalise(rows_in[rr, :].astype(f32))
            normed = (n * vec[6:7, :] + vec[0:1, :]).astype(bf16)
            normed_ref[rr, :] = normed
        else:
            normed = rows_in[rr, :]
        state[r] = normed

    def mix(r):
        rr = slice(r, r + sub)
        normed = state.pop(r)
        k_ref[rr, :] = dot(normed, w[:, half : 2 * half]).astype(bf16)
        if first:
            low = dot(normed, down[...]).astype(bf16)
            low_ref[rr, :] = low
        else:
            low = low_in[rr, :]
        q = dot(normed, w[:, :half]) + dot(low, up[:, cols]) + vec[2:3, cols]
        q_ref[rr, :] = (q * SCORE_SCALE).astype(bf16)
        v = dot(normed, w[:, 2 * half : 3 * half]) + dot(low, up[:, width:][:, cols]) + vec[3:4, cols]
        v_ref[rr, :] = v.astype(bf16)

    pipelined(list(range(0, rows_in.shape[0], sub)), (norm, mix), (0, 1))


def heads_kernel(first, carried, shards, pairs, wholes, wait, ins, outs, scratch):
    lengths, x_hbm, ins = ins[0], ins[1], ins[2:]
    mask, x_ref, q_ref, k_ref, v_ref, *normed_ref, sems = scratch
    o_ref, p_ref, linv_ref = outs[-3:]
    seq, half = q_ref.shape
    blocks = seq // LANES
    slot, step = pl.program_id(0), pl.program_id(1)

    def rows(s):
        return pl.ds(pl.multiple_of(s * seq, seq), seq)

    def load(s):
        return pltpu.make_async_copy(x_hbm.at[rows(s)], x_ref, sems.at[0])

    cols = pl.ds(0 if first else half, half)
    stores = [(ref, out.at[rows(slot), cols]) for ref, out in zip((q_ref, k_ref, v_ref), outs)]
    if first:
        stores.append((normed_ref[0], outs[4].at[rows(slot)]))
    stores = [pltpu.make_async_copy(a, b, sems.at[1 + i]) for i, (a, b) in enumerate(stores)]

    @pl.when((slot == 0) & (step == 0))
    def _():
        load(0).start()

    @pl.when(step == 0)
    def _():
        own = [q_ref, k_ref, v_ref] + ([outs[3], normed_ref[0], outs[5]] if first else [])
        project_slot(first, carried, shards, wholes[0], wait, [x_ref] + list(ins), own, load(slot))
        for store in stores:
            store.start()
        fill_masks(lengths, slot, mask, blocks)

    @pl.when((step == 1) & (slot + 1 < pl.num_programs(0)))
    def _():
        load(slot + 1).start()

    @pl.when(step != 0)
    def _():
        at = pl.multiple_of((step - 1) * pairs * PAIR, pairs * PAIR)
        attend_pairs(pairs, blocks, at, q_ref, k_ref, v_ref, o_ref, p_ref, linv_ref, mask)

    @pl.when(step == pl.num_programs(1) - 1)
    def _():
        for store in stores:
            store.wait()


def heads(weight, fsdp, lengths, x, down, up, vec=None, low=None, old=()):
    tokens, width = x.shape
    slots = lengths.shape[0]
    seq = tokens // slots
    blocks, heads2, pairs = seq // LANES, width // PAIR, 2
    steps = heads2 // pairs // 2
    first = low is None
    here = 0 if first else 1
    far = pl.BlockSpec(memory_space=pltpu.HBM)
    thin = pl.BlockSpec((seq, LANES), lambda s, j: (s, 0))
    group = lambda j: here * steps + jnp.maximum(j - 1, 0)
    tile = pl.BlockSpec((seq, pairs * PAIR), lambda s, j: (s, group(j)))
    probs = (pairs, blocks, BAND * LANES, 2 * LANES)
    sums = (pairs, blocks, 2 * LANES)
    ins = [lengths, x, down, up]
    in_specs = [pl.BlockSpec(memory_space=pltpu.SMEM), far, resident(down), resident(up)]
    outs, out_specs = [jax.ShapeDtypeStruct((tokens, width), bf16)] * 3, [far] * 3
    if first:
        outs = outs + [jax.ShapeDtypeStruct((tokens, n), bf16) for n in (LANES, width)]
        outs = outs + [jax.ShapeDtypeStruct((16, width), f32)]
        out_specs = out_specs + [thin, far, pl.BlockSpec((16, width), lambda s, j: (0, 0))]
    else:
        ins, in_specs = ins + [low], in_specs + [thin]
    if vec is not None:
        ins, in_specs = ins + [vec], in_specs + [resident(vec)]
    outs = outs + [
        jax.ShapeDtypeStruct((tokens, width), bf16),
        jax.ShapeDtypeStruct((slots, heads2) + probs[1:], bf16),
        jax.ShapeDtypeStruct((slots, heads2) + sums[1:], f32),
    ]
    out_specs = out_specs + [
        tile,
        pl.BlockSpec((1,) + probs, lambda s, j: (s, group(j), 0, 0, 0)),
        pl.BlockSpec((1,) + sums, lambda s, j: (s, group(j), 0, 0)),
    ]
    carried = first and vec is None
    columns = 3 * width // 2 + (LANES if carried else 0)
    return weight_call(
        functools.partial(heads_kernel, first, carried, fsdp, pairs),
        "heads",
        [(weight, (width, columns))],
        [(0, 0, columns)],
        (slots, 1 + steps),
        ins,
        in_specs,
        out_specs,
        outs,
        [pltpu.VMEM((blocks, BAND * LANES, LANES), f32), pltpu.VMEM((seq, width), bf16)]
        + [pltpu.VMEM((seq, width // 2), bf16)] * 3
        + [pltpu.VMEM((seq, width), bf16)] * first
        + [pltpu.SemaphoreType.DMA((5,))],
        9 * tokens * width * width,
        fsdp,
        old,
    )


def fill_masks(lengths, slot, mask, blocks):
    starts = []
    total = jnp.int32(0)
    for d in range(lengths.shape[1]):
        starts.append(total)
        total = total + lengths[slot, d]
    for qb in range(blocks):
        first = max(0, qb - BAND + 1)
        rows = (qb - first + 1) * LANES
        query = qb * LANES + lax.broadcasted_iota(jnp.int32, (8, LANES), 1)
        begin = jnp.zeros((8, LANES), jnp.int32)
        for start in starts:
            begin = jnp.where(query >= start, start, begin)
        key = first * LANES + lax.broadcasted_iota(jnp.int32, (rows, LANES), 0)
        ok = (key >= begin[0:1]) & (key <= query[0:1])
        mask[qb, :rows, :] = jnp.where(ok, 0.0, MASKED)


def half_lanes():
    return lax.broadcasted_iota(jnp.int32, (LANES, LANES), 1) < 64


def half_rows():
    return lax.broadcasted_iota(jnp.int32, (LANES, LANES), 0) < 64


def split_heads(x, left):
    zero = jnp.zeros_like(x)
    return jnp.concatenate([jnp.where(left, x, zero), jnp.where(left, zero, x)], axis=0)


def pipelined(units, stages, lags):
    for t in range(len(units) + lags[-1]):
        for stage, lag in zip(stages, lags):
            if 0 <= t - lag < len(units):
                stage(units[t - lag])


def geometry(qb):
    first = max(0, qb - BAND + 1)
    return first * LANES, (qb - first + 1) * LANES


def attend_pairs(pairs, blocks, at, q_ref, k_ref, v_ref, o_ref, p_ref, linv_ref, mask):
    left, top = half_lanes(), half_rows()
    scores, probs = {}, {}

    def score(unit):
        pair, qb = unit
        cols = pl.ds(at + pair * PAIR, PAIR)
        key0, rows = geometry(qb)
        q = split_heads(q_ref[qb * LANES : (qb + 1) * LANES, cols], left)
        scores[unit] = dot_nt(k_ref[key0 : key0 + rows, cols], q)

    def soften(unit):
        pair, qb = unit
        key0, rows = geometry(qb)
        bias = mask[qb, :rows, :]
        s = scores.pop(unit) + jnp.concatenate([bias, bias], axis=1)
        p = jnp.exp2(s - jnp.max(s, axis=0, keepdims=True))
        linv = 1.0 / jnp.sum(p, axis=0, keepdims=True)
        linv_ref[0, pair, qb : qb + 1, :] = linv
        low = p.astype(bf16)
        p_ref[0, pair, qb, :rows, :] = low
        probs[unit] = (low, linv)

    def mix(unit):
        pair, qb = unit
        key0, rows = geometry(qb)
        low, linv = probs.pop(unit)
        o = dot_tn(v_ref[key0 : key0 + rows, pl.ds(at + pair * PAIR, PAIR)], low)
        o = jnp.where(top, o[:, :LANES] * linv[:, :LANES], o[:, LANES:] * linv[:, LANES:])
        o_ref[qb * LANES : (qb + 1) * LANES, pair * PAIR : (pair + 1) * PAIR] = o.T.astype(bf16)

    units = [(pair, qb) for qb in range(blocks) for pair in range(pairs)]
    pipelined(units, (score, soften, mix), (0, 2, 5))


def attend_back_kernel(
    pairs, blocks, q_ref, k_ref, v_ref, g_ref, o_ref, p_ref, linv_ref, low, normed, up, *refs
):
    dq_ref, dk_ref, dv_ref, glow_ref, grads, dk_sum, dv_sum, glow_sum = refs
    left, top = half_lanes(), half_rows()
    ones = jnp.ones((BAND * LANES, LANES), bf16)
    dk_sum[...] = jnp.zeros_like(dk_sum)
    dv_sum[...] = jnp.zeros_like(dv_sum)
    first, second = {}, {}

    def grad_probs(unit):
        pair, qb = unit
        cols = slice(pair * PAIR, (pair + 1) * PAIR)
        key0, rows = geometry(qb)
        here = slice(qb * LANES, (qb + 1) * LANES)
        linv = linv_ref[0, pair, qb : qb + 1, :]
        linv = jnp.where(top, linv[:, :LANES], linv[:, LANES:]).T
        g = g_ref[here, cols].astype(f32) * linv
        delta = split_heads(-(g * o_ref[here, cols].astype(f32)).astype(bf16), left)
        g = split_heads(g.astype(bf16), left)
        values = jnp.concatenate([v_ref[key0 : key0 + rows, cols], ones[:rows]], axis=1)
        first[unit] = (dot_nt(values, jnp.concatenate([g, delta], axis=1)), g)

    def grad_values(unit):
        pair, qb = unit
        cols = slice(pair * PAIR, (pair + 1) * PAIR)
        key0, rows = geometry(qb)
        dp, g = first.pop(unit)
        low = p_ref[0, pair, qb, :rows, :]
        second[unit] = low * dp.astype(bf16)
        dv_sum[key0 : key0 + rows, cols] += dot(low, g)

    def grad_queries_keys(unit):
        pair, qb = unit
        cols = slice(pair * PAIR, (pair + 1) * PAIR)
        key0, rows = geometry(qb)
        here = slice(qb * LANES, (qb + 1) * LANES)
        ds = second.pop(unit)
        dk_sum[key0 : key0 + rows, cols] += dot(ds, split_heads(q_ref[here, cols], left))
        dq = dot_tn(k_ref[key0 : key0 + rows, cols], ds)
        dq = jnp.where(top, dq[:, :LANES], dq[:, LANES:]) * 0.125
        dq_ref[here, cols] = dq.T.astype(bf16)

    units = [(pair, qb) for qb in range(blocks) for pair in range(pairs)]
    pipelined(units, (grad_probs, grad_values, grad_queries_keys), (0, 2, 4))
    dk_ref[...] = (dk_sum[...] * (0.125 / SCORE_SCALE)).astype(bf16)
    dv_ref[...] = dv_sum[...].astype(bf16)

    slot, step, last = pl.program_id(0), pl.program_id(1), pl.num_programs(1) - 1
    width = normed.shape[1]
    at = pl.multiple_of(step * pairs * PAIR, pairs * PAIR)
    here = pl.ds(at, pairs * PAIR)
    both = jnp.concatenate([dq_ref[...], dv_ref[...]], axis=1)
    part = dot_tn(low[...], both)
    part = jnp.concatenate([part[0:4, : pairs * PAIR], part[4:8, pairs * PAIR :]], axis=0) * 8.0
    grads[0:8, here] = jnp.where(slot == 0, part, grads[0:8, here] + part)
    glow = dot_nt(both, jnp.concatenate([up[:, here], up[:, pl.ds(width + at, pairs * PAIR)]], axis=1))
    glow_sum[...] = jnp.where(step == 0, glow, glow_sum[...] + glow)

    @pl.when(step == last)
    def _():
        glow = glow_sum[...].astype(bf16)
        glow_ref[...] = glow
        part = dot_tn(glow, normed[...])[0:8]
        grads[8:16, :] = jnp.where(slot == 0, part, grads[8:16, :] + part)


def attend_back(slots, q, k, v, g, o, p, linv, low, normed, up):
    tokens, width = q.shape
    seq = tokens // slots
    blocks, heads2, pairs = seq // LANES, width // PAIR, 2
    rows = BAND * LANES
    tile = pl.BlockSpec((seq, pairs * PAIR), lambda s, h: (s, h))
    thin = pl.BlockSpec((seq, LANES), lambda s, h: (s, 0))
    return pl.pallas_call(
        functools.partial(attend_back_kernel, pairs, blocks),
        grid=(slots, heads2 // pairs),
        in_specs=[tile] * 5
        + [
            pl.BlockSpec((1, pairs, blocks, rows, 2 * LANES), lambda s, h: (s, h, 0, 0, 0)),
            pl.BlockSpec((1, pairs, blocks, 2 * LANES), lambda s, h: (s, h, 0, 0)),
            thin,
            pl.BlockSpec((seq, width), lambda s, h: (s, 0)),
            resident(up),
        ],
        out_specs=[tile] * 3 + [thin, pl.BlockSpec((16, width), lambda s, h: (0, 0))],
        scratch_shapes=[pltpu.VMEM((seq, pairs * PAIR), f32)] * 2 + [pltpu.VMEM((seq, LANES), f32)],
        out_shape=[jax.ShapeDtypeStruct(q.shape, bf16)] * 3
        + [jax.ShapeDtypeStruct((tokens, LANES), bf16), jax.ShapeDtypeStruct((16, width), f32)],
        compiler_params=params(),
        cost_estimate=pl.CostEstimate(flops=14 * tokens * width * width // COST, bytes_accessed=2**20, transcendentals=0),
        name="attend_back",
    )(q, k, v, g, o, p, linv, low, normed, up)


def feed_chunk(wait, first, normed, cot, w, at, bias):
    width = cot.shape[1]
    wait(first)
    wait(first + 1)
    size = width // 4
    up, down = slice(at, at + width), slice(at + width, at + 2 * width)
    acts, grads = [], []
    for i in range(0, width, size):
        grad = dot_nt(cot, w[i : i + size, down])
        act, slope = gelu_and_slope(dot(normed, w[:, at + i : at + i + size]) + bias[:, i : i + size])
        acts.append(act.astype(bf16))
        grads.append((slope * grad).astype(bf16))
    return dot(jnp.concatenate(acts, axis=1), w[:, down]), dot_nt(jnp.concatenate(grads, axis=1), w[:, up])


def feed_first_kernel(wholes, wait, ins, outs, _):
    tok, att, cot, vec = ins
    h1_ref, normed_ref, o_ref, g_ref = outs
    width = tok.shape[1]
    wait(0)
    h1 = tok[...].astype(f32) + dot(att[...], wholes[0][:, 2 * width :]) + vec[4:5, :]
    h1_ref[...] = h1
    n, _ = normalise(h1)
    normed = (n * vec[7:8, :] + vec[1:2, :]).astype(bf16)
    normed_ref[...] = normed
    o_ref[...], g_ref[...] = feed_chunk(wait, 1, normed, cot[...], wholes[0], 0, vec[8:9, :])


def feed_last_kernel(wholes, wait, ins, outs, scratch):
    normed, cot, vec, h1, old_o, old_g = ins
    out_ref, gh_ref, ga_ref = outs
    x_ref, o_sum, g_sum, sems = scratch
    rows, width = cot.shape
    here = pl.ds(pl.multiple_of(pl.program_id(0) * rows, rows), rows)
    loads = [(old_o, o_sum), (old_g, g_sum), (h1, x_ref)]
    loads = [pltpu.make_async_copy(a.at[here], b, sems.at[i]) for i, (a, b) in enumerate(loads)]
    for load in loads:
        load.start()
    chunks = wholes[0].shape[1] // (2 * width)
    for j in range(chunks):
        bias = vec[9 + j : 10 + j, :]
        o, g = feed_chunk(wait, 2 * j, normed[...], cot[...], wholes[0], 2 * j * width, bias)
        if j == 0:
            for load in loads:
                load.wait()
        if j < chunks - 1:
            o_sum[...] += o
            g_sum[...] += g
    x = x_ref[...]
    out_ref[...] = (x + (o_sum[...] + o) + vec[5:6, :]).astype(bf16)
    n, r = normalise(x)
    grad = cot[...].astype(f32) + norm_back(n, r, (g_sum[...] + g) * vec[7:8, :])
    low = grad.astype(bf16)
    gh_ref[...] = low
    wait(2 * chunks)
    ga_ref[...] = dot_nt(low, wholes[1][...]).astype(bf16)


def feed_call(kernel, name, weights, order, fsdp, rowwise, vec, far, out_types):
    tokens, width = rowwise[0].shape
    rows = 512
    row = pl.BlockSpec((rows, width), lambda i: (i, 0))
    scratch = [pltpu.VMEM((rows, width), f32)] * len(far)
    return weight_call(
        kernel,
        name,
        weights,
        order,
        (tokens // rows,),
        rowwise + [vec] + far,
        [row] * len(rowwise) + [resident(vec)] + [pl.BlockSpec(memory_space=pltpu.HBM)] * len(far),
        [row] * len(out_types),
        [jax.ShapeDtypeStruct((tokens, width), t) for t in out_types],
        scratch + ([pltpu.SemaphoreType.DMA((len(far),))] if far else []),
        18 * tokens * width * width,
        fsdp,
    )


def feed_order(width, chunks):
    return [(0, (2 * j + 1 - i) * width, width) for j in range(chunks) for i in (0, 1)]


def feed_first(feeds, fsdp, tok, att, cot, vec):
    width = tok.shape[1]
    weights = [(feeds[0], (width, 3 * width))]
    order = [(0, 2 * width, width)] + feed_order(width, 1)
    types = [f32, bf16, f32, f32]
    return feed_call(feed_first_kernel, "feed_first", weights, order, fsdp, [tok, att, cot], vec, [], types)


def feed_last(feeds, fsdp, h1, normed, o, g, cot, vec):
    width = cot.shape[1]
    weights = [(feeds[1], (width, 6 * width)), (feeds[0], (width, width))]
    order = feed_order(width, 3) + [(1, 2 * width, width)]
    rowwise, far = [normed, cot], [h1, o, g]
    return feed_call(feed_last_kernel, "feed_last", weights, order, fsdp, rowwise, vec, far, [bf16] * 3)


def input_kernel(wholes, wait, ins, outs, _):
    dq, dk, dv, glow, down, vec, tok, gh = ins
    (out_ref,) = outs
    half = dq.shape[1] // 2
    g = dot_nt(glow[...], down[...])
    for i, w in enumerate(wholes):
        wait(i)
        cols = slice(i * half, (i + 1) * half)
        g = g + dot_nt(dq[:, cols], w[:, :half])
        g = g + dot_nt(dk[:, cols], w[:, half : 2 * half])
        g = g + dot_nt(dv[:, cols], w[:, 2 * half : 3 * half])
    n, r = normalise(tok[...].astype(f32))
    out_ref[...] = (gh[...].astype(f32) + norm_back(n, r, g * vec[6:7, :])).astype(bf16)


def input_grad(joint, fsdp, tok, gh, dq, dk, dv, glow, down, vec):
    tokens, width = tok.shape
    rows = 512
    row = pl.BlockSpec((rows, width), lambda i: (i, 0))
    thin = pl.BlockSpec((rows, LANES), lambda i: (i, 0))
    return weight_call(
        input_kernel,
        "input_grad",
        [(w, (width, 3 * width // 2)) for w in joint],
        [(0, 0, 3 * width // 2), (1, 0, 3 * width // 2)],
        (tokens // rows,),
        [dq, dk, dv, glow, down, vec, tok, gh],
        [row] * 3 + [thin, resident(down), resident(vec), row, row],
        [row],
        [jax.ShapeDtypeStruct((tokens, width), bf16)],
        [],
        6 * tokens * width * width,
        fsdp,
    )[0]


def per_device(
    tokens,
    document_length_list,
    joint_projection_weight,
    attention_out_weight,
    feed_up_weight,
    feed_down_weight,
    frozen_norm_gains,
    biases,
    hidden_up_bias,
    query_down_adapter,
    query_up_adapter,
    value_down_adapter,
    value_up_adapter,
    cotangent,
):
    micro, local, seq, width = tokens.shape
    slots = micro * local
    shards = width // joint_projection_weight.shape[0]
    hidden = feed_down_weight.shape[0]
    tok = tokens.reshape(slots * seq, width)
    cot = cotangent.reshape(slots * seq, width)
    lengths = document_length_list.reshape(slots, -1)

    dp = lax.axis_size("dp")
    chunks = 4
    part = hidden // chunks
    stepped = dp == 4 and shards == 8 and part == LANES and width == shards * LANES

    def gather(x):
        return lax.all_gather(x, "fsdp", axis=0, tiled=True)

    adapters = [query_down_adapter, query_up_adapter, value_down_adapter, value_up_adapter]
    if stepped:
        a, part_a = cut(joint_projection_weight, biases, frozen_norm_gains, hidden_up_bias, dp)
        link = Gather(dp, shards)
        near = link.step_1(part_a)
        shards_here = [joint_projection_weight, feed_up_weight, feed_down_weight, attention_out_weight]
        *shards_here, part_a = after_all(shards_here + [part_a], a)
        b, c, part_b, part_c, down_map, up_map = pack(*shards_here, adapters, chunks, shards, dp)
        b_near = link.step_1(part_b)
        near = after_all(near, part_c)
        a_far = link.all_far(near)
        b_far = link.all_far(b_near)
        c_near = link.step_1(after(part_c, b_near))
        joint = [pieces(a, link.swap(a), [a_far], [link.swap(a_far)])]
        vec = None
    else:
        small = jnp.concatenate([biases, frozen_norm_gains], axis=0)
        small = lax.all_gather(small, "fsdp", axis=1, tiled=True)
        hidden_bias = lax.all_gather(hidden_up_bias, "fsdp", axis=0, tiled=False)
        hidden_bias = [hidden_bias[:, j * part : (j + 1) * part].reshape(1, -1) for j in range(chunks)]
        vec = jnp.concatenate([small] + hidden_bias, axis=0)
        vec = jnp.pad(vec, ((0, 16 - 8 - chunks), (0, 0))).astype(f32)
        third = [width * i // 2 for i in range(6)]
        joint = []
        for i in (0, 1):
            cols = [lax.slice_in_dim(joint_projection_weight, t, t + width // 2, axis=1) for t in third[i::2]]
            joint.append([(gather(jnp.concatenate(cols, axis=1)), 0, 0, "whole")])
        up_parts = feed_up_weight.reshape(-1, shards, chunks, part)
        feeds = []
        for group in ((0,), tuple(range(1, chunks))):
            cols = []
            for j in group:
                cols.append(up_parts[:, :, j, :].reshape(-1, shards * part))
                cols.append(feed_down_weight[j * part : (j + 1) * part])
            if group[0] == 0:
                cols.append(attention_out_weight)
            feeds.append([(gather(jnp.concatenate(cols, axis=1)), 0, 0, "whole")])
        rank = query_down_adapter.shape[1]
        down_map = jnp.concatenate([query_down_adapter, value_down_adapter], axis=1)
        down_map = jnp.pad(down_map, ((0, 0), (0, LANES - 2 * rank)))
        zero = jnp.zeros_like(query_up_adapter)
        up_map = jnp.concatenate(
            [
                jnp.concatenate([query_up_adapter, zero], axis=1),
                jnp.concatenate([zero, value_up_adapter], axis=1),
            ],
            axis=0,
        )
        up_map = jnp.pad(up_map * 8, ((0, LANES - 2 * rank), (0, 0))).astype(bf16)

    q, k, v, low, normed, vec, *kept = heads(joint[0], shards, lengths, tok, down_map, up_map, vec)
    if stepped:
        b_far, *c_near, q = after_all([b_far] + c_near + [q], low)
        b_rest = [link.swap(b), [b_far], [link.swap(b_far)]]
        c_far = link.each_far(c_near)
        joint.append(pieces(b, *b_rest))
    old = [q, k, v] + kept
    q, k, v, att, probs, linv = heads(joint[1], shards, lengths, normed, down_map, up_map, vec, low, old)
    if stepped:
        feeds = [pieces(b, *b_rest, joint_projection_weight.shape[1] // 2, joint_projection_weight.shape[1] // 2)]
        c_other = [link.swap(c_far[0])]
        *c_other, att = after_all(c_other + [att], vec)
    h1, normed_2, o, g = feed_first(feeds, shards, tok, att, cot, vec)
    if stepped:
        *far, o = after_all(c_far[1:] + [o], h1)
        c_other += [link.swap(x) for x in far]
        feeds.append(pieces(c, link.swap(after(c, vec)), c_far[:1] + far, c_other))
    out, gh, ga = feed_last(feeds, shards, h1, normed_2, o, g, cot, vec)

    dq, dk, dv, glow, grads = attend_back(slots, q, k, v, ga, att, probs, linv, low, normed, up_map)
    if stepped:
        total = Gather(dp, shards)
        grads = grads + total.move(grads, lambda d, f: (d, f ^ 1))
        _, a, b, c = total.each_far([grads])
        grads = (grads + a) + (b + c)
        a, b, c = [total.move(grads, lambda d, f, k=k: (d, (f + 2 * k) % shards)) for k in (1, 2, 3)]
        dq = after(dq, grads)
        grad_in = input_grad(joint, shards, tok, gh, dq, dk, dv, glow, down_map, vec)
        a, b, c = after_all([a, b, c], grad_in)
        grads = (grads + b) + (a + c)
    else:
        grads = jnp.sum(lax.all_gather(grads, ("dp", "fsdp"), axis=0, tiled=False), axis=0)
        grad_in = input_grad(joint, shards, tok, gh, dq, dk, dv, glow, down_map, vec)
    return (
        out.reshape(tokens.shape),
        grad_in.reshape(tokens.shape),
        grads[8:12].T,
        grads[0:4],
        grads[12:16].T,
        grads[4:8],
    )


def solution(mesh):
    slots = P(None, ("dp", "fsdp"), None, None)
    return jax.shard_map(
        per_device,
        mesh=mesh,
        in_specs=(
            slots,
            P(None, ("dp", "fsdp"), None),
            P("fsdp", None),
            P("fsdp", None),
            P("fsdp", None),
            P("fsdp", None),
            P(None, "fsdp"),
            P(None, "fsdp"),
            P("fsdp"),
            P(),
            P(),
            P(),
            P(),
            slots,
        ),
        out_specs=(slots, slots, P(), P(), P(), P()),
        check_vma=False,
    )
```

```python
import functools
import math

import jax
import jax.numpy as jnp
from jax import lax
from jax.experimental import pallas as pl
from jax.experimental.pallas import tpu as pltpu
from jax.sharding import PartitionSpec as P

f32 = jnp.float32
bf16 = jnp.bfloat16
LANES = 128
PAIR = 128
BAND = 3
EPS = 1e-5
MASKED = -1e30
SCORE_SCALE = 0.125 * math.log2(math.e)
GELU_C = math.sqrt(2.0 / math.pi)
VMEM_LIMIT = 58 * 2**20
COST = 8
NT = (((1,), (1,)), ((), ()))
TN = (((0,), (0,)), ((), ()))


def dot(a, b):
    return jnp.dot(a, b, preferred_element_type=f32)


def dot_nt(a, b):
    return lax.dot_general(a, b, NT, preferred_element_type=f32)


def dot_tn(a, b):
    return lax.dot_general(a, b, TN, preferred_element_type=f32)


def params():
    return pltpu.CompilerParams(vmem_limit_bytes=VMEM_LIMIT)


def resident(array):
    zeros = (0,) * array.ndim
    return pl.BlockSpec(array.shape, lambda *_: zeros, pipeline_mode=pl.Buffered(1))


def normalise(x):
    centred = x - jnp.mean(x, axis=-1, keepdims=True)
    r = lax.rsqrt(jnp.mean(centred * centred, axis=-1, keepdims=True) + EPS)
    return centred * r, r


def norm_back(n, r, w):
    return r * (w - jnp.mean(w, axis=-1, keepdims=True) - n * jnp.mean(w * n, axis=-1, keepdims=True))


def gelu_and_slope(x):
    x2 = x * x
    t = jnp.tanh(x * (GELU_C + (GELU_C * 0.044715) * x2))
    half = 0.5 + 0.5 * t
    act = x * half
    slope = half + (act * (1.0 - half)) * (2 * GELU_C + (6 * GELU_C * 0.044715) * x2)
    return act, slope


def ring_pairs(dp, fsdp, move):
    pairs = []
    for d in range(dp):
        for f in range(fsdp):
            e, g = move(d, f)
            pairs.append((d * fsdp + f, e * fsdp + g))
    return pairs


def after(x, others):
    return lax.optimization_barrier((x, others))[0]


def after_all(xs, others):
    return lax.optimization_barrier((xs, others))[0]


class Gather:
    def __init__(self, dp, fsdp):
        self.dp, self.fsdp = dp, fsdp

    def move(self, x, where):
        return lax.ppermute(x, ("dp", "fsdp"), ring_pairs(self.dp, self.fsdp, where))

    def step_1(self, mine):
        fsdp = self.fsdp
        return [self.move(mine, lambda d, f, k=k: (d, (f + 2 * k) % fsdp)) for k in range(1, fsdp // 2)]

    def all_far(self, near):
        near = [jnp.broadcast_to(x[None], (self.dp,) + x.shape) for x in near]
        return lax.all_to_all(jnp.concatenate(near, axis=1), "dp", 0, 0, tiled=False)

    def each_far(self, near):
        near = stack(near) if len(near) > 1 else near[0]
        return [near] + [self.move(near, lambda d, f, e=e: (d ^ e, f)) for e in range(1, self.dp)]

    def swap(self, x):
        return self.move(x, lambda d, f: (d, f ^ 1))


def pieces(shard, other_shard, far, other_far, shard_column=0, far_column=0):
    made = [(shard, shard_column, 0, "shard"), (other_shard, shard_column, 1, "shard")]
    for swapped, arrays in ((0, far), (1, other_far)):
        if len(arrays) == 1:
            made.append((arrays[0], far_column, swapped, "all"))
        else:
            made += [(x, far_column, swapped, e) for e, x in enumerate(arrays)]
    return made


def copies(weight, refs, whole, sems, place, cols, base, dp, fsdp):
    made = []
    start, size = cols
    rows = whole.shape[0] // fsdp
    part = rows // dp
    index = place[1]

    def add(source, first, at, rows):
        target = whole.at[pl.ds(at, rows), pl.ds(start - base, size)]
        made.append(pltpu.make_async_copy(source.at[:, pl.ds(first + start, size)], target, sems.at[len(made)]))

    for (_, column, swapped, what), ref in zip(weight, refs):
        other = swapped * (1 - 2 * lax.rem(index, 2))
        if what == "whole":
            add(ref, column, 0, whole.shape[0])
        elif what == "shard":
            add(ref, column, pl.multiple_of((index + other) * rows, rows), rows)
        else:
            for e in range(dp) if what == "all" else [what]:
                quarter = e if what == "all" else jnp.bitwise_xor(place[0], e)
                for k in range(1, fsdp // 2):
                    owner = lax.rem(index + fsdp - 2 * k, fsdp) + other
                    at = pl.multiple_of(owner * rows + quarter * part, part)
                    here = pl.ds((k - 1) * part, part)
                    add(ref.at[e, here] if what == "all" else ref.at[here], column, at, part)
    return made


def copy_count(weight, dp, fsdp):
    count = 0
    for _, _, _, what in weight:
        count += 1 if what in ("whole", "shard") else (fsdp // 2 - 1) * (dp if what == "all" else 1)
    return count


def weight_call(kernel, name, weights, order, grid, blocked, in_specs, out_specs, out_shape, scratch, cost, fsdp, old=()):
    dp = lax.axis_size("dp")
    arrays = [[piece[0] for piece in w] for w, _ in weights]
    flat = [a for some in arrays for a in some]
    counts = [copy_count(weights[i][0], dp, fsdp) for i, _, _ in order]

    def body(*refs):
        refs = list(refs)
        place = [lax.axis_index("dp"), lax.axis_index("fsdp")]
        take = lambda n: [refs.pop(0) for _ in range(n)]
        sources = [take(len(some)) for some in arrays]
        ins, _, outs = take(len(blocked)), take(len(old)), take(len(out_shape))
        wholes, sems = take(len(weights)), take(len(order))

        first_step = pl.program_id(0) == 0
        for axis in range(1, len(grid)):
            first_step = first_step & (pl.program_id(axis) == 0)

        def group(n):
            i, start, size = order[n]
            base = start if wholes[i].shape[1] == size else 0
            return copies(weights[i][0], sources[i], wholes[i], sems[n], place, (start, size), base, dp, fsdp)

        @pl.when(first_step)
        def _():
            for n in range(len(order)):
                for copy in group(n):
                    copy.start()

        def wait(n):
            @pl.when(first_step)
            def _():
                for copy in group(n):
                    copy.wait()

        kernel(wholes, wait, ins, outs, refs)

    return pl.pallas_call(
        body,
        grid=grid,
        in_specs=[pl.BlockSpec(memory_space=pltpu.HBM)] * len(flat)
        + in_specs
        + [pl.BlockSpec(memory_space=pl.ANY)] * len(old),
        out_specs=out_specs,
        scratch_shapes=[pltpu.VMEM(shape, bf16) for _, shape in weights]
        + [pltpu.SemaphoreType.DMA((n,)) for n in counts]
        + scratch,
        out_shape=out_shape,
        compiler_params=params(),
        cost_estimate=pl.CostEstimate(flops=cost // COST, bytes_accessed=2**20, transcendentals=0),
        input_output_aliases={len(flat) + len(blocked) + i: i for i in range(len(old))},
        name=name,
    )(*flat, *blocked, *old)


def own_quarter(rows):
    return pl.ds(pl.multiple_of(lax.axis_index("dp") * rows, rows), rows)


def stack_rows(arrays, rows):
    arrays = [a.astype(f32) for a in arrays]
    used = sum(a.shape[0] for a in arrays)
    return jnp.concatenate(arrays + [jnp.zeros((rows - used, arrays[0].shape[1]), f32)], axis=0).astype(bf16)


def stack_kernel(*refs):
    rows = refs[0].shape[0]
    for i, ref in enumerate(refs[:-1]):
        refs[-1][i * rows : (i + 1) * rows, :] = ref[...]


def stack(arrays):
    rows, columns = arrays[0].shape
    return local_call(stack_kernel, "stack", [(rows * len(arrays), columns)], arrays)[0]


def cut_kernel(joint, biases, gains, hidden, first, part):
    half = joint.shape[1] // 6
    for i in range(3):
        first[:, i * half : (i + 1) * half] = joint[:, 2 * i * half : (2 * i + 1) * half]
    small = [biases[...], gains[...], hidden[...].astype(f32).reshape(-1, LANES)]
    first[:, 3 * half :] = stack_rows(small, first.shape[0])
    part[...] = first[own_quarter(part.shape[0]), :]


def local_call(kernel, name, shapes, arrays):
    return pl.pallas_call(
        kernel,
        out_shape=[jax.ShapeDtypeStruct(s, bf16) for s in shapes],
        compiler_params=params(),
        name=name,
    )(*arrays)


def cut(joint, biases, gains, hidden, dp):
    rows, width = joint.shape
    columns = width // 2 + LANES
    return local_call(cut_kernel, "cut", [(rows, columns), (rows // dp, columns)], [joint, biases, gains, hidden])


def pack_kernel(chunks, shards, joint, up, down, wo, q_down, q_up, v_down, v_up, *refs):
    outs, parts = refs[:2], refs[2:4]
    down_map, up_map = refs[4:]
    hidden, width = down.shape
    part = hidden // chunks
    half = joint.shape[1] // 6
    for i in range(3):
        outs[0][:, i * half : (i + 1) * half] = joint[:, (2 * i + 1) * half : (2 * i + 2) * half]
    for j in range(chunks):
        out, at = (outs[1], (j - 1) * 2 * width) if j else (outs[0], 3 * half)
        for s in range(shards):
            start = s * hidden + j * part
            out[:, at + s * part : at + (s + 1) * part] = up[:, start : start + part]
        out[:, at + width : at + 2 * width] = down[j * part : (j + 1) * part, :]
    outs[0][:, 3 * half + 2 * width :] = wo[...]
    for out, part_ref in zip(outs, parts):
        part_ref[...] = out[own_quarter(part_ref.shape[0]), :]
    rank = q_up.shape[0]
    down_map[...] = jnp.zeros_like(down_map)
    down_map[:, :rank] = q_down[...]
    down_map[:, rank : 2 * rank] = v_down[...]
    zero = jnp.zeros(q_up.shape, f32)
    rows = [jnp.concatenate([q_up[...].astype(f32) * 8.0, zero], axis=1)]
    rows += [jnp.concatenate([zero, v_up[...].astype(f32) * 8.0], axis=1)]
    up_map[...] = stack_rows(rows, up_map.shape[0])


def pack(joint, up, down, wo, adapters, chunks, shards, dp):
    rows, width = up.shape[0], down.shape[1]
    shapes = [(rows, joint.shape[1] // 2 + 3 * width), (rows, 2 * (chunks - 1) * width)]
    shapes += [(r // dp, c) for r, c in shapes]
    shapes += [(width, LANES), (LANES, 2 * width)]
    return local_call(functools.partial(pack_kernel, chunks, shards), "pack", shapes, [joint, up, down, wo, *adapters])


def project_slot(first, carried, shards, w, wait, ins, outs, load):
    rows_in, down, up = ins[:3]
    q_ref, k_ref, v_ref = outs[:3]
    half = q_ref.shape[1]
    width = 2 * half
    cols = slice(0, half) if first else slice(half, width)
    wait(0)
    if first:
        low_ref, normed_ref, vec = outs[3:6]

        @pl.when(pl.program_id(0) == 0)
        def _():
            if carried:
                rows = w.shape[0] // shards
                parts = [w[s * rows : s * rows + vec.shape[0], 3 * half :] for s in range(shards)]
                vec[...] = jnp.concatenate(parts, axis=1).astype(f32)
            else:
                vec[...] = ins[3][...]
    else:
        low_in, vec = ins[3:]
    load.wait()
    sub = 256
    state = {}

    def norm(r):
        rr = slice(r, r + sub)
        if first:
            n, _ = normalise(rows_in[rr, :].astype(f32))
            normed = (n * vec[6:7, :] + vec[0:1, :]).astype(bf16)
            normed_ref[rr, :] = normed
        else:
            normed = rows_in[rr, :]
        state[r] = normed

    def mix(r):
        rr = slice(r, r + sub)
        normed = state.pop(r)
        k_ref[rr, :] = dot(normed, w[:, half : 2 * half]).astype(bf16)
        if first:
            low = dot(normed, down[...]).astype(bf16)
            low_ref[rr, :] = low
        else:
            low = low_in[rr, :]
        q = dot(normed, w[:, :half]) + dot(low, up[:, cols]) + vec[2:3, cols]
        q_ref[rr, :] = (q * SCORE_SCALE).astype(bf16)
        v = dot(normed, w[:, 2 * half : 3 * half]) + dot(low, up[:, width:][:, cols]) + vec[3:4, cols]
        v_ref[rr, :] = v.astype(bf16)

    pipelined(list(range(0, rows_in.shape[0], sub)), (norm, mix), (0, 1))


def heads_kernel(first, carried, shards, pairs, wholes, wait, ins, outs, scratch):
    lengths, x_hbm, ins = ins[0], ins[1], ins[2:]
    mask, x_ref, q_ref, k_ref, v_ref, *normed_ref, sems = scratch
    o_ref, p_ref, linv_ref = outs[-3:]
    seq, half = q_ref.shape
    blocks = seq // LANES
    slot, step = pl.program_id(0), pl.program_id(1)

    def rows(s):
        return pl.ds(pl.multiple_of(s * seq, seq), seq)

    def load(s):
        return pltpu.make_async_copy(x_hbm.at[rows(s)], x_ref, sems.at[0])

    cols = pl.ds(0 if first else half, half)
    stores = [(ref, out.at[rows(slot), cols]) for ref, out in zip((q_ref, k_ref, v_ref), outs)]
    if first:
        stores.append((normed_ref[0], outs[4].at[rows(slot)]))
    stores = [pltpu.make_async_copy(a, b, sems.at[1 + i]) for i, (a, b) in enumerate(stores)]

    @pl.when((slot == 0) & (step == 0))
    def _():
        load(0).start()

    @pl.when(step == 0)
    def _():
        own = [q_ref, k_ref, v_ref] + ([outs[3], normed_ref[0], outs[5]] if first else [])
        project_slot(first, carried, shards, wholes[0], wait, [x_ref] + list(ins), own, load(slot))
        for store in stores:
            store.start()
        fill_masks(lengths, slot, mask, blocks)

    @pl.when((step == 1) & (slot + 1 < pl.num_programs(0)))
    def _():
        load(slot + 1).start()

    @pl.when(step != 0)
    def _():
        at = pl.multiple_of((step - 1) * pairs * PAIR, pairs * PAIR)
        attend_pairs(pairs, blocks, at, q_ref, k_ref, v_ref, o_ref, p_ref, linv_ref, mask)

    @pl.when(step == pl.num_programs(1) - 1)
    def _():
        for store in stores:
            store.wait()


def heads(weight, fsdp, lengths, x, down, up, vec=None, low=None, old=()):
    tokens, width = x.shape
    slots = lengths.shape[0]
    seq = tokens // slots
    blocks, heads2, pairs = seq // LANES, width // PAIR, 2
    steps = heads2 // pairs // 2
    first = low is None
    here = 0 if first else 1
    far = pl.BlockSpec(memory_space=pltpu.HBM)
    thin = pl.BlockSpec((seq, LANES), lambda s, j: (s, 0))
    group = lambda j: here * steps + jnp.maximum(j - 1, 0)
    tile = pl.BlockSpec((seq, pairs * PAIR), lambda s, j: (s, group(j)))
    probs = (pairs, blocks, BAND * LANES, 2 * LANES)
    sums = (pairs, blocks, 2 * LANES)
    ins = [lengths, x, down, up]
    in_specs = [pl.BlockSpec(memory_space=pltpu.SMEM), far, resident(down), resident(up)]
    outs, out_specs = [jax.ShapeDtypeStruct((tokens, width), bf16)] * 3, [far] * 3
    if first:
        outs = outs + [jax.ShapeDtypeStruct((tokens, n), bf16) for n in (LANES, width)]
        outs = outs + [jax.ShapeDtypeStruct((16, width), f32)]
        out_specs = out_specs + [thin, far, pl.BlockSpec((16, width), lambda s, j: (0, 0))]
    else:
        ins, in_specs = ins + [low], in_specs + [thin]
    if vec is not None:
        ins, in_specs = ins + [vec], in_specs + [resident(vec)]
    outs = outs + [
        jax.ShapeDtypeStruct((tokens, width), bf16),
        jax.ShapeDtypeStruct((slots, heads2) + probs[1:], bf16),
        jax.ShapeDtypeStruct((slots, heads2) + sums[1:], f32),
    ]
    out_specs = out_specs + [
        tile,
        pl.BlockSpec((1,) + probs, lambda s, j: (s, group(j), 0, 0, 0)),
        pl.BlockSpec((1,) + sums, lambda s, j: (s, group(j), 0, 0)),
    ]
    carried = first and vec is None
    columns = 3 * width // 2 + (LANES if carried else 0)
    return weight_call(
        functools.partial(heads_kernel, first, carried, fsdp, pairs),
        "heads",
        [(weight, (width, columns))],
        [(0, 0, columns)],
        (slots, 1 + steps),
        ins,
        in_specs,
        out_specs,
        outs,
        [pltpu.VMEM((blocks, BAND * LANES, LANES), f32), pltpu.VMEM((seq, width), bf16)]
        + [pltpu.VMEM((seq, width // 2), bf16)] * 3
        + [pltpu.VMEM((seq, width), bf16)] * first
        + [pltpu.SemaphoreType.DMA((5,))],
        9 * tokens * width * width,
        fsdp,
        old,
    )


def fill_masks(lengths, slot, mask, blocks):
    starts = []
    total = jnp.int32(0)
    for d in range(lengths.shape[1]):
        starts.append(total)
        total = total + lengths[slot, d]
    for qb in range(blocks):
        first = max(0, qb - BAND + 1)
        rows = (qb - first + 1) * LANES
        query = qb * LANES + lax.broadcasted_iota(jnp.int32, (8, LANES), 1)
        begin = jnp.zeros((8, LANES), jnp.int32)
        for start in starts:
            begin = jnp.where(query >= start, start, begin)
        key = first * LANES + lax.broadcasted_iota(jnp.int32, (rows, LANES), 0)
        ok = (key >= begin[0:1]) & (key <= query[0:1])
        mask[qb, :rows, :] = jnp.where(ok, 0.0, MASKED)


def half_lanes():
    return lax.broadcasted_iota(jnp.int32, (LANES, LANES), 1) < 64


def half_rows():
    return lax.broadcasted_iota(jnp.int32, (LANES, LANES), 0) < 64


def split_heads(x, left):
    zero = jnp.zeros_like(x)
    return jnp.concatenate([jnp.where(left, x, zero), jnp.where(left, zero, x)], axis=0)


def pipelined(units, stages, lags):
    for t in range(len(units) + lags[-1]):
        for stage, lag in zip(stages, lags):
            if 0 <= t - lag < len(units):
                stage(units[t - lag])


def geometry(qb):
    first = max(0, qb - BAND + 1)
    return first * LANES, (qb - first + 1) * LANES


def attend_pairs(pairs, blocks, at, q_ref, k_ref, v_ref, o_ref, p_ref, linv_ref, mask):
    left, top = half_lanes(), half_rows()
    scores, probs = {}, {}

    def score(unit):
        pair, qb = unit
        cols = pl.ds(at + pair * PAIR, PAIR)
        key0, rows = geometry(qb)
        q = split_heads(q_ref[qb * LANES : (qb + 1) * LANES, cols], left)
        scores[unit] = dot_nt(k_ref[key0 : key0 + rows, cols], q)

    def soften(unit):
        pair, qb = unit
        key0, rows = geometry(qb)
        bias = mask[qb, :rows, :]
        s = scores.pop(unit) + jnp.concatenate([bias, bias], axis=1)
        p = jnp.exp2(s - jnp.max(s, axis=0, keepdims=True))
        linv = 1.0 / jnp.sum(p, axis=0, keepdims=True)
        linv_ref[0, pair, qb : qb + 1, :] = linv
        low = p.astype(bf16)
        p_ref[0, pair, qb, :rows, :] = low
        probs[unit] = (low, linv)

    def mix(unit):
        pair, qb = unit
        key0, rows = geometry(qb)
        low, linv = probs.pop(unit)
        o = dot_tn(v_ref[key0 : key0 + rows, pl.ds(at + pair * PAIR, PAIR)], low)
        o = jnp.where(top, o[:, :LANES] * linv[:, :LANES], o[:, LANES:] * linv[:, LANES:])
        o_ref[qb * LANES : (qb + 1) * LANES, pair * PAIR : (pair + 1) * PAIR] = o.T.astype(bf16)

    units = [(pair, qb) for qb in range(blocks) for pair in range(pairs)]
    pipelined(units, (score, soften, mix), (0, 2, 5))


def attend_back_kernel(
    pairs, blocks, q_ref, k_ref, v_ref, g_ref, o_ref, p_ref, linv_ref, low, normed, up, *refs
):
    dq_ref, dk_ref, dv_ref, glow_ref, grads, dk_sum, dv_sum, glow_sum = refs
    left, top = half_lanes(), half_rows()
    ones = jnp.ones((BAND * LANES, LANES), bf16)
    dk_sum[...] = jnp.zeros_like(dk_sum)
    dv_sum[...] = jnp.zeros_like(dv_sum)
    first, second = {}, {}

    def grad_probs(unit):
        pair, qb = unit
        cols = slice(pair * PAIR, (pair + 1) * PAIR)
        key0, rows = geometry(qb)
        here = slice(qb * LANES, (qb + 1) * LANES)
        linv = linv_ref[0, pair, qb : qb + 1, :]
        linv = jnp.where(top, linv[:, :LANES], linv[:, LANES:]).T
        g = g_ref[here, cols].astype(f32) * linv
        delta = split_heads(-(g * o_ref[here, cols].astype(f32)).astype(bf16), left)
        g = split_heads(g.astype(bf16), left)
        values = jnp.concatenate([v_ref[key0 : key0 + rows, cols], ones[:rows]], axis=1)
        first[unit] = (dot_nt(values, jnp.concatenate([g, delta], axis=1)), g)

    def grad_values(unit):
        pair, qb = unit
        cols = slice(pair * PAIR, (pair + 1) * PAIR)
        key0, rows = geometry(qb)
        dp, g = first.pop(unit)
        low = p_ref[0, pair, qb, :rows, :]
        second[unit] = low * dp.astype(bf16)
        dv_sum[key0 : key0 + rows, cols] += dot(low, g)

    def grad_queries_keys(unit):
        pair, qb = unit
        cols = slice(pair * PAIR, (pair + 1) * PAIR)
        key0, rows = geometry(qb)
        here = slice(qb * LANES, (qb + 1) * LANES)
        ds = second.pop(unit)
        dk_sum[key0 : key0 + rows, cols] += dot(ds, split_heads(q_ref[here, cols], left))
        dq = dot_tn(k_ref[key0 : key0 + rows, cols], ds)
        dq = jnp.where(top, dq[:, :LANES], dq[:, LANES:]) * 0.125
        dq_ref[here, cols] = dq.T.astype(bf16)

    units = [(pair, qb) for qb in range(blocks) for pair in range(pairs)]
    pipelined(units, (grad_probs, grad_values, grad_queries_keys), (0, 2, 4))
    dk_ref[...] = (dk_sum[...] * (0.125 / SCORE_SCALE)).astype(bf16)
    dv_ref[...] = dv_sum[...].astype(bf16)

    slot, step, last = pl.program_id(0), pl.program_id(1), pl.num_programs(1) - 1
    width = normed.shape[1]
    at = pl.multiple_of(step * pairs * PAIR, pairs * PAIR)
    here = pl.ds(at, pairs * PAIR)
    both = jnp.concatenate([dq_ref[...], dv_ref[...]], axis=1)
    part = dot_tn(low[...], both)
    part = jnp.concatenate([part[0:4, : pairs * PAIR], part[4:8, pairs * PAIR :]], axis=0) * 8.0
    grads[0:8, here] = jnp.where(slot == 0, part, grads[0:8, here] + part)
    glow = dot_nt(both, jnp.concatenate([up[:, here], up[:, pl.ds(width + at, pairs * PAIR)]], axis=1))
    glow_sum[...] = jnp.where(step == 0, glow, glow_sum[...] + glow)

    @pl.when(step == last)
    def _():
        glow = glow_sum[...].astype(bf16)
        glow_ref[...] = glow
        part = dot_tn(glow, normed[...])[0:8]
        grads[8:16, :] = jnp.where(slot == 0, part, grads[8:16, :] + part)


def attend_back(slots, q, k, v, g, o, p, linv, low, normed, up):
    tokens, width = q.shape
    seq = tokens // slots
    blocks, heads2, pairs = seq // LANES, width // PAIR, 2
    rows = BAND * LANES
    tile = pl.BlockSpec((seq, pairs * PAIR), lambda s, h: (s, h))
    thin = pl.BlockSpec((seq, LANES), lambda s, h: (s, 0))
    return pl.pallas_call(
        functools.partial(attend_back_kernel, pairs, blocks),
        grid=(slots, heads2 // pairs),
        in_specs=[tile] * 5
        + [
            pl.BlockSpec((1, pairs, blocks, rows, 2 * LANES), lambda s, h: (s, h, 0, 0, 0)),
            pl.BlockSpec((1, pairs, blocks, 2 * LANES), lambda s, h: (s, h, 0, 0)),
            thin,
            pl.BlockSpec((seq, width), lambda s, h: (s, 0)),
            resident(up),
        ],
        out_specs=[tile] * 3 + [thin, pl.BlockSpec((16, width), lambda s, h: (0, 0))],
        scratch_shapes=[pltpu.VMEM((seq, pairs * PAIR), f32)] * 2 + [pltpu.VMEM((seq, LANES), f32)],
        out_shape=[jax.ShapeDtypeStruct(q.shape, bf16)] * 3
        + [jax.ShapeDtypeStruct((tokens, LANES), bf16), jax.ShapeDtypeStruct((16, width), f32)],
        compiler_params=params(),
        cost_estimate=pl.CostEstimate(flops=14 * tokens * width * width // COST, bytes_accessed=2**20, transcendentals=0),
        name="attend_back",
    )(q, k, v, g, o, p, linv, low, normed, up)


def feed_chunk(wait, first, normed, cot, w, at, bias):
    width = cot.shape[1]
    wait(first)
    wait(first + 1)
    size = width // 4
    up, down = slice(at, at + width), slice(at + width, at + 2 * width)
    acts, grads = [], []
    for i in range(0, width, size):
        grad = dot_nt(cot, w[i : i + size, down])
        act, slope = gelu_and_slope(dot(normed, w[:, at + i : at + i + size]) + bias[:, i : i + size])
        acts.append(act.astype(bf16))
        grads.append((slope * grad).astype(bf16))
    return dot(jnp.concatenate(acts, axis=1), w[:, down]), dot_nt(jnp.concatenate(grads, axis=1), w[:, up])


def feed_first_kernel(wholes, wait, ins, outs, _):
    tok, att, cot, vec = ins
    h1_ref, normed_ref, o_ref, g_ref = outs
    width = tok.shape[1]
    wait(0)
    h1 = tok[...].astype(f32) + dot(att[...], wholes[0][:, 2 * width :]) + vec[4:5, :]
    h1_ref[...] = h1
    n, _ = normalise(h1)
    normed = (n * vec[7:8, :] + vec[1:2, :]).astype(bf16)
    normed_ref[...] = normed
    o_ref[...], g_ref[...] = feed_chunk(wait, 1, normed, cot[...], wholes[0], 0, vec[8:9, :])


def feed_last_kernel(wholes, wait, ins, outs, scratch):
    normed, cot, vec, h1, old_o, old_g = ins
    out_ref, gh_ref, ga_ref = outs
    x_ref, o_sum, g_sum, sems = scratch
    rows, width = cot.shape
    here = pl.ds(pl.multiple_of(pl.program_id(0) * rows, rows), rows)
    loads = [(old_o, o_sum), (old_g, g_sum), (h1, x_ref)]
    loads = [pltpu.make_async_copy(a.at[here], b, sems.at[i]) for i, (a, b) in enumerate(loads)]
    for load in loads:
        load.start()
    chunks = wholes[0].shape[1] // (2 * width)
    for j in range(chunks):
        bias = vec[9 + j : 10 + j, :]
        o, g = feed_chunk(wait, 2 * j, normed[...], cot[...], wholes[0], 2 * j * width, bias)
        if j == 0:
            for load in loads:
                load.wait()
        if j < chunks - 1:
            o_sum[...] += o
            g_sum[...] += g
    x = x_ref[...]
    out_ref[...] = (x + (o_sum[...] + o) + vec[5:6, :]).astype(bf16)
    n, r = normalise(x)
    grad = cot[...].astype(f32) + norm_back(n, r, (g_sum[...] + g) * vec[7:8, :])
    low = grad.astype(bf16)
    gh_ref[...] = low
    wait(2 * chunks)
    ga_ref[...] = dot_nt(low, wholes[1][...]).astype(bf16)


def feed_call(kernel, name, weights, order, fsdp, rowwise, vec, far, out_types):
    tokens, width = rowwise[0].shape
    rows = 512
    row = pl.BlockSpec((rows, width), lambda i: (i, 0))
    scratch = [pltpu.VMEM((rows, width), f32)] * len(far)
    return weight_call(
        kernel,
        name,
        weights,
        order,
        (tokens // rows,),
        rowwise + [vec] + far,
        [row] * len(rowwise) + [resident(vec)] + [pl.BlockSpec(memory_space=pltpu.HBM)] * len(far),
        [row] * len(out_types),
        [jax.ShapeDtypeStruct((tokens, width), t) for t in out_types],
        scratch + ([pltpu.SemaphoreType.DMA((len(far),))] if far else []),
        18 * tokens * width * width,
        fsdp,
    )


def feed_order(width, chunks):
    return [(0, (2 * j + 1 - i) * width, width) for j in range(chunks) for i in (0, 1)]


def feed_first(feeds, fsdp, tok, att, cot, vec):
    width = tok.shape[1]
    weights = [(feeds[0], (width, 3 * width))]
    order = [(0, 2 * width, width)] + feed_order(width, 1)
    types = [f32, bf16, f32, f32]
    return feed_call(feed_first_kernel, "feed_first", weights, order, fsdp, [tok, att, cot], vec, [], types)


def feed_last(feeds, fsdp, h1, normed, o, g, cot, vec):
    width = cot.shape[1]
    weights = [(feeds[1], (width, 6 * width)), (feeds[0], (width, width))]
    order = feed_order(width, 3) + [(1, 2 * width, width)]
    rowwise, far = [normed, cot], [h1, o, g]
    return feed_call(feed_last_kernel, "feed_last", weights, order, fsdp, rowwise, vec, far, [bf16] * 3)


def input_kernel(wholes, wait, ins, outs, _):
    dq, dk, dv, glow, down, vec, tok, gh = ins
    (out_ref,) = outs
    half = dq.shape[1] // 2
    g = dot_nt(glow[...], down[...])
    for i, w in enumerate(wholes):
        wait(i)
        cols = slice(i * half, (i + 1) * half)
        g = g + dot_nt(dq[:, cols], w[:, :half])
        g = g + dot_nt(dk[:, cols], w[:, half : 2 * half])
        g = g + dot_nt(dv[:, cols], w[:, 2 * half : 3 * half])
    n, r = normalise(tok[...].astype(f32))
    out_ref[...] = (gh[...].astype(f32) + norm_back(n, r, g * vec[6:7, :])).astype(bf16)


def input_grad(joint, fsdp, tok, gh, dq, dk, dv, glow, down, vec):
    tokens, width = tok.shape
    rows = 512
    row = pl.BlockSpec((rows, width), lambda i: (i, 0))
    thin = pl.BlockSpec((rows, LANES), lambda i: (i, 0))
    return weight_call(
        input_kernel,
        "input_grad",
        [(w, (width, 3 * width // 2)) for w in joint],
        [(0, 0, 3 * width // 2), (1, 0, 3 * width // 2)],
        (tokens // rows,),
        [dq, dk, dv, glow, down, vec, tok, gh],
        [row] * 3 + [thin, resident(down), resident(vec), row, row],
        [row],
        [jax.ShapeDtypeStruct((tokens, width), bf16)],
        [],
        6 * tokens * width * width,
        fsdp,
    )[0]


def per_device(
    tokens,
    document_length_list,
    joint_projection_weight,
    attention_out_weight,
    feed_up_weight,
    feed_down_weight,
    frozen_norm_gains,
    biases,
    hidden_up_bias,
    query_down_adapter,
    query_up_adapter,
    value_down_adapter,
    value_up_adapter,
    cotangent,
):
    micro, local, seq, width = tokens.shape
    slots = micro * local
    shards = width // joint_projection_weight.shape[0]
    hidden = feed_down_weight.shape[0]
    tok = tokens.reshape(slots * seq, width)
    cot = cotangent.reshape(slots * seq, width)
    lengths = document_length_list.reshape(slots, -1)

    dp = lax.axis_size("dp")
    chunks = 4
    part = hidden // chunks
    stepped = dp == 4 and shards == 8 and part == LANES and width == shards * LANES

    def gather(x):
        return lax.all_gather(x, "fsdp", axis=0, tiled=True)

    adapters = [query_down_adapter, query_up_adapter, value_down_adapter, value_up_adapter]
    if stepped:
        a, part_a = cut(joint_projection_weight, biases, frozen_norm_gains, hidden_up_bias, dp)
        link = Gather(dp, shards)
        near = link.step_1(part_a)
        shards_here = [joint_projection_weight, feed_up_weight, feed_down_weight, attention_out_weight]
        *shards_here, part_a = after_all(shards_here + [part_a], a)
        b, c, part_b, part_c, down_map, up_map = pack(*shards_here, adapters, chunks, shards, dp)
        b_near = link.step_1(part_b)
        near = after_all(near, part_c)
        a_far = link.all_far(near)
        b_far = link.all_far(b_near)
        c_near = link.step_1(after(part_c, b_near))
        joint = [pieces(a, link.swap(a), [a_far], [link.swap(a_far)])]
        vec = None
    else:
        small = jnp.concatenate([biases, frozen_norm_gains], axis=0)
        small = lax.all_gather(small, "fsdp", axis=1, tiled=True)
        hidden_bias = lax.all_gather(hidden_up_bias, "fsdp", axis=0, tiled=False)
        hidden_bias = [hidden_bias[:, j * part : (j + 1) * part].reshape(1, -1) for j in range(chunks)]
        vec = jnp.concatenate([small] + hidden_bias, axis=0)
        vec = jnp.pad(vec, ((0, 16 - 8 - chunks), (0, 0))).astype(f32)
        third = [width * i // 2 for i in range(6)]
        joint = []
        for i in (0, 1):
            cols = [lax.slice_in_dim(joint_projection_weight, t, t + width // 2, axis=1) for t in third[i::2]]
            joint.append([(gather(jnp.concatenate(cols, axis=1)), 0, 0, "whole")])
        up_parts = feed_up_weight.reshape(-1, shards, chunks, part)
        feeds = []
        for group in ((0,), tuple(range(1, chunks))):
            cols = []
            for j in group:
                cols.append(up_parts[:, :, j, :].reshape(-1, shards * part))
                cols.append(feed_down_weight[j * part : (j + 1) * part])
            if group[0] == 0:
                cols.append(attention_out_weight)
            feeds.append([(gather(jnp.concatenate(cols, axis=1)), 0, 0, "whole")])
        rank = query_down_adapter.shape[1]
        down_map = jnp.concatenate([query_down_adapter, value_down_adapter], axis=1)
        down_map = jnp.pad(down_map, ((0, 0), (0, LANES - 2 * rank)))
        zero = jnp.zeros_like(query_up_adapter)
        up_map = jnp.concatenate(
            [
                jnp.concatenate([query_up_adapter, zero], axis=1),
                jnp.concatenate([zero, value_up_adapter], axis=1),
            ],
            axis=0,
        )
        up_map = jnp.pad(up_map * 8, ((0, LANES - 2 * rank), (0, 0))).astype(bf16)

    q, k, v, low, normed, vec, *kept = heads(joint[0], shards, lengths, tok, down_map, up_map, vec)
    if stepped:
        b_far, *c_near, q = after_all([b_far] + c_near + [q], low)
        b_rest = [link.swap(b), [b_far], [link.swap(b_far)]]
        c_far = link.each_far(c_near)
        joint.append(pieces(b, *b_rest))
    old = [q, k, v] + kept
    q, k, v, att, probs, linv = heads(joint[1], shards, lengths, normed, down_map, up_map, vec, low, old)
    if stepped:
        feeds = [pieces(b, *b_rest, joint_projection_weight.shape[1] // 2, joint_projection_weight.shape[1] // 2)]
        c_other = [link.swap(c_far[0])]
        *c_other, att = after_all(c_other + [att], vec)
    h1, normed_2, o, g = feed_first(feeds, shards, tok, att, cot, vec)
    if stepped:
        *far, o = after_all(c_far[1:] + [o], h1)
        c_other += [link.swap(x) for x in far]
        feeds.append(pieces(c, link.swap(after(c, vec)), c_far[:1] + far, c_other))
    out, gh, ga = feed_last(feeds, shards, h1, normed_2, o, g, cot, vec)

    dq, dk, dv, glow, grads = attend_back(slots, q, k, v, ga, att, probs, linv, low, normed, up_map)
    if stepped:
        total = Gather(dp, shards)
        grads = grads + total.move(grads, lambda d, f: (d, f ^ 1))
        _, a, b, c = total.each_far([grads])
        grads = (grads + a) + (b + c)
        a, b, c = [total.move(grads, lambda d, f, k=k: (d, (f + 2 * k) % shards)) for k in (1, 2, 3)]
        dq = after(dq, grads)
        grad_in = input_grad(joint, shards, tok, gh, dq, dk, dv, glow, down_map, vec)
        a, b, c = after_all([a, b, c], grad_in)
        grads = (grads + b) + (a + c)
    else:
        grads = jnp.sum(lax.all_gather(grads, ("dp", "fsdp"), axis=0, tiled=False), axis=0)
        grad_in = input_grad(joint, shards, tok, gh, dq, dk, dv, glow, down_map, vec)
    return (
        out.reshape(tokens.shape),
        grad_in.reshape(tokens.shape),
        grads[8:12].T,
        grads[0:4],
        grads[12:16].T,
        grads[4:8],
    )


def solution(mesh):
    slots = P(None, ("dp", "fsdp"), None, None)
    return jax.shard_map(
        per_device,
        mesh=mesh,
        in_specs=(
            slots,
            P(None, ("dp", "fsdp"), None),
            P("fsdp", None),
            P("fsdp", None),
            P("fsdp", None),
            P("fsdp", None),
            P(None, "fsdp"),
            P(None, "fsdp"),
            P("fsdp"),
            P(),
            P(),
            P(),
            P(),
            slots,
        ),
        out_specs=(slots, slots, P(), P(), P(), P()),
        check_vma=False,
    )
```

```python
import functools
import math

import jax
import jax.numpy as jnp
from jax import lax
from jax.experimental import pallas as pl
from jax.experimental.pallas import tpu as pltpu
from jax.sharding import PartitionSpec as P

f32 = jnp.float32
bf16 = jnp.bfloat16
LANES = 128
PAIR = 128
BAND = 3
EPS = 1e-5
MASKED = -1e30
SCORE_SCALE = 0.125 * math.log2(math.e)
GELU_C = math.sqrt(2.0 / math.pi)
VMEM_LIMIT = 58 * 2**20
COST = 8
NT = (((1,), (1,)), ((), ()))
TN = (((0,), (0,)), ((), ()))


def dot(a, b):
    return jnp.dot(a, b, preferred_element_type=f32)


def dot_nt(a, b):
    return lax.dot_general(a, b, NT, preferred_element_type=f32)


def dot_tn(a, b):
    return lax.dot_general(a, b, TN, preferred_element_type=f32)


def params():
    return pltpu.CompilerParams(vmem_limit_bytes=VMEM_LIMIT)


def resident(array):
    zeros = (0,) * array.ndim
    return pl.BlockSpec(array.shape, lambda *_: zeros, pipeline_mode=pl.Buffered(1))


def normalise(x):
    centred = x - jnp.mean(x, axis=-1, keepdims=True)
    r = lax.rsqrt(jnp.mean(centred * centred, axis=-1, keepdims=True) + EPS)
    return centred * r, r


def norm_back(n, r, w):
    return r * (w - jnp.mean(w, axis=-1, keepdims=True) - n * jnp.mean(w * n, axis=-1, keepdims=True))


def gelu_and_slope(x):
    x2 = x * x
    t = jnp.tanh(x * (GELU_C + (GELU_C * 0.044715) * x2))
    half = 0.5 + 0.5 * t
    act = x * half
    slope = half + (act * (1.0 - half)) * (2 * GELU_C + (6 * GELU_C * 0.044715) * x2)
    return act, slope


def ring_pairs(dp, fsdp, move):
    pairs = []
    for d in range(dp):
        for f in range(fsdp):
            e, g = move(d, f)
            pairs.append((d * fsdp + f, e * fsdp + g))
    return pairs


def after(x, others):
    return lax.optimization_barrier((x, others))[0]


def after_all(xs, others):
    return lax.optimization_barrier((xs, others))[0]


class Gather:
    def __init__(self, dp, fsdp):
        self.dp, self.fsdp = dp, fsdp

    def move(self, x, where):
        return lax.ppermute(x, ("dp", "fsdp"), ring_pairs(self.dp, self.fsdp, where))

    def step_1(self, mine):
        fsdp = self.fsdp
        return [self.move(mine, lambda d, f, k=k: (d, (f + 2 * k) % fsdp)) for k in range(1, fsdp // 2)]

    def all_far(self, near):
        near = [jnp.broadcast_to(x[None], (self.dp,) + x.shape) for x in near]
        return lax.all_to_all(jnp.concatenate(near, axis=1), "dp", 0, 0, tiled=False)

    def each_far(self, near):
        near = stack(near) if len(near) > 1 else near[0]
        return [near] + [self.move(near, lambda d, f, e=e: (d ^ e, f)) for e in range(1, self.dp)]

    def swap(self, x):
        return self.move(x, lambda d, f: (d, f ^ 1))


def pieces(shard, other_shard, far, other_far, shard_column=0, far_column=0):
    made = [(shard, shard_column, 0, "shard"), (other_shard, shard_column, 1, "shard")]
    for swapped, arrays in ((0, far), (1, other_far)):
        if len(arrays) == 1:
            made.append((arrays[0], far_column, swapped, "all"))
        else:
            made += [(x, far_column, swapped, e) for e, x in enumerate(arrays)]
    return made


def copies(weight, refs, whole, sems, place, cols, base, dp, fsdp):
    made = []
    start, size = cols
    rows = whole.shape[0] // fsdp
    part = rows // dp
    index = place[1]

    def add(source, first, at, rows):
        target = whole.at[pl.ds(at, rows), pl.ds(start - base, size)]
        made.append(pltpu.make_async_copy(source.at[:, pl.ds(first + start, size)], target, sems.at[len(made)]))

    for (_, column, swapped, what), ref in zip(weight, refs):
        other = swapped * (1 - 2 * lax.rem(index, 2))
        if what == "whole":
            add(ref, column, 0, whole.shape[0])
        elif what == "shard":
            add(ref, column, pl.multiple_of((index + other) * rows, rows), rows)
        else:
            for e in range(dp) if what == "all" else [what]:
                quarter = e if what == "all" else jnp.bitwise_xor(place[0], e)
                for k in range(1, fsdp // 2):
                    owner = lax.rem(index + fsdp - 2 * k, fsdp) + other
                    at = pl.multiple_of(owner * rows + quarter * part, part)
                    here = pl.ds((k - 1) * part, part)
                    add(ref.at[e, here] if what == "all" else ref.at[here], column, at, part)
    return made


def copy_count(weight, dp, fsdp):
    count = 0
    for _, _, _, what in weight:
        count += 1 if what in ("whole", "shard") else (fsdp // 2 - 1) * (dp if what == "all" else 1)
    return count


def weight_call(kernel, name, weights, order, grid, blocked, in_specs, out_specs, out_shape, scratch, cost, fsdp, old=()):
    dp = lax.axis_size("dp")
    arrays = [[piece[0] for piece in w] for w, _ in weights]
    flat = [a for some in arrays for a in some]
    counts = [copy_count(weights[i][0], dp, fsdp) for i, _, _ in order]

    def body(*refs):
        refs = list(refs)
        place = [lax.axis_index("dp"), lax.axis_index("fsdp")]
        take = lambda n: [refs.pop(0) for _ in range(n)]
        sources = [take(len(some)) for some in arrays]
        ins, _, outs = take(len(blocked)), take(len(old)), take(len(out_shape))
        wholes, sems = take(len(weights)), take(len(order))

        first_step = pl.program_id(0) == 0
        for axis in range(1, len(grid)):
            first_step = first_step & (pl.program_id(axis) == 0)

        def group(n):
            i, start, size = order[n]
            base = start if wholes[i].shape[1] == size else 0
            return copies(weights[i][0], sources[i], wholes[i], sems[n], place, (start, size), base, dp, fsdp)

        @pl.when(first_step)
        def _():
            for n in range(len(order)):
                for copy in group(n):
                    copy.start()

        def wait(n):
            @pl.when(first_step)
            def _():
                for copy in group(n):
                    copy.wait()

        kernel(wholes, wait, ins, outs, refs)

    return pl.pallas_call(
        body,
        grid=grid,
        in_specs=[pl.BlockSpec(memory_space=pltpu.HBM)] * len(flat)
        + in_specs
        + [pl.BlockSpec(memory_space=pl.ANY)] * len(old),
        out_specs=out_specs,
        scratch_shapes=[pltpu.VMEM(shape, bf16) for _, shape in weights]
        + [pltpu.SemaphoreType.DMA((n,)) for n in counts]
        + scratch,
        out_shape=out_shape,
        compiler_params=params(),
        cost_estimate=pl.CostEstimate(flops=cost // COST, bytes_accessed=2**20, transcendentals=0),
        input_output_aliases={len(flat) + len(blocked) + i: i for i in range(len(old))},
        name=name,
    )(*flat, *blocked, *old)


def own_quarter(rows):
    return pl.ds(pl.multiple_of(lax.axis_index("dp") * rows, rows), rows)


def stack_rows(arrays, rows):
    arrays = [a.astype(f32) for a in arrays]
    used = sum(a.shape[0] for a in arrays)
    return jnp.concatenate(arrays + [jnp.zeros((rows - used, arrays[0].shape[1]), f32)], axis=0).astype(bf16)


def stack_kernel(*refs):
    rows = refs[0].shape[0]
    for i, ref in enumerate(refs[:-1]):
        refs[-1][i * rows : (i + 1) * rows, :] = ref[...]


def stack(arrays):
    rows, columns = arrays[0].shape
    return local_call(stack_kernel, "stack", [(rows * len(arrays), columns)], arrays)[0]


def cut_kernel(joint, biases, gains, hidden, first, part):
    half = joint.shape[1] // 6
    for i in range(3):
        first[:, i * half : (i + 1) * half] = joint[:, 2 * i * half : (2 * i + 1) * half]
    small = [biases[...], gains[...], hidden[...].astype(f32).reshape(-1, LANES)]
    first[:, 3 * half :] = stack_rows(small, first.shape[0])
    part[...] = first[own_quarter(part.shape[0]), :]


def local_call(kernel, name, shapes, arrays):
    return pl.pallas_call(
        kernel,
        out_shape=[jax.ShapeDtypeStruct(s, bf16) for s in shapes],
        compiler_params=params(),
        name=name,
    )(*arrays)


def cut(joint, biases, gains, hidden, dp):
    rows, width = joint.shape
    columns = width // 2 + LANES
    return local_call(cut_kernel, "cut", [(rows, columns), (rows // dp, columns)], [joint, biases, gains, hidden])


def pack_kernel(chunks, shards, joint, up, down, wo, q_down, q_up, v_down, v_up, *refs):
    outs, parts = refs[:2], refs[2:4]
    down_map, up_map = refs[4:]
    hidden, width = down.shape
    part = hidden // chunks
    half = joint.shape[1] // 6
    for i in range(3):
        outs[0][:, i * half : (i + 1) * half] = joint[:, (2 * i + 1) * half : (2 * i + 2) * half]
    for j in range(chunks):
        out, at = (outs[1], (j - 1) * 2 * width) if j else (outs[0], 3 * half)
        for s in range(shards):
            start = s * hidden + j * part
            out[:, at + s * part : at + (s + 1) * part] = up[:, start : start + part]
        out[:, at + width : at + 2 * width] = down[j * part : (j + 1) * part, :]
    outs[0][:, 3 * half + 2 * width :] = wo[...]
    for out, part_ref in zip(outs, parts):
        part_ref[...] = out[own_quarter(part_ref.shape[0]), :]
    rank = q_up.shape[0]
    down_map[...] = jnp.zeros_like(down_map)
    down_map[:, :rank] = q_down[...]
    down_map[:, rank : 2 * rank] = v_down[...]
    zero = jnp.zeros(q_up.shape, f32)
    rows = [jnp.concatenate([q_up[...].astype(f32) * 8.0, zero], axis=1)]
    rows += [jnp.concatenate([zero, v_up[...].astype(f32) * 8.0], axis=1)]
    up_map[...] = stack_rows(rows, up_map.shape[0])


def pack(joint, up, down, wo, adapters, chunks, shards, dp):
    rows, width = up.shape[0], down.shape[1]
    shapes = [(rows, joint.shape[1] // 2 + 3 * width), (rows, 2 * (chunks - 1) * width)]
    shapes += [(r // dp, c) for r, c in shapes]
    shapes += [(width, LANES), (LANES, 2 * width)]
    return local_call(functools.partial(pack_kernel, chunks, shards), "pack", shapes, [joint, up, down, wo, *adapters])


def project_slot(first, carried, shards, w, wait, ins, outs, load):
    rows_in, down, up = ins[:3]
    q_ref, k_ref, v_ref = outs[:3]
    half = q_ref.shape[1]
    width = 2 * half
    cols = slice(0, half) if first else slice(half, width)
    wait(0)
    if first:
        low_ref, normed_ref, vec = outs[3:6]

        @pl.when(pl.program_id(0) == 0)
        def _():
            if carried:
                rows = w.shape[0] // shards
                parts = [w[s * rows : s * rows + vec.shape[0], 3 * half :] for s in range(shards)]
                vec[...] = jnp.concatenate(parts, axis=1).astype(f32)
            else:
                vec[...] = ins[3][...]
    else:
        low_in, vec = ins[3:]
    load.wait()
    sub = 256
    state = {}

    def norm(r):
        rr = slice(r, r + sub)
        if first:
            n, _ = normalise(rows_in[rr, :].astype(f32))
            normed = (n * vec[6:7, :] + vec[0:1, :]).astype(bf16)
            normed_ref[rr, :] = normed
        else:
            normed = rows_in[rr, :]
        state[r] = normed

    def mix(r):
        rr = slice(r, r + sub)
        normed = state.pop(r)
        k_ref[rr, :] = dot(normed, w[:, half : 2 * half]).astype(bf16)
        if first:
            low = dot(normed, down[...]).astype(bf16)
            low_ref[rr, :] = low
        else:
            low = low_in[rr, :]
        q = dot(normed, w[:, :half]) + dot(low, up[:, cols]) + vec[2:3, cols]
        q_ref[rr, :] = (q * SCORE_SCALE).astype(bf16)
        v = dot(normed, w[:, 2 * half : 3 * half]) + dot(low, up[:, width:][:, cols]) + vec[3:4, cols]
        v_ref[rr, :] = v.astype(bf16)

    pipelined(list(range(0, rows_in.shape[0], sub)), (norm, mix), (0, 1))


def heads_kernel(first, carried, shards, pairs, wholes, wait, ins, outs, scratch):
    lengths, x_hbm, ins = ins[0], ins[1], ins[2:]
    mask, x_ref, q_ref, k_ref, v_ref, *normed_ref, sems = scratch
    o_ref, p_ref, linv_ref = outs[-3:]
    seq, half = q_ref.shape
    blocks = seq // LANES
    slot, step = pl.program_id(0), pl.program_id(1)

    def rows(s):
        return pl.ds(pl.multiple_of(s * seq, seq), seq)

    def load(s):
        return pltpu.make_async_copy(x_hbm.at[rows(s)], x_ref, sems.at[0])

    cols = pl.ds(0 if first else half, half)
    stores = [(ref, out.at[rows(slot), cols]) for ref, out in zip((q_ref, k_ref, v_ref), outs)]
    if first:
        stores.append((normed_ref[0], outs[4].at[rows(slot)]))
    stores = [pltpu.make_async_copy(a, b, sems.at[1 + i]) for i, (a, b) in enumerate(stores)]

    @pl.when((slot == 0) & (step == 0))
    def _():
        load(0).start()

    @pl.when(step == 0)
    def _():
        own = [q_ref, k_ref, v_ref] + ([outs[3], normed_ref[0], outs[5]] if first else [])
        project_slot(first, carried, shards, wholes[0], wait, [x_ref] + list(ins), own, load(slot))
        for store in stores:
            store.start()
        fill_masks(lengths, slot, mask, blocks)

    @pl.when((step == 1) & (slot + 1 < pl.num_programs(0)))
    def _():
        load(slot + 1).start()

    @pl.when(step != 0)
    def _():
        at = pl.multiple_of((step - 1) * pairs * PAIR, pairs * PAIR)
        attend_pairs(pairs, blocks, at, q_ref, k_ref, v_ref, o_ref, p_ref, linv_ref, mask)

    @pl.when(step == pl.num_programs(1) - 1)
    def _():
        for store in stores:
            store.wait()


def heads(weight, fsdp, lengths, x, down, up, vec=None, low=None, old=()):
    tokens, width = x.shape
    slots = lengths.shape[0]
    seq = tokens // slots
    blocks, heads2, pairs = seq // LANES, width // PAIR, 2
    steps = heads2 // pairs // 2
    first = low is None
    here = 0 if first else 1
    far = pl.BlockSpec(memory_space=pltpu.HBM)
    thin = pl.BlockSpec((seq, LANES), lambda s, j: (s, 0))
    group = lambda j: here * steps + jnp.maximum(j - 1, 0)
    tile = pl.BlockSpec((seq, pairs * PAIR), lambda s, j: (s, group(j)))
    probs = (pairs, blocks, BAND * LANES, 2 * LANES)
    sums = (pairs, blocks, 2 * LANES)
    ins = [lengths, x, down, up]
    in_specs = [pl.BlockSpec(memory_space=pltpu.SMEM), far, resident(down), resident(up)]
    outs, out_specs = [jax.ShapeDtypeStruct((tokens, width), bf16)] * 3, [far] * 3
    if first:
        outs = outs + [jax.ShapeDtypeStruct((tokens, n), bf16) for n in (LANES, width)]
        outs = outs + [jax.ShapeDtypeStruct((16, width), f32)]
        out_specs = out_specs + [thin, far, pl.BlockSpec((16, width), lambda s, j: (0, 0))]
    else:
        ins, in_specs = ins + [low], in_specs + [thin]
    if vec is not None:
        ins, in_specs = ins + [vec], in_specs + [resident(vec)]
    outs = outs + [
        jax.ShapeDtypeStruct((tokens, width), bf16),
        jax.ShapeDtypeStruct((slots, heads2) + probs[1:], bf16),
        jax.ShapeDtypeStruct((slots, heads2) + sums[1:], f32),
    ]
    out_specs = out_specs + [
        tile,
        pl.BlockSpec((1,) + probs, lambda s, j: (s, group(j), 0, 0, 0)),
        pl.BlockSpec((1,) + sums, lambda s, j: (s, group(j), 0, 0)),
    ]
    carried = first and vec is None
    columns = 3 * width // 2 + (LANES if carried else 0)
    return weight_call(
        functools.partial(heads_kernel, first, carried, fsdp, pairs),
        "heads",
        [(weight, (width, columns))],
        [(0, 0, columns)],
        (slots, 1 + steps),
        ins,
        in_specs,
        out_specs,
        outs,
        [pltpu.VMEM((blocks, BAND * LANES, LANES), f32), pltpu.VMEM((seq, width), bf16)]
        + [pltpu.VMEM((seq, width // 2), bf16)] * 3
        + [pltpu.VMEM((seq, width), bf16)] * first
        + [pltpu.SemaphoreType.DMA((5,))],
        9 * tokens * width * width,
        fsdp,
        old,
    )


def fill_masks(lengths, slot, mask, blocks):
    starts = []
    total = jnp.int32(0)
    for d in range(lengths.shape[1]):
        starts.append(total)
        total = total + lengths[slot, d]
    for qb in range(blocks):
        first = max(0, qb - BAND + 1)
        rows = (qb - first + 1) * LANES
        query = qb * LANES + lax.broadcasted_iota(jnp.int32, (8, LANES), 1)
        begin = jnp.zeros((8, LANES), jnp.int32)
        for start in starts:
            begin = jnp.where(query >= start, start, begin)
        key = first * LANES + lax.broadcasted_iota(jnp.int32, (rows, LANES), 0)
        ok = (key >= begin[0:1]) & (key <= query[0:1])
        mask[qb, :rows, :] = jnp.where(ok, 0.0, MASKED)


def half_lanes():
    return lax.broadcasted_iota(jnp.int32, (LANES, LANES), 1) < 64


def half_rows():
    return lax.broadcasted_iota(jnp.int32, (LANES, LANES), 0) < 64


def split_heads(x, left):
    zero = jnp.zeros_like(x)
    return jnp.concatenate([jnp.where(left, x, zero), jnp.where(left, zero, x)], axis=0)


def pipelined(units, stages, lags):
    for t in range(len(units) + lags[-1]):
        for stage, lag in zip(stages, lags):
            if 0 <= t - lag < len(units):
                stage(units[t - lag])


def geometry(qb):
    first = max(0, qb - BAND + 1)
    return first * LANES, (qb - first + 1) * LANES


def attend_pairs(pairs, blocks, at, q_ref, k_ref, v_ref, o_ref, p_ref, linv_ref, mask):
    left, top = half_lanes(), half_rows()
    scores, probs = {}, {}

    def score(unit):
        pair, qb = unit
        cols = pl.ds(at + pair * PAIR, PAIR)
        key0, rows = geometry(qb)
        q = split_heads(q_ref[qb * LANES : (qb + 1) * LANES, cols], left)
        scores[unit] = dot_nt(k_ref[key0 : key0 + rows, cols], q)

    def soften(unit):
        pair, qb = unit
        key0, rows = geometry(qb)
        bias = mask[qb, :rows, :]
        s = scores.pop(unit) + jnp.concatenate([bias, bias], axis=1)
        p = jnp.exp2(s - jnp.max(s, axis=0, keepdims=True))
        linv = 1.0 / jnp.sum(p, axis=0, keepdims=True)
        linv_ref[0, pair, qb : qb + 1, :] = linv
        low = p.astype(bf16)
        p_ref[0, pair, qb, :rows, :] = low
        probs[unit] = (low, linv)

    def mix(unit):
        pair, qb = unit
        key0, rows = geometry(qb)
        low, linv = probs.pop(unit)
        o = dot_tn(v_ref[key0 : key0 + rows, pl.ds(at + pair * PAIR, PAIR)], low)
        o = jnp.where(top, o[:, :LANES] * linv[:, :LANES], o[:, LANES:] * linv[:, LANES:])
        o_ref[qb * LANES : (qb + 1) * LANES, pair * PAIR : (pair + 1) * PAIR] = o.T.astype(bf16)

    units = [(pair, qb) for qb in range(blocks) for pair in range(pairs)]
    pipelined(units, (score, soften, mix), (0, 2, 5))


def attend_back_kernel(
    pairs, blocks, q_ref, k_ref, v_ref, g_ref, o_ref, p_ref, linv_ref, low, normed, up, *refs
):
    dq_ref, dk_ref, dv_ref, glow_ref, grads, dk_sum, dv_sum, glow_sum = refs
    left, top = half_lanes(), half_rows()
    ones = jnp.ones((BAND * LANES, LANES), bf16)
    dk_sum[...] = jnp.zeros_like(dk_sum)
    dv_sum[...] = jnp.zeros_like(dv_sum)
    first, second = {}, {}

    def grad_probs(unit):
        pair, qb = unit
        cols = slice(pair * PAIR, (pair + 1) * PAIR)
        key0, rows = geometry(qb)
        here = slice(qb * LANES, (qb + 1) * LANES)
        linv = linv_ref[0, pair, qb : qb + 1, :]
        linv = jnp.where(top, linv[:, :LANES], linv[:, LANES:]).T
        g = g_ref[here, cols].astype(f32) * linv
        delta = split_heads(-(g * o_ref[here, cols].astype(f32)).astype(bf16), left)
        g = split_heads(g.astype(bf16), left)
        values = jnp.concatenate([v_ref[key0 : key0 + rows, cols], ones[:rows]], axis=1)
        first[unit] = (dot_nt(values, jnp.concatenate([g, delta], axis=1)), g)

    def grad_values(unit):
        pair, qb = unit
        cols = slice(pair * PAIR, (pair + 1) * PAIR)
        key0, rows = geometry(qb)
        dp, g = first.pop(unit)
        low = p_ref[0, pair, qb, :rows, :]
        second[unit] = low * dp.astype(bf16)
        dv_sum[key0 : key0 + rows, cols] += dot(low, g)

    def grad_queries_keys(unit):
        pair, qb = unit
        cols = slice(pair * PAIR, (pair + 1) * PAIR)
        key0, rows = geometry(qb)
        here = slice(qb * LANES, (qb + 1) * LANES)
        ds = second.pop(unit)
        dk_sum[key0 : key0 + rows, cols] += dot(ds, split_heads(q_ref[here, cols], left))
        dq = dot_tn(k_ref[key0 : key0 + rows, cols], ds)
        dq = jnp.where(top, dq[:, :LANES], dq[:, LANES:]) * 0.125
        dq_ref[here, cols] = dq.T.astype(bf16)

    units = [(pair, qb) for qb in range(blocks) for pair in range(pairs)]
    pipelined(units, (grad_probs, grad_values, grad_queries_keys), (0, 2, 4))
    dk_ref[...] = (dk_sum[...] * (0.125 / SCORE_SCALE)).astype(bf16)
    dv_ref[...] = dv_sum[...].astype(bf16)

    slot, step, last = pl.program_id(0), pl.program_id(1), pl.num_programs(1) - 1
    width = normed.shape[1]
    at = pl.multiple_of(step * pairs * PAIR, pairs * PAIR)
    here = pl.ds(at, pairs * PAIR)
    both = jnp.concatenate([dq_ref[...], dv_ref[...]], axis=1)
    part = dot_tn(low[...], both)
    part = jnp.concatenate([part[0:4, : pairs * PAIR], part[4:8, pairs * PAIR :]], axis=0) * 8.0
    grads[0:8, here] = jnp.where(slot == 0, part, grads[0:8, here] + part)
    glow = dot_nt(both, jnp.concatenate([up[:, here], up[:, pl.ds(width + at, pairs * PAIR)]], axis=1))
    glow_sum[...] = jnp.where(step == 0, glow, glow_sum[...] + glow)

    @pl.when(step == last)
    def _():
        glow = glow_sum[...].astype(bf16)
        glow_ref[...] = glow
        part = dot_tn(glow, normed[...])[0:8]
        grads[8:16, :] = jnp.where(slot == 0, part, grads[8:16, :] + part)


def attend_back(slots, q, k, v, g, o, p, linv, low, normed, up):
    tokens, width = q.shape
    seq = tokens // slots
    blocks, heads2, pairs = seq // LANES, width // PAIR, 2
    rows = BAND * LANES
    tile = pl.BlockSpec((seq, pairs * PAIR), lambda s, h: (s, h))
    thin = pl.BlockSpec((seq, LANES), lambda s, h: (s, 0))
    return pl.pallas_call(
        functools.partial(attend_back_kernel, pairs, blocks),
        grid=(slots, heads2 // pairs),
        in_specs=[tile] * 5
        + [
            pl.BlockSpec((1, pairs, blocks, rows, 2 * LANES), lambda s, h: (s, h, 0, 0, 0)),
            pl.BlockSpec((1, pairs, blocks, 2 * LANES), lambda s, h: (s, h, 0, 0)),
            thin,
            pl.BlockSpec((seq, width), lambda s, h: (s, 0)),
            resident(up),
        ],
        out_specs=[tile] * 3 + [thin, pl.BlockSpec((16, width), lambda s, h: (0, 0))],
        scratch_shapes=[pltpu.VMEM((seq, pairs * PAIR), f32)] * 2 + [pltpu.VMEM((seq, LANES), f32)],
        out_shape=[jax.ShapeDtypeStruct(q.shape, bf16)] * 3
        + [jax.ShapeDtypeStruct((tokens, LANES), bf16), jax.ShapeDtypeStruct((16, width), f32)],
        compiler_params=params(),
        cost_estimate=pl.CostEstimate(flops=14 * tokens * width * width // COST, bytes_accessed=2**20, transcendentals=0),
        name="attend_back",
    )(q, k, v, g, o, p, linv, low, normed, up)


def feed_chunk(wait, first, normed, cot, w, at, bias):
    width = cot.shape[1]
    wait(first)
    wait(first + 1)
    size = width // 4
    up, down = slice(at, at + width), slice(at + width, at + 2 * width)
    acts, grads = [], []
    for i in range(0, width, size):
        grad = dot_nt(cot, w[i : i + size, down])
        act, slope = gelu_and_slope(dot(normed, w[:, at + i : at + i + size]) + bias[:, i : i + size])
        acts.append(act.astype(bf16))
        grads.append((slope * grad).astype(bf16))
    return dot(jnp.concatenate(acts, axis=1), w[:, down]), dot_nt(jnp.concatenate(grads, axis=1), w[:, up])


def feed_first_kernel(wholes, wait, ins, outs, _):
    tok, att, cot, vec = ins
    h1_ref, normed_ref, o_ref, g_ref = outs
    width = tok.shape[1]
    wait(0)
    h1 = tok[...].astype(f32) + dot(att[...], wholes[0][:, 2 * width :]) + vec[4:5, :]
    h1_ref[...] = h1
    n, _ = normalise(h1)
    normed = (n * vec[7:8, :] + vec[1:2, :]).astype(bf16)
    normed_ref[...] = normed
    o_ref[...], g_ref[...] = feed_chunk(wait, 1, normed, cot[...], wholes[0], 0, vec[8:9, :])


def feed_last_kernel(wholes, wait, ins, outs, scratch):
    normed, cot, vec, h1, old_o, old_g = ins
    out_ref, gh_ref, ga_ref = outs
    x_ref, o_sum, g_sum, sems = scratch
    rows, width = cot.shape
    here = pl.ds(pl.multiple_of(pl.program_id(0) * rows, rows), rows)
    loads = [(old_o, o_sum), (old_g, g_sum), (h1, x_ref)]
    loads = [pltpu.make_async_copy(a.at[here], b, sems.at[i]) for i, (a, b) in enumerate(loads)]
    for load in loads:
        load.start()
    chunks = wholes[0].shape[1] // (2 * width)
    for j in range(chunks):
        bias = vec[9 + j : 10 + j, :]
        o, g = feed_chunk(wait, 2 * j, normed[...], cot[...], wholes[0], 2 * j * width, bias)
        if j == 0:
            for load in loads:
                load.wait()
        if j < chunks - 1:
            o_sum[...] += o
            g_sum[...] += g
    x = x_ref[...]
    out_ref[...] = (x + (o_sum[...] + o) + vec[5:6, :]).astype(bf16)
    n, r = normalise(x)
    grad = cot[...].astype(f32) + norm_back(n, r, (g_sum[...] + g) * vec[7:8, :])
    low = grad.astype(bf16)
    gh_ref[...] = low
    wait(2 * chunks)
    ga_ref[...] = dot_nt(low, wholes[1][...]).astype(bf16)


def feed_call(kernel, name, weights, order, fsdp, rowwise, vec, far, out_types):
    tokens, width = rowwise[0].shape
    rows = 512
    row = pl.BlockSpec((rows, width), lambda i: (i, 0))
    scratch = [pltpu.VMEM((rows, width), f32)] * len(far)
    return weight_call(
        kernel,
        name,
        weights,
        order,
        (tokens // rows,),
        rowwise + [vec] + far,
        [row] * len(rowwise) + [resident(vec)] + [pl.BlockSpec(memory_space=pltpu.HBM)] * len(far),
        [row] * len(out_types),
        [jax.ShapeDtypeStruct((tokens, width), t) for t in out_types],
        scratch + ([pltpu.SemaphoreType.DMA((len(far),))] if far else []),
        18 * tokens * width * width,
        fsdp,
    )


def feed_order(width, chunks):
    return [(0, (2 * j + 1 - i) * width, width) for j in range(chunks) for i in (0, 1)]


def feed_first(feeds, fsdp, tok, att, cot, vec):
    width = tok.shape[1]
    weights = [(feeds[0], (width, 3 * width))]
    order = [(0, 2 * width, width)] + feed_order(width, 1)
    types = [f32, bf16, f32, f32]
    return feed_call(feed_first_kernel, "feed_first", weights, order, fsdp, [tok, att, cot], vec, [], types)


def feed_last(feeds, fsdp, h1, normed, o, g, cot, vec):
    width = cot.shape[1]
    weights = [(feeds[1], (width, 6 * width)), (feeds[0], (width, width))]
    order = feed_order(width, 3) + [(1, 2 * width, width)]
    rowwise, far = [normed, cot], [h1, o, g]
    return feed_call(feed_last_kernel, "feed_last", weights, order, fsdp, rowwise, vec, far, [bf16] * 3)


def input_kernel(wholes, wait, ins, outs, _):
    dq, dk, dv, glow, down, vec, tok, gh = ins
    (out_ref,) = outs
    half = dq.shape[1] // 2
    g = dot_nt(glow[...], down[...])
    for i, w in enumerate(wholes):
        wait(i)
        cols = slice(i * half, (i + 1) * half)
        g = g + dot_nt(dq[:, cols], w[:, :half])
        g = g + dot_nt(dk[:, cols], w[:, half : 2 * half])
        g = g + dot_nt(dv[:, cols], w[:, 2 * half : 3 * half])
    n, r = normalise(tok[...].astype(f32))
    out_ref[...] = (gh[...].astype(f32) + norm_back(n, r, g * vec[6:7, :])).astype(bf16)


def input_grad(joint, fsdp, tok, gh, dq, dk, dv, glow, down, vec):
    tokens, width = tok.shape
    rows = 512
    row = pl.BlockSpec((rows, width), lambda i: (i, 0))
    thin = pl.BlockSpec((rows, LANES), lambda i: (i, 0))
    return weight_call(
        input_kernel,
        "input_grad",
        [(w, (width, 3 * width // 2)) for w in joint],
        [(0, 0, 3 * width // 2), (1, 0, 3 * width // 2)],
        (tokens // rows,),
        [dq, dk, dv, glow, down, vec, tok, gh],
        [row] * 3 + [thin, resident(down), resident(vec), row, row],
        [row],
        [jax.ShapeDtypeStruct((tokens, width), bf16)],
        [],
        6 * tokens * width * width,
        fsdp,
    )[0]


def per_device(
    tokens,
    document_length_list,
    joint_projection_weight,
    attention_out_weight,
    feed_up_weight,
    feed_down_weight,
    frozen_norm_gains,
    biases,
    hidden_up_bias,
    query_down_adapter,
    query_up_adapter,
    value_down_adapter,
    value_up_adapter,
    cotangent,
):
    micro, local, seq, width = tokens.shape
    slots = micro * local
    shards = width // joint_projection_weight.shape[0]
    hidden = feed_down_weight.shape[0]
    tok = tokens.reshape(slots * seq, width)
    cot = cotangent.reshape(slots * seq, width)
    lengths = document_length_list.reshape(slots, -1)

    dp = lax.axis_size("dp")
    chunks = 4
    part = hidden // chunks
    stepped = dp == 4 and shards == 8 and part == LANES and width == shards * LANES

    def gather(x):
        return lax.all_gather(x, "fsdp", axis=0, tiled=True)

    adapters = [query_down_adapter, query_up_adapter, value_down_adapter, value_up_adapter]
    if stepped:
        a, part_a = cut(joint_projection_weight, biases, frozen_norm_gains, hidden_up_bias, dp)
        link = Gather(dp, shards)
        near = link.step_1(part_a)
        shards_here = [joint_projection_weight, feed_up_weight, feed_down_weight, attention_out_weight]
        *shards_here, part_a = after_all(shards_here + [part_a], a)
        b, c, part_b, part_c, down_map, up_map = pack(*shards_here, adapters, chunks, shards, dp)
        b_near = link.step_1(part_b)
        near = after_all(near, part_c)
        a_far = link.all_far(near)
        b_far = link.all_far(b_near)
        c_near = link.step_1(after(part_c, b_near))
        joint = [pieces(a, link.swap(a), [a_far], [link.swap(a_far)])]
        b_other = link.swap(after(b, a_far))
        tok = after(tok, b_other)
        vec = None
    else:
        small = jnp.concatenate([biases, frozen_norm_gains], axis=0)
        small = lax.all_gather(small, "fsdp", axis=1, tiled=True)
        hidden_bias = lax.all_gather(hidden_up_bias, "fsdp", axis=0, tiled=False)
        hidden_bias = [hidden_bias[:, j * part : (j + 1) * part].reshape(1, -1) for j in range(chunks)]
        vec = jnp.concatenate([small] + hidden_bias, axis=0)
        vec = jnp.pad(vec, ((0, 16 - 8 - chunks), (0, 0))).astype(f32)
        third = [width * i // 2 for i in range(6)]
        joint = []
        for i in (0, 1):
            cols = [lax.slice_in_dim(joint_projection_weight, t, t + width // 2, axis=1) for t in third[i::2]]
            joint.append([(gather(jnp.concatenate(cols, axis=1)), 0, 0, "whole")])
        up_parts = feed_up_weight.reshape(-1, shards, chunks, part)
        feeds = []
        for group in ((0,), tuple(range(1, chunks))):
            cols = []
            for j in group:
                cols.append(up_parts[:, :, j, :].reshape(-1, shards * part))
                cols.append(feed_down_weight[j * part : (j + 1) * part])
            if group[0] == 0:
                cols.append(attention_out_weight)
            feeds.append([(gather(jnp.concatenate(cols, axis=1)), 0, 0, "whole")])
        rank = query_down_adapter.shape[1]
        down_map = jnp.concatenate([query_down_adapter, value_down_adapter], axis=1)
        down_map = jnp.pad(down_map, ((0, 0), (0, LANES - 2 * rank)))
        zero = jnp.zeros_like(query_up_adapter)
        up_map = jnp.concatenate(
            [
                jnp.concatenate([query_up_adapter, zero], axis=1),
                jnp.concatenate([zero, value_up_adapter], axis=1),
            ],
            axis=0,
        )
        up_map = jnp.pad(up_map * 8, ((0, LANES - 2 * rank), (0, 0))).astype(bf16)

    q, k, v, low, normed, vec, *kept = heads(joint[0], shards, lengths, tok, down_map, up_map, vec)
    if stepped:
        b_far, *c_near, q = after_all([b_far] + c_near + [q], low)
        b_rest = [b_other, [b_far], [link.swap(b_far)]]
        c_far = link.each_far(c_near)
        joint.append(pieces(b, *b_rest))
    old = [q, k, v] + kept
    q, k, v, att, probs, linv = heads(joint[1], shards, lengths, normed, down_map, up_map, vec, low, old)
    if stepped:
        feeds = [pieces(b, *b_rest, joint_projection_weight.shape[1] // 2, joint_projection_weight.shape[1] // 2)]
        c_other = [link.swap(c_far[0])]
        *c_other, att = after_all(c_other + [att], vec)
    h1, normed_2, o, g = feed_first(feeds, shards, tok, att, cot, vec)
    if stepped:
        *far, o = after_all(c_far[1:] + [o], h1)
        c_other += [link.swap(x) for x in far]
        feeds.append(pieces(c, link.swap(after(c, vec)), c_far[:1] + far, c_other))
    out, gh, ga = feed_last(feeds, shards, h1, normed_2, o, g, cot, vec)

    dq, dk, dv, glow, grads = attend_back(slots, q, k, v, ga, att, probs, linv, low, normed, up_map)
    if stepped:
        total = Gather(dp, shards)
        grads = grads + total.move(grads, lambda d, f: (d, f ^ 1))
        _, a, b, c = total.each_far([grads])
        grads = (grads + a) + (b + c)
        a, b, c = [total.move(grads, lambda d, f, k=k: (d, (f + 2 * k) % shards)) for k in (1, 2, 3)]
        dq = after(dq, grads)
        grad_in = input_grad(joint, shards, tok, gh, dq, dk, dv, glow, down_map, vec)
        a, b, c = after_all([a, b, c], grad_in)
        grads = (grads + b) + (a + c)
    else:
        grads = jnp.sum(lax.all_gather(grads, ("dp", "fsdp"), axis=0, tiled=False), axis=0)
        grad_in = input_grad(joint, shards, tok, gh, dq, dk, dv, glow, down_map, vec)
    return (
        out.reshape(tokens.shape),
        grad_in.reshape(tokens.shape),
        grads[8:12].T,
        grads[0:4],
        grads[12:16].T,
        grads[4:8],
    )


def solution(mesh):
    slots = P(None, ("dp", "fsdp"), None, None)
    return jax.shard_map(
        per_device,
        mesh=mesh,
        in_specs=(
            slots,
            P(None, ("dp", "fsdp"), None),
            P("fsdp", None),
            P("fsdp", None),
            P("fsdp", None),
            P("fsdp", None),
            P(None, "fsdp"),
            P(None, "fsdp"),
            P("fsdp"),
            P(),
            P(),
            P(),
            P(),
            slots,
        ),
        out_specs=(slots, slots, P(), P(), P(), P()),
        check_vma=False,
    )
```

```python
import functools
import math

import jax
import jax.numpy as jnp
from jax import lax
from jax.experimental import pallas as pl
from jax.experimental.pallas import tpu as pltpu
from jax.sharding import PartitionSpec as P

f32 = jnp.float32
bf16 = jnp.bfloat16
LANES = 128
PAIR = 128
BAND = 3
EPS = 1e-5
MASKED = -1e30
SCORE_SCALE = 0.125 * math.log2(math.e)
GELU_C = math.sqrt(2.0 / math.pi)
VMEM_LIMIT = 58 * 2**20
COST = 8
NT = (((1,), (1,)), ((), ()))
TN = (((0,), (0,)), ((), ()))


def dot(a, b):
    return jnp.dot(a, b, preferred_element_type=f32)


def dot_nt(a, b):
    return lax.dot_general(a, b, NT, preferred_element_type=f32)


def dot_tn(a, b):
    return lax.dot_general(a, b, TN, preferred_element_type=f32)


def params():
    return pltpu.CompilerParams(vmem_limit_bytes=VMEM_LIMIT)


def resident(array):
    zeros = (0,) * array.ndim
    return pl.BlockSpec(array.shape, lambda *_: zeros, pipeline_mode=pl.Buffered(1))


def normalise(x):
    centred = x - jnp.mean(x, axis=-1, keepdims=True)
    r = lax.rsqrt(jnp.mean(centred * centred, axis=-1, keepdims=True) + EPS)
    return centred * r, r


def norm_back(n, r, w):
    return r * (w - jnp.mean(w, axis=-1, keepdims=True) - n * jnp.mean(w * n, axis=-1, keepdims=True))


def gelu_and_slope(x):
    x2 = x * x
    t = jnp.tanh(x * (GELU_C + (GELU_C * 0.044715) * x2))
    half = 0.5 + 0.5 * t
    act = x * half
    slope = half + (act * (1.0 - half)) * (2 * GELU_C + (6 * GELU_C * 0.044715) * x2)
    return act, slope


def ring_pairs(dp, fsdp, move):
    pairs = []
    for d in range(dp):
        for f in range(fsdp):
            e, g = move(d, f)
            pairs.append((d * fsdp + f, e * fsdp + g))
    return pairs


def after(x, others):
    return lax.optimization_barrier((x, others))[0]


def after_all(xs, others):
    return lax.optimization_barrier((xs, others))[0]


class Gather:
    def __init__(self, dp, fsdp):
        self.dp, self.fsdp = dp, fsdp

    def move(self, x, where):
        return lax.ppermute(x, ("dp", "fsdp"), ring_pairs(self.dp, self.fsdp, where))

    def step_1(self, mine):
        fsdp = self.fsdp
        return [self.move(mine, lambda d, f, k=k: (d, (f + 2 * k) % fsdp)) for k in range(1, fsdp // 2)]

    def all_far(self, near):
        near = [jnp.broadcast_to(x[None], (self.dp,) + x.shape) for x in near]
        return lax.all_to_all(jnp.concatenate(near, axis=1), "dp", 0, 0, tiled=False)

    def each_far(self, near):
        near = stack(near) if len(near) > 1 else near[0]
        return [near] + [self.move(near, lambda d, f, e=e: (d ^ e, f)) for e in range(1, self.dp)]

    def swap(self, x):
        return self.move(x, lambda d, f: (d, f ^ 1))


def pieces(shard, other_shard, far, other_far, shard_column=0, far_column=0):
    made = [(shard, shard_column, 0, "shard"), (other_shard, shard_column, 1, "shard")]
    for swapped, arrays in ((0, far), (1, other_far)):
        if len(arrays) == 1:
            made.append((arrays[0], far_column, swapped, "all"))
        else:
            made += [(x, far_column, swapped, e) for e, x in enumerate(arrays)]
    return made


def copies(weight, refs, whole, sems, place, cols, base, dp, fsdp):
    made = []
    start, size = cols
    rows = whole.shape[0] // fsdp
    part = rows // dp
    index = place[1]

    def add(source, first, at, rows):
        target = whole.at[pl.ds(at, rows), pl.ds(start - base, size)]
        made.append(pltpu.make_async_copy(source.at[:, pl.ds(first + start, size)], target, sems.at[len(made)]))

    for (_, column, swapped, what), ref in zip(weight, refs):
        other = swapped * (1 - 2 * lax.rem(index, 2))
        if what == "whole":
            add(ref, column, 0, whole.shape[0])
        elif what == "shard":
            add(ref, column, pl.multiple_of((index + other) * rows, rows), rows)
        else:
            for e in range(dp) if what == "all" else [what]:
                quarter = e if what == "all" else jnp.bitwise_xor(place[0], e)
                for k in range(1, fsdp // 2):
                    owner = lax.rem(index + fsdp - 2 * k, fsdp) + other
                    at = pl.multiple_of(owner * rows + quarter * part, part)
                    here = pl.ds((k - 1) * part, part)
                    add(ref.at[e, here] if what == "all" else ref.at[here], column, at, part)
    return made


def copy_count(weight, dp, fsdp):
    count = 0
    for _, _, _, what in weight:
        count += 1 if what in ("whole", "shard") else (fsdp // 2 - 1) * (dp if what == "all" else 1)
    return count


def weight_call(kernel, name, weights, order, grid, blocked, in_specs, out_specs, out_shape, scratch, cost, fsdp, old=()):
    dp = lax.axis_size("dp")
    arrays = [[piece[0] for piece in w] for w, _ in weights]
    flat = [a for some in arrays for a in some]
    counts = [copy_count(weights[i][0], dp, fsdp) for i, _, _ in order]

    def body(*refs):
        refs = list(refs)
        place = [lax.axis_index("dp"), lax.axis_index("fsdp")]
        take = lambda n: [refs.pop(0) for _ in range(n)]
        sources = [take(len(some)) for some in arrays]
        ins, _, outs = take(len(blocked)), take(len(old)), take(len(out_shape))
        wholes, sems = take(len(weights)), take(len(order))

        first_step = pl.program_id(0) == 0
        for axis in range(1, len(grid)):
            first_step = first_step & (pl.program_id(axis) == 0)

        def group(n):
            i, start, size = order[n]
            base = start if wholes[i].shape[1] == size else 0
            return copies(weights[i][0], sources[i], wholes[i], sems[n], place, (start, size), base, dp, fsdp)

        @pl.when(first_step)
        def _():
            for n in range(len(order)):
                for copy in group(n):
                    copy.start()

        def wait(n):
            @pl.when(first_step)
            def _():
                for copy in group(n):
                    copy.wait()

        kernel(wholes, wait, ins, outs, refs)

    return pl.pallas_call(
        body,
        grid=grid,
        in_specs=[pl.BlockSpec(memory_space=pltpu.HBM)] * len(flat)
        + in_specs
        + [pl.BlockSpec(memory_space=pl.ANY)] * len(old),
        out_specs=out_specs,
        scratch_shapes=[pltpu.VMEM(shape, bf16) for _, shape in weights]
        + [pltpu.SemaphoreType.DMA((n,)) for n in counts]
        + scratch,
        out_shape=out_shape,
        compiler_params=params(),
        cost_estimate=pl.CostEstimate(flops=cost // COST, bytes_accessed=2**20, transcendentals=0),
        input_output_aliases={len(flat) + len(blocked) + i: i for i in range(len(old))},
        name=name,
    )(*flat, *blocked, *old)


def own_quarter(rows):
    return pl.ds(pl.multiple_of(lax.axis_index("dp") * rows, rows), rows)


def stack_rows(arrays, rows):
    arrays = [a.astype(f32) for a in arrays]
    used = sum(a.shape[0] for a in arrays)
    return jnp.concatenate(arrays + [jnp.zeros((rows - used, arrays[0].shape[1]), f32)], axis=0).astype(bf16)


def stack_kernel(*refs):
    rows = refs[0].shape[0]
    for i, ref in enumerate(refs[:-1]):
        refs[-1][i * rows : (i + 1) * rows, :] = ref[...]


def stack(arrays):
    rows, columns = arrays[0].shape
    return local_call(stack_kernel, "stack", [(rows * len(arrays), columns)], arrays)[0]


def cut_kernel(joint, biases, gains, hidden, first, part):
    half = joint.shape[1] // 6
    for i in range(3):
        first[:, i * half : (i + 1) * half] = joint[:, 2 * i * half : (2 * i + 1) * half]
    small = [biases[...], gains[...], hidden[...].astype(f32).reshape(-1, LANES)]
    first[:, 3 * half :] = stack_rows(small, first.shape[0])
    part[...] = first[own_quarter(part.shape[0]), :]


def local_call(kernel, name, shapes, arrays):
    return pl.pallas_call(
        kernel,
        out_shape=[jax.ShapeDtypeStruct(s, bf16) for s in shapes],
        compiler_params=params(),
        name=name,
    )(*arrays)


def cut(joint, biases, gains, hidden, dp):
    rows, width = joint.shape
    columns = width // 2 + LANES
    return local_call(cut_kernel, "cut", [(rows, columns), (rows // dp, columns)], [joint, biases, gains, hidden])


def pack_kernel(chunks, shards, joint, up, down, wo, q_down, q_up, v_down, v_up, *refs):
    outs, parts = refs[:2], refs[2:4]
    down_map, up_map = refs[4:]
    hidden, width = down.shape
    part = hidden // chunks
    half = joint.shape[1] // 6
    for i in range(3):
        outs[0][:, i * half : (i + 1) * half] = joint[:, (2 * i + 1) * half : (2 * i + 2) * half]
    for j in range(chunks):
        out, at = (outs[1], (j - 1) * 2 * width) if j else (outs[0], 3 * half)
        for s in range(shards):
            start = s * hidden + j * part
            out[:, at + s * part : at + (s + 1) * part] = up[:, start : start + part]
        out[:, at + width : at + 2 * width] = down[j * part : (j + 1) * part, :]
    outs[0][:, 3 * half + 2 * width :] = wo[...]
    for out, part_ref in zip(outs, parts):
        part_ref[...] = out[own_quarter(part_ref.shape[0]), :]
    rank = q_up.shape[0]
    down_map[...] = jnp.zeros_like(down_map)
    down_map[:, :rank] = q_down[...]
    down_map[:, rank : 2 * rank] = v_down[...]
    zero = jnp.zeros(q_up.shape, f32)
    rows = [jnp.concatenate([q_up[...].astype(f32) * 8.0, zero], axis=1)]
    rows += [jnp.concatenate([zero, v_up[...].astype(f32) * 8.0], axis=1)]
    up_map[...] = stack_rows(rows, up_map.shape[0])


def pack(joint, up, down, wo, adapters, chunks, shards, dp):
    rows, width = up.shape[0], down.shape[1]
    shapes = [(rows, joint.shape[1] // 2 + 3 * width), (rows, 2 * (chunks - 1) * width)]
    shapes += [(r // dp, c) for r, c in shapes]
    shapes += [(width, LANES), (LANES, 2 * width)]
    return local_call(functools.partial(pack_kernel, chunks, shards), "pack", shapes, [joint, up, down, wo, *adapters])


def project_slot(first, carried, shards, w, wait, ins, outs, load):
    rows_in, down, up = ins[:3]
    q_ref, k_ref, v_ref = outs[:3]
    half = q_ref.shape[1]
    width = 2 * half
    cols = slice(0, half) if first else slice(half, width)
    wait(0)
    if first:
        low_ref, normed_ref, vec = outs[3:6]

        @pl.when(pl.program_id(0) == 0)
        def _():
            if carried:
                rows = w.shape[0] // shards
                parts = [w[s * rows : s * rows + vec.shape[0], 3 * half :] for s in range(shards)]
                vec[...] = jnp.concatenate(parts, axis=1).astype(f32)
            else:
                vec[...] = ins[3][...]
    else:
        low_in, vec = ins[3:]
    load.wait()
    sub = 256
    state = {}

    def norm(r):
        rr = slice(r, r + sub)
        if first:
            n, _ = normalise(rows_in[rr, :].astype(f32))
            normed = (n * vec[6:7, :] + vec[0:1, :]).astype(bf16)
            normed_ref[rr, :] = normed
        else:
            normed = rows_in[rr, :]
        state[r] = normed

    def mix(r):
        rr = slice(r, r + sub)
        normed = state.pop(r)
        k_ref[rr, :] = dot(normed, w[:, half : 2 * half]).astype(bf16)
        if first:
            low = dot(normed, down[...]).astype(bf16)
            low_ref[rr, :] = low
        else:
            low = low_in[rr, :]
        q = dot(normed, w[:, :half]) + dot(low, up[:, cols]) + vec[2:3, cols]
        q_ref[rr, :] = (q * SCORE_SCALE).astype(bf16)
        v = dot(normed, w[:, 2 * half : 3 * half]) + dot(low, up[:, width:][:, cols]) + vec[3:4, cols]
        v_ref[rr, :] = v.astype(bf16)

    pipelined(list(range(0, rows_in.shape[0], sub)), (norm, mix), (0, 1))


def heads_kernel(first, carried, shards, pairs, wholes, wait, ins, outs, scratch):
    lengths, x_hbm, ins = ins[0], ins[1], ins[2:]
    mask, x_ref, q_ref, k_ref, v_ref, *normed_ref, sems = scratch
    o_ref, p_ref, linv_ref = outs[-3:]
    seq, half = q_ref.shape
    blocks = seq // LANES
    slot, step = pl.program_id(0), pl.program_id(1)

    def rows(s):
        return pl.ds(pl.multiple_of(s * seq, seq), seq)

    def load(s):
        return pltpu.make_async_copy(x_hbm.at[rows(s)], x_ref, sems.at[0])

    cols = pl.ds(0 if first else half, half)
    stores = [(ref, out.at[rows(slot), cols]) for ref, out in zip((q_ref, k_ref, v_ref), outs)]
    if first:
        stores.append((normed_ref[0], outs[4].at[rows(slot)]))
    stores = [pltpu.make_async_copy(a, b, sems.at[1 + i]) for i, (a, b) in enumerate(stores)]

    @pl.when((slot == 0) & (step == 0))
    def _():
        load(0).start()

    @pl.when(step == 0)
    def _():
        own = [q_ref, k_ref, v_ref] + ([outs[3], normed_ref[0], outs[5]] if first else [])
        project_slot(first, carried, shards, wholes[0], wait, [x_ref] + list(ins), own, load(slot))
        for store in stores:
            store.start()
        fill_masks(lengths, slot, mask, blocks)

    @pl.when((step == 1) & (slot + 1 < pl.num_programs(0)))
    def _():
        load(slot + 1).start()

    @pl.when(step != 0)
    def _():
        at = pl.multiple_of((step - 1) * pairs * PAIR, pairs * PAIR)
        attend_pairs(pairs, blocks, at, q_ref, k_ref, v_ref, o_ref, p_ref, linv_ref, mask)

    @pl.when(step == pl.num_programs(1) - 1)
    def _():
        for store in stores:
            store.wait()


def heads(weight, fsdp, lengths, x, down, up, vec=None, low=None, old=()):
    tokens, width = x.shape
    slots = lengths.shape[0]
    seq = tokens // slots
    blocks, heads2, pairs = seq // LANES, width // PAIR, 2
    steps = heads2 // pairs // 2
    first = low is None
    here = 0 if first else 1
    far = pl.BlockSpec(memory_space=pltpu.HBM)
    thin = pl.BlockSpec((seq, LANES), lambda s, j: (s, 0))
    group = lambda j: here * steps + jnp.maximum(j - 1, 0)
    tile = pl.BlockSpec((seq, pairs * PAIR), lambda s, j: (s, group(j)))
    probs = (pairs, blocks, BAND * LANES, 2 * LANES)
    sums = (pairs, blocks, 2 * LANES)
    ins = [lengths, x, down, up]
    in_specs = [pl.BlockSpec(memory_space=pltpu.SMEM), far, resident(down), resident(up)]
    outs, out_specs = [jax.ShapeDtypeStruct((tokens, width), bf16)] * 3, [far] * 3
    if first:
        outs = outs + [jax.ShapeDtypeStruct((tokens, n), bf16) for n in (LANES, width)]
        outs = outs + [jax.ShapeDtypeStruct((16, width), f32)]
        out_specs = out_specs + [thin, far, pl.BlockSpec((16, width), lambda s, j: (0, 0))]
    else:
        ins, in_specs = ins + [low], in_specs + [thin]
    if vec is not None:
        ins, in_specs = ins + [vec], in_specs + [resident(vec)]
    outs = outs + [
        jax.ShapeDtypeStruct((tokens, width), bf16),
        jax.ShapeDtypeStruct((slots, heads2) + probs[1:], bf16),
        jax.ShapeDtypeStruct((slots, heads2) + sums[1:], f32),
    ]
    out_specs = out_specs + [
        tile,
        pl.BlockSpec((1,) + probs, lambda s, j: (s, group(j), 0, 0, 0)),
        pl.BlockSpec((1,) + sums, lambda s, j: (s, group(j), 0, 0)),
    ]
    carried = first and vec is None
    columns = 3 * width // 2 + (LANES if carried else 0)
    return weight_call(
        functools.partial(heads_kernel, first, carried, fsdp, pairs),
        "heads",
        [(weight, (width, columns))],
        [(0, 0, columns)],
        (slots, 1 + steps),
        ins,
        in_specs,
        out_specs,
        outs,
        [pltpu.VMEM((blocks, BAND * LANES, LANES), f32), pltpu.VMEM((seq, width), bf16)]
        + [pltpu.VMEM((seq, width // 2), bf16)] * 3
        + [pltpu.VMEM((seq, width), bf16)] * first
        + [pltpu.SemaphoreType.DMA((5,))],
        9 * tokens * width * width,
        fsdp,
        old,
    )


def fill_masks(lengths, slot, mask, blocks):
    starts = []
    total = jnp.int32(0)
    for d in range(lengths.shape[1]):
        starts.append(total)
        total = total + lengths[slot, d]
    for qb in range(blocks):
        first = max(0, qb - BAND + 1)
        rows = (qb - first + 1) * LANES
        query = qb * LANES + lax.broadcasted_iota(jnp.int32, (8, LANES), 1)
        begin = jnp.zeros((8, LANES), jnp.int32)
        for start in starts:
            begin = jnp.where(query >= start, start, begin)
        key = first * LANES + lax.broadcasted_iota(jnp.int32, (rows, LANES), 0)
        ok = (key >= begin[0:1]) & (key <= query[0:1])
        mask[qb, :rows, :] = jnp.where(ok, 0.0, MASKED)


def half_lanes():
    return lax.broadcasted_iota(jnp.int32, (LANES, LANES), 1) < 64


def half_rows():
    return lax.broadcasted_iota(jnp.int32, (LANES, LANES), 0) < 64


def split_heads(x, left):
    zero = jnp.zeros_like(x)
    return jnp.concatenate([jnp.where(left, x, zero), jnp.where(left, zero, x)], axis=0)


def pipelined(units, stages, lags):
    for t in range(len(units) + lags[-1]):
        for stage, lag in zip(stages, lags):
            if 0 <= t - lag < len(units):
                stage(units[t - lag])


def geometry(qb):
    first = max(0, qb - BAND + 1)
    return first * LANES, (qb - first + 1) * LANES


def attend_pairs(pairs, blocks, at, q_ref, k_ref, v_ref, o_ref, p_ref, linv_ref, mask):
    left, top = half_lanes(), half_rows()
    scores, probs = {}, {}

    def score(unit):
        pair, qb = unit
        cols = pl.ds(at + pair * PAIR, PAIR)
        key0, rows = geometry(qb)
        q = split_heads(q_ref[qb * LANES : (qb + 1) * LANES, cols], left)
        scores[unit] = dot_nt(k_ref[key0 : key0 + rows, cols], q)

    def soften(unit):
        pair, qb = unit
        key0, rows = geometry(qb)
        bias = mask[qb, :rows, :]
        s = scores.pop(unit) + jnp.concatenate([bias, bias], axis=1)
        p = jnp.exp2(s - jnp.max(s, axis=0, keepdims=True))
        linv = 1.0 / jnp.sum(p, axis=0, keepdims=True)
        linv_ref[0, pair, qb : qb + 1, :] = linv
        low = p.astype(bf16)
        p_ref[0, pair, qb, :rows, :] = low
        probs[unit] = (low, linv)

    def mix(unit):
        pair, qb = unit
        key0, rows = geometry(qb)
        low, linv = probs.pop(unit)
        o = dot_tn(v_ref[key0 : key0 + rows, pl.ds(at + pair * PAIR, PAIR)], low)
        o = jnp.where(top, o[:, :LANES] * linv[:, :LANES], o[:, LANES:] * linv[:, LANES:])
        o_ref[qb * LANES : (qb + 1) * LANES, pair * PAIR : (pair + 1) * PAIR] = o.T.astype(bf16)

    units = [(pair, qb) for qb in range(blocks) for pair in range(pairs)]
    pipelined(units, (score, soften, mix), (0, 2, 5))


def attend_back_kernel(
    pairs, blocks, q_ref, k_ref, v_ref, g_ref, o_ref, p_ref, linv_ref, low, normed, up, *refs
):
    dq_ref, dk_ref, dv_ref, glow_ref, grads, dk_sum, dv_sum, glow_sum = refs
    left, top = half_lanes(), half_rows()
    ones = jnp.ones((BAND * LANES, LANES), bf16)
    dk_sum[...] = jnp.zeros_like(dk_sum)
    dv_sum[...] = jnp.zeros_like(dv_sum)
    first, second = {}, {}

    def grad_probs(unit):
        pair, qb = unit
        cols = slice(pair * PAIR, (pair + 1) * PAIR)
        key0, rows = geometry(qb)
        here = slice(qb * LANES, (qb + 1) * LANES)
        linv = linv_ref[0, pair, qb : qb + 1, :]
        linv = jnp.where(top, linv[:, :LANES], linv[:, LANES:]).T
        g = g_ref[here, cols].astype(f32) * linv
        delta = split_heads(-(g * o_ref[here, cols].astype(f32)).astype(bf16), left)
        g = split_heads(g.astype(bf16), left)
        values = jnp.concatenate([v_ref[key0 : key0 + rows, cols], ones[:rows]], axis=1)
        first[unit] = (dot_nt(values, jnp.concatenate([g, delta], axis=1)), g)

    def grad_values(unit):
        pair, qb = unit
        cols = slice(pair * PAIR, (pair + 1) * PAIR)
        key0, rows = geometry(qb)
        dp, g = first.pop(unit)
        low = p_ref[0, pair, qb, :rows, :]
        second[unit] = low * dp.astype(bf16)
        dv_sum[key0 : key0 + rows, cols] += dot(low, g)

    def grad_queries_keys(unit):
        pair, qb = unit
        cols = slice(pair * PAIR, (pair + 1) * PAIR)
        key0, rows = geometry(qb)
        here = slice(qb * LANES, (qb + 1) * LANES)
        ds = second.pop(unit)
        dk_sum[key0 : key0 + rows, cols] += dot(ds, split_heads(q_ref[here, cols], left))
        dq = dot_tn(k_ref[key0 : key0 + rows, cols], ds)
        dq = jnp.where(top, dq[:, :LANES], dq[:, LANES:]) * 0.125
        dq_ref[here, cols] = dq.T.astype(bf16)

    units = [(pair, qb) for qb in range(blocks) for pair in range(pairs)]
    pipelined(units, (grad_probs, grad_values, grad_queries_keys), (0, 2, 4))
    dk_ref[...] = (dk_sum[...] * (0.125 / SCORE_SCALE)).astype(bf16)
    dv_ref[...] = dv_sum[...].astype(bf16)

    slot, step, last = pl.program_id(0), pl.program_id(1), pl.num_programs(1) - 1
    width = normed.shape[1]
    at = pl.multiple_of(step * pairs * PAIR, pairs * PAIR)
    here = pl.ds(at, pairs * PAIR)
    both = jnp.concatenate([dq_ref[...], dv_ref[...]], axis=1)
    part = dot_tn(low[...], both)
    part = jnp.concatenate([part[0:4, : pairs * PAIR], part[4:8, pairs * PAIR :]], axis=0) * 8.0
    grads[0:8, here] = jnp.where(slot == 0, part, grads[0:8, here] + part)
    glow = dot_nt(both, jnp.concatenate([up[:, here], up[:, pl.ds(width + at, pairs * PAIR)]], axis=1))
    glow_sum[...] = jnp.where(step == 0, glow, glow_sum[...] + glow)

    @pl.when(step == last)
    def _():
        glow = glow_sum[...].astype(bf16)
        glow_ref[...] = glow
        part = dot_tn(glow, normed[...])[0:8]
        grads[8:16, :] = jnp.where(slot == 0, part, grads[8:16, :] + part)


def attend_back(slots, q, k, v, g, o, p, linv, low, normed, up):
    tokens, width = q.shape
    seq = tokens // slots
    blocks, heads2, pairs = seq // LANES, width // PAIR, 2
    rows = BAND * LANES
    tile = pl.BlockSpec((seq, pairs * PAIR), lambda s, h: (s, h))
    thin = pl.BlockSpec((seq, LANES), lambda s, h: (s, 0))
    return pl.pallas_call(
        functools.partial(attend_back_kernel, pairs, blocks),
        grid=(slots, heads2 // pairs),
        in_specs=[tile] * 5
        + [
            pl.BlockSpec((1, pairs, blocks, rows, 2 * LANES), lambda s, h: (s, h, 0, 0, 0)),
            pl.BlockSpec((1, pairs, blocks, 2 * LANES), lambda s, h: (s, h, 0, 0)),
            thin,
            pl.BlockSpec((seq, width), lambda s, h: (s, 0)),
            resident(up),
        ],
        out_specs=[tile] * 3 + [thin, pl.BlockSpec((16, width), lambda s, h: (0, 0))],
        scratch_shapes=[pltpu.VMEM((seq, pairs * PAIR), f32)] * 2 + [pltpu.VMEM((seq, LANES), f32)],
        out_shape=[jax.ShapeDtypeStruct(q.shape, bf16)] * 3
        + [jax.ShapeDtypeStruct((tokens, LANES), bf16), jax.ShapeDtypeStruct((16, width), f32)],
        compiler_params=params(),
        cost_estimate=pl.CostEstimate(flops=14 * tokens * width * width // COST, bytes_accessed=2**20, transcendentals=0),
        name="attend_back",
    )(q, k, v, g, o, p, linv, low, normed, up)


def feed_chunk(wait, first, normed, cot, w, at, bias):
    width = cot.shape[1]
    wait(first)
    wait(first + 1)
    size = width // 4
    up, down = slice(at, at + width), slice(at + width, at + 2 * width)
    acts, grads = [], []
    for i in range(0, width, size):
        grad = dot_nt(cot, w[i : i + size, down])
        act, slope = gelu_and_slope(dot(normed, w[:, at + i : at + i + size]) + bias[:, i : i + size])
        acts.append(act.astype(bf16))
        grads.append((slope * grad).astype(bf16))
    return dot(jnp.concatenate(acts, axis=1), w[:, down]), dot_nt(jnp.concatenate(grads, axis=1), w[:, up])


def feed_first_kernel(wholes, wait, ins, outs, _):
    tok, att, cot, vec = ins
    h1_ref, normed_ref, o_ref, g_ref = outs
    width = tok.shape[1]
    wait(0)
    h1 = tok[...].astype(f32) + dot(att[...], wholes[0][:, 2 * width :]) + vec[4:5, :]
    h1_ref[...] = h1
    n, _ = normalise(h1)
    normed = (n * vec[7:8, :] + vec[1:2, :]).astype(bf16)
    normed_ref[...] = normed
    o_ref[...], g_ref[...] = feed_chunk(wait, 1, normed, cot[...], wholes[0], 0, vec[8:9, :])


def feed_last_kernel(wholes, wait, ins, outs, scratch):
    normed, cot, vec, h1, old_o, old_g = ins
    out_ref, gh_ref, ga_ref = outs
    x_ref, o_sum, g_sum, sems = scratch
    rows, width = cot.shape
    here = pl.ds(pl.multiple_of(pl.program_id(0) * rows, rows), rows)
    loads = [(old_o, o_sum), (old_g, g_sum), (h1, x_ref)]
    loads = [pltpu.make_async_copy(a.at[here], b, sems.at[i]) for i, (a, b) in enumerate(loads)]
    for load in loads:
        load.start()
    chunks = wholes[0].shape[1] // (2 * width)
    for j in range(chunks):
        bias = vec[9 + j : 10 + j, :]
        o, g = feed_chunk(wait, 2 * j, normed[...], cot[...], wholes[0], 2 * j * width, bias)
        if j == 0:
            for load in loads:
                load.wait()
        if j < chunks - 1:
            o_sum[...] += o
            g_sum[...] += g
    x = x_ref[...]
    out_ref[...] = (x + (o_sum[...] + o) + vec[5:6, :]).astype(bf16)
    n, r = normalise(x)
    grad = cot[...].astype(f32) + norm_back(n, r, (g_sum[...] + g) * vec[7:8, :])
    low = grad.astype(bf16)
    gh_ref[...] = low
    wait(2 * chunks)
    ga_ref[...] = dot_nt(low, wholes[1][...]).astype(bf16)


def feed_call(kernel, name, weights, order, fsdp, rowwise, vec, far, out_types):
    tokens, width = rowwise[0].shape
    rows = 512
    row = pl.BlockSpec((rows, width), lambda i: (i, 0))
    scratch = [pltpu.VMEM((rows, width), f32)] * len(far)
    return weight_call(
        kernel,
        name,
        weights,
        order,
        (tokens // rows,),
        rowwise + [vec] + far,
        [row] * len(rowwise) + [resident(vec)] + [pl.BlockSpec(memory_space=pltpu.HBM)] * len(far),
        [row] * len(out_types),
        [jax.ShapeDtypeStruct((tokens, width), t) for t in out_types],
        scratch + ([pltpu.SemaphoreType.DMA((len(far),))] if far else []),
        18 * tokens * width * width,
        fsdp,
    )


def feed_order(width, chunks):
    return [(0, (2 * j + 1 - i) * width, width) for j in range(chunks) for i in (0, 1)]


def feed_first(feeds, fsdp, tok, att, cot, vec):
    width = tok.shape[1]
    weights = [(feeds[0], (width, 3 * width))]
    order = [(0, 2 * width, width)] + feed_order(width, 1)
    types = [f32, bf16, f32, f32]
    return feed_call(feed_first_kernel, "feed_first", weights, order, fsdp, [tok, att, cot], vec, [], types)


def feed_last(feeds, fsdp, h1, normed, o, g, cot, vec):
    width = cot.shape[1]
    weights = [(feeds[1], (width, 6 * width)), (feeds[0], (width, width))]
    order = feed_order(width, 3) + [(1, 2 * width, width)]
    rowwise, far = [normed, cot], [h1, o, g]
    return feed_call(feed_last_kernel, "feed_last", weights, order, fsdp, rowwise, vec, far, [bf16] * 3)


def input_kernel(wholes, wait, ins, outs, _):
    dq, dk, dv, glow, down, vec, tok, gh = ins
    (out_ref,) = outs
    half = dq.shape[1] // 2
    g = dot_nt(glow[...], down[...])
    for i, w in enumerate(wholes):
        wait(i)
        cols = slice(i * half, (i + 1) * half)
        g = g + dot_nt(dq[:, cols], w[:, :half])
        g = g + dot_nt(dk[:, cols], w[:, half : 2 * half])
        g = g + dot_nt(dv[:, cols], w[:, 2 * half : 3 * half])
    n, r = normalise(tok[...].astype(f32))
    out_ref[...] = (gh[...].astype(f32) + norm_back(n, r, g * vec[6:7, :])).astype(bf16)


def input_grad(joint, fsdp, tok, gh, dq, dk, dv, glow, down, vec):
    tokens, width = tok.shape
    rows = 512
    row = pl.BlockSpec((rows, width), lambda i: (i, 0))
    thin = pl.BlockSpec((rows, LANES), lambda i: (i, 0))
    return weight_call(
        input_kernel,
        "input_grad",
        [(w, (width, 3 * width // 2)) for w in joint],
        [(0, 0, 3 * width // 2), (1, 0, 3 * width // 2)],
        (tokens // rows,),
        [dq, dk, dv, glow, down, vec, tok, gh],
        [row] * 3 + [thin, resident(down), resident(vec), row, row],
        [row],
        [jax.ShapeDtypeStruct((tokens, width), bf16)],
        [],
        6 * tokens * width * width,
        fsdp,
    )[0]


def per_device(
    tokens,
    document_length_list,
    joint_projection_weight,
    attention_out_weight,
    feed_up_weight,
    feed_down_weight,
    frozen_norm_gains,
    biases,
    hidden_up_bias,
    query_down_adapter,
    query_up_adapter,
    value_down_adapter,
    value_up_adapter,
    cotangent,
):
    micro, local, seq, width = tokens.shape
    slots = micro * local
    shards = width // joint_projection_weight.shape[0]
    hidden = feed_down_weight.shape[0]
    tok = tokens.reshape(slots * seq, width)
    cot = cotangent.reshape(slots * seq, width)
    lengths = document_length_list.reshape(slots, -1)

    dp = lax.axis_size("dp")
    chunks = 4
    part = hidden // chunks
    stepped = dp == 4 and shards == 8 and part == LANES and width == shards * LANES

    def gather(x):
        return lax.all_gather(x, "fsdp", axis=0, tiled=True)

    adapters = [query_down_adapter, query_up_adapter, value_down_adapter, value_up_adapter]
    if stepped:
        a, part_a = cut(joint_projection_weight, biases, frozen_norm_gains, hidden_up_bias, dp)
        link = Gather(dp, shards)
        near = link.step_1(part_a)
        shards_here = [joint_projection_weight, feed_up_weight, feed_down_weight, attention_out_weight]
        *shards_here, part_a = after_all(shards_here + [part_a], a)
        b, c, part_b, part_c, down_map, up_map = pack(*shards_here, adapters, chunks, shards, dp)
        b_near = link.step_1(part_b)
        near = after_all(near, part_c)
        a_far = link.all_far(near)
        b_far = link.all_far(b_near)
        c_near = link.step_1(after(part_c, b_near))
        joint = [pieces(a, link.swap(a), [a_far], [link.swap(a_far)])]
        b_other = link.swap(after(b, a_far))
        tok = after(tok, b_other)
        vec = None
    else:
        small = jnp.concatenate([biases, frozen_norm_gains], axis=0)
        small = lax.all_gather(small, "fsdp", axis=1, tiled=True)
        hidden_bias = lax.all_gather(hidden_up_bias, "fsdp", axis=0, tiled=False)
        hidden_bias = [hidden_bias[:, j * part : (j + 1) * part].reshape(1, -1) for j in range(chunks)]
        vec = jnp.concatenate([small] + hidden_bias, axis=0)
        vec = jnp.pad(vec, ((0, 16 - 8 - chunks), (0, 0))).astype(f32)
        third = [width * i // 2 for i in range(6)]
        joint = []
        for i in (0, 1):
            cols = [lax.slice_in_dim(joint_projection_weight, t, t + width // 2, axis=1) for t in third[i::2]]
            joint.append([(gather(jnp.concatenate(cols, axis=1)), 0, 0, "whole")])
        up_parts = feed_up_weight.reshape(-1, shards, chunks, part)
        feeds = []
        for group in ((0,), tuple(range(1, chunks))):
            cols = []
            for j in group:
                cols.append(up_parts[:, :, j, :].reshape(-1, shards * part))
                cols.append(feed_down_weight[j * part : (j + 1) * part])
            if group[0] == 0:
                cols.append(attention_out_weight)
            feeds.append([(gather(jnp.concatenate(cols, axis=1)), 0, 0, "whole")])
        rank = query_down_adapter.shape[1]
        down_map = jnp.concatenate([query_down_adapter, value_down_adapter], axis=1)
        down_map = jnp.pad(down_map, ((0, 0), (0, LANES - 2 * rank)))
        zero = jnp.zeros_like(query_up_adapter)
        up_map = jnp.concatenate(
            [
                jnp.concatenate([query_up_adapter, zero], axis=1),
                jnp.concatenate([zero, value_up_adapter], axis=1),
            ],
            axis=0,
        )
        up_map = jnp.pad(up_map * 8, ((0, LANES - 2 * rank), (0, 0))).astype(bf16)

    q, k, v, low, normed, vec, *kept = heads(joint[0], shards, lengths, tok, down_map, up_map, vec)
    if stepped:
        b_far, q = after_all([b_far, q], low)
        c_near = after_all(c_near, q)
        b_rest = [b_other, [b_far], [link.swap(b_far)]]
        c_far = link.each_far(c_near)
        joint.append(pieces(b, *b_rest))
    old = [q, k, v] + kept
    q, k, v, att, probs, linv = heads(joint[1], shards, lengths, normed, down_map, up_map, vec, low, old)
    if stepped:
        feeds = [pieces(b, *b_rest, joint_projection_weight.shape[1] // 2, joint_projection_weight.shape[1] // 2)]
        c_other = [link.swap(c_far[0])]
        *c_other, att = after_all(c_other + [att], vec)
    h1, normed_2, o, g = feed_first(feeds, shards, tok, att, cot, vec)
    if stepped:
        *far, o = after_all(c_far[1:] + [o], h1)
        c_other += [link.swap(x) for x in far]
        feeds.append(pieces(c, link.swap(after(c, vec)), c_far[:1] + far, c_other))
    out, gh, ga = feed_last(feeds, shards, h1, normed_2, o, g, cot, vec)

    dq, dk, dv, glow, grads = attend_back(slots, q, k, v, ga, att, probs, linv, low, normed, up_map)
    if stepped:
        total = Gather(dp, shards)
        grads = grads + total.move(grads, lambda d, f: (d, f ^ 1))
        _, a, b, c = total.each_far([grads])
        grads = (grads + a) + (b + c)
        a, b, c = [total.move(grads, lambda d, f, k=k: (d, (f + 2 * k) % shards)) for k in (1, 2, 3)]
        dq = after(dq, grads)
        grad_in = input_grad(joint, shards, tok, gh, dq, dk, dv, glow, down_map, vec)
        a, b, c = after_all([a, b, c], grad_in)
        grads = (grads + b) + (a + c)
    else:
        grads = jnp.sum(lax.all_gather(grads, ("dp", "fsdp"), axis=0, tiled=False), axis=0)
        grad_in = input_grad(joint, shards, tok, gh, dq, dk, dv, glow, down_map, vec)
    return (
        out.reshape(tokens.shape),
        grad_in.reshape(tokens.shape),
        grads[8:12].T,
        grads[0:4],
        grads[12:16].T,
        grads[4:8],
    )


def solution(mesh):
    slots = P(None, ("dp", "fsdp"), None, None)
    return jax.shard_map(
        per_device,
        mesh=mesh,
        in_specs=(
            slots,
            P(None, ("dp", "fsdp"), None),
            P("fsdp", None),
            P("fsdp", None),
            P("fsdp", None),
            P("fsdp", None),
            P(None, "fsdp"),
            P(None, "fsdp"),
            P("fsdp"),
            P(),
            P(),
            P(),
            P(),
            slots,
        ),
        out_specs=(slots, slots, P(), P(), P(), P()),
        check_vma=False,
    )
```
